256 devices in a mesh: gx: 8 (over z), gy: 4 (over x), gz: 8 (over y, core).
Axes of the slice: x: 4, y: 4, z: 8, core: 2. Of those that a mesh axis runs over, the one named last changes fastest.
Arguments:
- density: float32 [128, 128, 512], P('gz', 'gx', 'gy'), may hold values from 0.02 to 1, as said below
- volume_power_source: float32 [128, 128, 512], P('gz', 'gx', 'gy'), may hold values from -2.4 to 2.4
Outputs:
- thermal_solution: float32 [128, 128, 512], P('gz', 'gx', 'gy')
- filtered_sensitivity: float32 [128, 128, 512], P('gz', 'gx', 'gy')
The draws below stay inside these ranges and needn't reach their ends.
Inputs may be any that keep to these rules, and one draw needn't show every extreme that they name: density of each cell, solid cells near one and void cells far lower.
All inputs are finite; a program needn't handle non-finite values.
Results may differ from the reference program's by a relative error of at most 0.00018.
Values sent between devices are 32-bit elements; how exact they have to be, the bound alone decides.
A program may use at most 64 MiB of HBM per device.

```python
import jax
import jax.numpy as jnp

ITERS = 2
NX = 128
NY = 512
NZ = 128


def draw_density(key, part):
    key = jax.random.fold_in(key, 11)
    shape = (NZ, NX, NY)
    pick_key, solid_key, void_key = jax.random.split(key, 3)
    solid = jax.random.uniform(solid_key, shape, jnp.float32, 0.6, 1.0)
    void = jnp.exp(jax.random.uniform(void_key, shape, jnp.float32, jnp.log(0.02), jnp.log(0.3)))
    is_solid = jax.random.bernoulli(pick_key, 0.7, shape)
    return jnp.clip(jnp.where(is_solid, solid, void), 0.02, 1.0).astype(jnp.float32)


def draw_volume_power_source(key, part):
    key = jax.random.fold_in(key, 7)
    shape = (NZ, NX, NY)
    values = 0.3 * jax.random.normal(key, shape, jnp.float32)
    return jnp.clip(values, -2.4, 2.4).astype(jnp.float32)


def setup_inputs(seed: int = 0) -> dict:
    keys = jax.random.split(jax.random.key(seed), 3)
    return {
        "density": draw_density(jax.random.fold_in(keys[2], 71), 0),
        "volume_power_source": draw_volume_power_source(jax.random.fold_in(keys[2], 71), 0),
    }


KMIN = 1e-3
OMEGA = 0.8
FILTER_WEIGHT = 4.0


def neighbour_sum(padded):
    total = padded[2:, 1:-1, 1:-1] + padded[:-2, 1:-1, 1:-1]
    total = total + padded[1:-1, 2:, 1:-1] + padded[1:-1, :-2, 1:-1]
    return total + padded[1:-1, 1:-1, 2:] + padded[1:-1, 1:-1, :-2]


def gap_squares(field, padded):
    total = jnp.zeros_like(field)
    for piece in (padded[2:, 1:-1, 1:-1], padded[:-2, 1:-1, 1:-1], padded[1:-1, 2:, 1:-1],
                  padded[1:-1, :-2, 1:-1], padded[1:-1, 1:-1, 2:], padded[1:-1, 1:-1, :-2]):
        total = total + (field - piece) ** 2
    return total


def operator(field, conduct, cond_pad, factor):
    field_pad = jnp.pad(field, 1)
    return factor * 0.5 * (6.0 * conduct * field + field * neighbour_sum(cond_pad)
                           - conduct * neighbour_sum(field_pad) - neighbour_sum(cond_pad * field_pad))


def block_sum(field):
    depth, rows, cols = field.shape
    return field.reshape(depth // 2, 2, rows // 2, 2, cols // 2, 2).sum(axis=(1, 3, 5))


def refine(field):
    return jnp.repeat(jnp.repeat(jnp.repeat(field, 2, axis=0), 2, axis=1), 2, axis=2)


def reference(density, volume_power_source):
    conduct = KMIN + (1.0 - KMIN) * density ** 3
    cond_pad = jnp.pad(conduct, 1)
    diag_fine = 0.5 * (6.0 * conduct + neighbour_sum(cond_pad))
    coarse_cond = block_sum(conduct) * 0.125
    coarse_pad = jnp.pad(coarse_cond, 1)
    diag_coarse = 4.0 * 0.5 * (6.0 * coarse_cond + neighbour_sum(coarse_pad))

    def precondition(resid):
        smooth = OMEGA * resid / diag_fine
        coarse_rhs = block_sum(resid - operator(smooth, conduct, cond_pad, 1.0))
        correction = OMEGA * coarse_rhs / diag_coarse
        for sweep in range(3):
            correction = correction + OMEGA * (coarse_rhs - operator(correction, coarse_cond, coarse_pad, 4.0)) / diag_coarse
        smooth = smooth + refine(correction)
        return smooth + OMEGA * (resid - operator(smooth, conduct, cond_pad, 1.0)) / diag_fine

    thermal_solution = jnp.zeros_like(volume_power_source)
    residual = volume_power_source
    precond = precondition(residual)
    update_vector = precond
    rz_now = jnp.sum(residual * precond)
    for step in range(ITERS):
        image = operator(update_vector, conduct, cond_pad, 1.0)
        update_scale = rz_now / jnp.sum(update_vector * image)
        thermal_solution = thermal_solution + update_scale * update_vector
        residual = residual - update_scale * image
        if step + 1 < ITERS:
            precond = precondition(residual)
            rz_next = jnp.sum(residual * precond)
            update_vector = precond + (rz_next / rz_now) * update_vector
            rz_now = rz_next
    interface_gaps = gap_squares(thermal_solution, jnp.pad(thermal_solution, 1))
    sensitivity = -3.0 * (1.0 - KMIN) * density ** 2 * 0.5 * interface_gaps
    blurred_density = sensitivity
    for sweep in range(3):
        blurred_density = (sensitivity + FILTER_WEIGHT * neighbour_sum(jnp.pad(blurred_density, 1, mode="edge"))) / (1.0 + 6.0 * FILTER_WEIGHT)
    return thermal_solution, blurred_density
```

```python
import functools
import itertools

import jax
import jax.numpy as jnp
from jax import lax
from jax.experimental import pallas as pl
from jax.experimental.pallas import tpu as pltpu
from jax.sharding import PartitionSpec as P

KMIN = 0.001
OMEGA = 0.8
FILTER_WEIGHT = 4.0
MESH = pl.DeviceIdType.MESH
F32 = jnp.float32

LANES = 128
NZ = NX = 16
CZ = CX = 8
PAD = 8
FZ = NZ + 2 * PAD
CZP = CZ + 2 * PAD
LO, HI = 4, 28
WIN = HI - LO
CLO, CWIN = 4, 16

NEIGHBOURS = sorted(
    (o for o in itertools.product((-1, 0, 1), repeat=3) if o != (0, 0, 0)),
    key=lambda o: (sum(map(abs, o)), o),
)


def place(sizes, offset):
    dz, dx, dy = offset
    gx, gy, gz = sizes
    return (
        lax.rem(lax.axis_index("gx") + dx + gx, gx),
        lax.rem(lax.axis_index("gy") + dy + gy, gy),
        lax.rem(lax.axis_index("gz") + dz + gz, gz),
    )


def other_core():
    gz = lax.axis_index("gz")
    return gz + 1 - 2 * lax.rem(gz, 2)


def lane_iota(rows):
    return lax.broadcasted_iota(jnp.int32, (rows, LANES), 1)


def lane_neighbours(main, side, step):
    lane = lane_iota(main.shape[0])
    up_main, up_side = pltpu.roll(main, LANES - step, 1), pltpu.roll(side, LANES - step, 1)
    dn_main, dn_side = pltpu.roll(main, step, 1), pltpu.roll(side, step, 1)
    last, first = lane >= LANES - step, lane < step
    ahead = (jnp.where(last, up_side, up_main), jnp.where(last, up_main, up_side))
    behind = (jnp.where(first, dn_side, dn_main), jnp.where(first, dn_main, dn_side))
    return ahead, behind


def pair_lanes(v):
    even = lax.rem(lane_iota(v.shape[0]), 2) == 0
    return v + jnp.where(even, pltpu.roll(v, LANES - 1, 1), pltpu.roll(v, 1, 1))


def loop(lower, upper, body):
    lax.fori_loop(lower, upper, lambda i, c: (body(i), c)[1], 0)


class Exchange:
    def __init__(self, sizes, arr, fields, halo, n, group, pks, pkr, ssem, rsem):
        self.sizes, self.arr, self.fields, self.halo, self.n = sizes, arr, fields, halo, n
        self.group = group
        self.per = LANES // group
        self.pks, self.pkr, self.ssem, self.rsem = pks, pkr, ssem, rsem
        self.copies = []

    def pack(self):
        per, group, n = self.per, self.group, self.n
        lane = lane_iota(n)
        for f in range(self.fields):
            for g in range(n // per):
                acc = None
                for k in range(per):
                    v = self.arr[f, 0, PAD + g * per + k, PAD : PAD + n, :]
                    v = pltpu.roll(v, group * k + group // 2, 1)
                    acc = v if acc is None else jnp.where(lane >= group * k, v, acc)
                self.pks[f, g] = acc

    def start(self):
        n, h, per = self.n, self.halo, self.per
        groups = n // per
        side_groups = -(-h // per)
        for i, (dz, dx, dy) in enumerate(NEIGHBOURS):
            rows = {0: (0, n, PAD), 1: (n - PAD, PAD, 0), -1: (0, PAD, PAD + n)}[dx]
            if dy == 0:
                planes = {0: (0, n, PAD), 1: (n - h, h, PAD - h), -1: (0, h, PAD + n)}[dz]
                src = self.arr.at[:, 0, pl.ds(PAD + planes[0], planes[1]), pl.ds(PAD + rows[0], rows[1]), :]
                dst = self.arr.at[:, 0, pl.ds(planes[2], planes[1]), pl.ds(rows[2], rows[1]), :]
            else:
                first = PAD // per
                s = side_groups
                gr = {0: (0, groups, first), 1: (groups - s, s, first - s), -1: (0, s, first + groups)}[dz]
                src = self.pks.at[:, pl.ds(gr[0], gr[1]), pl.ds(rows[0], rows[1]), :]
                dst = self.pkr.at[0 if dy == 1 else 1, :, pl.ds(gr[2], gr[1]), pl.ds(rows[2], rows[1]), :]
            cp = pltpu.make_async_remote_copy(
                src_ref=src,
                dst_ref=dst,
                send_sem=self.ssem.at[i],
                recv_sem=self.rsem.at[i],
                device_id=place(self.sizes, (dz, dx, dy)),
                device_id_type=MESH,
            )
            cp.start()
            self.copies.append(cp)

    def wait(self):
        for cp in self.copies:
            cp.wait_recv()

    def unpack(self):
        per, group, n, h = self.per, self.group, self.n, self.halo
        rows = n + 2 * PAD
        low = lax.rem(lane_iota(rows), group) < group // 2

        def body(g):
            for f in range(self.fields):
                merged = jnp.where(low, self.pkr[0, f, g], self.pkr[1, f, g])
                for k in range(per):
                    self.arr[f, 1, g * per + k, 0:rows, :] = pltpu.roll(
                        merged, LANES - group * k - group // 2, 1
                    )

        first = (PAD - h) // per
        last = -(-(PAD + n + h) // per)
        loop(first, last, body)

    def finish(self):
        for cp in self.copies:
            cp.wait_send()


def kernel(
    sizes,
    rho_ref,
    src_ref,
    out_t,
    out_f,
    fin,
    cond,
    kzm,
    kx,
    kyp,
    kym,
    diag,
    inv,
    zpre,
    vv,
    z0,
    q0,
    last,
    ww,
    mask,
    cin,
    cin2,
    cc,
    kcz,
    kcx,
    kcyp,
    kcym,
    cinv,
    ea,
    eb,
    cmask,
    refined,
    tmp,
    pks1,
    pkr1,
    pks2,
    pkr2,
    pks3,
    pkr3,
    pks4,
    pkr4,
    red1,
    red2,
    ssems,
    rsems,
    rs1,
    rr1,
    rs2,
    rr2,
):
    gxs, gys, gzs = sizes
    gx, gy, gz = lax.axis_index("gx"), lax.axis_index("gy"), lax.axis_index("gz")

    def peer1(dy, dz):
        return (gx, lax.rem(gy + dy, gys), lax.rem(gz + 2 * dz, gzs))

    def peer2(dx, flip):
        return (lax.rem(gx + dx, gxs), gy, other_core() if flip else gz)

    group1 = [(dy, dz) for dy in range(gys) for dz in range(gzs // 2) if (dy, dz) != (0, 0)]
    group2 = [(dx, fl) for dx in range(gxs) for fl in range(2) if (dx, fl) != (0, 0)]

    barrier = pltpu.get_barrier_semaphore()
    partners = [place(sizes, o) for o in NEIGHBOURS]
    partners += [peer1(*o) for o in group1 if o not in ((1, 0), (gys - 1, 0))]
    partners += [peer2(*o) for o in group2 if o[0] not in (0, 1, gxs - 1)]
    for device in partners:
        pl.semaphore_signal(barrier, inc=1, device_id=device, device_id_type=MESH)

    fin[0, 0, PAD : PAD + NZ, PAD : PAD + NX, :] = rho_ref[...]
    fin[1, 0, PAD : PAD + NZ, PAD : PAD + NX, :] = src_ref[...]
    ex1 = Exchange(sizes, fin, 2, 5, NZ, 16, pks1, pkr1, ssems.at[0], rsems.at[0])
    ex1.pack()

    row = lax.broadcasted_iota(jnp.int32, (FZ, LANES), 0) - PAD + gx * NX
    lane = lane_iota(FZ)
    row_in = (row >= 0) & (row < gxs * NX)
    left, right = gy > 0, gy < gys - 1
    right_end = jnp.where(right, 8, 0)
    left_start = jnp.where(left, LANES - 8, LANES)
    side_in = row_in & ((lane < right_end) | (lane >= left_start))
    mask[0] = jnp.where(row_in, 1.0, 0.0)
    mask[1] = jnp.where(side_in, 1.0, 0.0)
    crow = lax.broadcasted_iota(jnp.int32, (24, LANES), 0) - PAD + gx * CX
    clane = lane_iota(24)
    crow_in = (crow >= 0) & (crow < gxs * CX)
    cside_in = crow_in & (
        (clane < jnp.where(right, 16, 0)) | (clane >= jnp.where(left, LANES - 16, LANES))
    )
    cmask[0] = jnp.where(crow_in, 1.0, 0.0)
    cmask[1] = jnp.where(cside_in, 1.0, 0.0)

    def plane_in(z, cells):
        g = gz * cells + z - PAD
        return jnp.where((g >= 0) & (g < gzs * cells), 1.0, 0.0).astype(F32)

    pl.semaphore_wait(barrier, len(partners))
    ex1.start()
    ex1.wait()
    ex1.unpack()

    def conductivity(z):
        inside = plane_in(z, NZ)
        for s in range(2):
            r = fin[0, s, z]
            cond[s, z, 0:FZ, :] = (mask[s] * inside) * (KMIN + (1.0 - KMIN) * (r * r * r))

    loop(3, 29, conductivity)

    def faces(z):
        here = [cond[s, z, LO:HI, :] for s in range(2)]
        ahead, behind = lane_neighbours(here[0], here[1], 1)
        inside = plane_in(z, NZ)
        for s in range(2):
            c = here[s]
            zm = 0.5 * (cond[s, z - 1, LO:HI, :] + c)
            zp = 0.5 * (cond[s, z + 1, LO:HI, :] + c)
            xp = 0.5 * (cond[s, z, LO + 1 : HI + 1, :] + c)
            xm = 0.5 * (cond[s, z, LO - 1 : HI - 1, :] + c)
            yp = 0.5 * (ahead[s] + c)
            ym = 0.5 * (behind[s] + c)
            d = (zm + zp) + (xp + xm) + (yp + ym)
            kzm[s, z, LO:HI, :] = zm
            kx[s, z, LO:HI, :] = xp
            kx[s, z, LO - 1 : LO, :] = xm[0:1, :]
            kyp[s, z, LO:HI, :] = yp
            kym[s, z, LO:HI, :] = ym
            diag[s, z, LO:HI, :] = d
            ok = mask[s, LO:HI, :] * inside > 0.5
            i = jnp.where(ok, OMEGA / d, 0.0)
            inv[s, z, LO:HI, :] = i
            zpre[s, z, LO:HI, :] = i * fin[1, s, z, LO:HI, :]

    loop(4, 28, faces)

    def off_diagonal(field, z, lo, n, sides):
        here = [field[s, z, lo : lo + n, :] for s in range(2)]
        ahead, behind = lane_neighbours(here[0], here[1], 1)
        out = []
        for s in range(sides):
            t = kzm[s, z, lo : lo + n, :] * field[s, z - 1, lo : lo + n, :]
            t = t + kzm[s, z + 1, lo : lo + n, :] * field[s, z + 1, lo : lo + n, :]
            u = kx[s, z, lo : lo + n, :] * field[s, z, lo + 1 : lo + n + 1, :]
            u = u + kx[s, z, lo - 1 : lo + n - 1, :] * field[s, z, lo - 1 : lo + n - 1, :]
            v = kyp[s, z, lo : lo + n, :] * ahead[s] + kym[s, z, lo : lo + n, :] * behind[s]
            out.append((t + u) + v)
        return out

    def coarse_rhs(load, field, dest):
        def body(k):
            total = None
            for j in range(2):
                z = PAD + 2 * k + j
                t = (1.0 - OMEGA) * load(z) + off_diagonal(field, z, PAD, NX, 1)[0]
                total = t if total is None else total + t
            tmp[k, 0, 0:NX, :] = pair_lanes(total)
            dest[0, 0, PAD + k, PAD : PAD + CX, :] = (
                tmp[k, 0, pl.ds(0, CX, 2), :] + tmp[k, 0, pl.ds(1, CX, 2), :]
            )

        loop(0, CZ, body)

    coarse_rhs(lambda z: fin[1, 0, z, PAD : PAD + NX, :], zpre, cin)

    def coarse_cond(vc):
        z = 2 * vc - PAD
        for s in range(2):
            u = cond[s, z, 0:FZ, :] + cond[s, z + 1, 0:FZ, :]
            refined[vc, s] = pair_lanes(u)
            cc[s, vc, 4:20, :] = 0.125 * (
                refined[vc, s, pl.ds(0, 16, 2), :] + refined[vc, s, pl.ds(1, 16, 2), :]
            )

    loop(7, 17, coarse_cond)

    def coarse_diag(vc):
        c = cc[0, vc, 8:16, :]
        ahead, behind = lane_neighbours(c, cc[1, vc, 8:16, :], 2)
        t = cc[0, vc - 1, 8:16, :] + cc[0, vc + 1, 8:16, :]
        t = t + (cc[0, vc, 7:15, :] + cc[0, vc, 9:17, :])
        t = t + (ahead[0] + behind[0])
        cin[1, 0, vc, 8:16, :] = c
        cin[2, 0, vc, 8:16, :] = OMEGA / (2.0 * (6.0 * c + t))

    loop(8, 16, coarse_diag)

    ex2 = Exchange(sizes, cin, 3, 5, CZ, 32, pks2, pkr2, ssems.at[1], rsems.at[1])
    ex2.pack()
    ex2.start()
    ex2.wait()
    ex2.unpack()

    def coarse_masked(vc):
        inside = plane_in(vc, CZ)
        for s in range(2):
            ok = cmask[s] * inside > 0.5
            cc[s, vc, 0:24, :] = jnp.where(ok, cin[1, s, vc, 0:24, :], 0.0)
            i = jnp.where(ok, cin[2, s, vc, 0:24, :], 0.0)
            cinv[s, vc, 0:24, :] = i
            ea[s, vc, 0:24, :] = i * cin[0, s, vc, 0:24, :]

    loop(3, 21, coarse_masked)

    def coarse_faces(vc):
        lo, hi = CLO, CLO + CWIN
        here = [cc[s, vc, lo:hi, :] for s in range(2)]
        ahead, behind = lane_neighbours(here[0], here[1], 2)
        for s in range(2):
            c = here[s]
            kcz[s, vc, lo:hi, :] = 2.0 * (c + cc[s, vc - 1, lo:hi, :])
            kcx[s, vc, lo:hi, :] = 2.0 * (c + cc[s, vc, lo + 1 : hi + 1, :])
            kcx[s, vc, lo - 1 : lo, :] = 2.0 * (c[0:1, :] + cc[s, vc, lo - 1 : lo, :])
            kcyp[s, vc, lo:hi, :] = 2.0 * (c + ahead[s])
            kcym[s, vc, lo:hi, :] = 2.0 * (c + behind[s])

    loop(4, 21, coarse_faces)

    def sweep(e, e_next, rhs, first, end):
        lo, hi = CLO, CLO + CWIN

        def body(vc):
            here = [e[s, vc, lo:hi, :] for s in range(2)]
            ahead, behind = lane_neighbours(here[0], here[1], 2)
            for s in range(2):
                t = kcz[s, vc, lo:hi, :] * e[s, vc - 1, lo:hi, :]
                t = t + kcz[s, vc + 1, lo:hi, :] * e[s, vc + 1, lo:hi, :]
                u = kcx[s, vc, lo:hi, :] * e[s, vc, lo + 1 : hi + 1, :]
                u = u + kcx[s, vc, lo - 1 : hi - 1, :] * e[s, vc, lo - 1 : hi - 1, :]
                v = kcyp[s, vc, lo:hi, :] * ahead[s] + kcym[s, vc, lo:hi, :] * behind[s]
                r = rhs[0, s, vc, lo:hi, :] + ((t + u) + v)
                e_next[s, vc, lo:hi, :] = (1.0 - OMEGA) * here[s] + cinv[s, vc, lo:hi, :] * r

        loop(first, end, body)

    def add_refined(e, base, first, end):
        def body(vc):
            for s in range(2):
                v = e[s, vc, CLO : CLO + CWIN, :]
                refined[vc, s, pl.ds(0, CWIN, 2), :] = v
                refined[vc, s, pl.ds(1, CWIN, 2), :] = v
                fine = refined[vc, s, LO:HI, :]
                for j in range(2):
                    z = 2 * vc - PAD + j
                    vv[s, z, LO:HI, :] = base[s, z, LO:HI, :] + fine

        loop(first, end, body)

    sweep(ea, eb, cin, 4, 20)
    sweep(eb, ea, cin, 5, 19)
    sweep(ea, eb, cin, 6, 18)
    add_refined(eb, zpre, 6, 18)

    def post(z):
        b = off_diagonal(vv, z, LO, WIN, 2)
        for s in range(2):
            z0[s, z, LO:HI, :] = (1.0 - OMEGA) * vv[s, z, LO:HI, :] + inv[s, z, LO:HI, :] * (
                fin[1, s, z, LO:HI, :] + b[s]
            )

    loop(5, 27, post)

    def image(z):
        b = off_diagonal(z0, z, LO, WIN, 2)
        for s in range(2):
            q = diag[s, z, LO:HI, :] * z0[s, z, LO:HI, :] - b[s]
            q0[s, z, LO:HI, :] = q
            zpre[s, z, LO:HI, :] = inv[s, z, LO:HI, :] * q

    loop(6, 26, image)

    coarse_rhs(lambda z: q0[0, z, PAD : PAD + NX, :], zpre, cin2)
    ex3 = Exchange(sizes, cin2, 1, 4, CZ, 32, pks3, pkr3, ssems.at[2], rsems.at[2])
    ex3.pack()
    ex3.start()
    ex3.wait()
    ex3.unpack()

    def first_correction(vc):
        for s in range(2):
            ea[s, vc, 0:24, :] = cinv[s, vc, 0:24, :] * cin2[0, s, vc, 0:24, :]

    loop(4, 20, first_correction)
    sweep(ea, eb, cin2, 5, 19)
    sweep(eb, ea, cin2, 6, 18)
    sweep(ea, eb, cin2, 7, 17)
    add_refined(eb, zpre, 7, 17)

    def post_second(z):
        b = off_diagonal(vv, z, LO, WIN, 2)
        for s in range(2):
            ww[s, z, LO:HI, :] = (1.0 - OMEGA) * vv[s, z, LO:HI, :] + inv[s, z, LO:HI, :] * (
                q0[s, z, LO:HI, :] + b[s]
            )

    loop(7, 25, post_second)

    own = slice(PAD, PAD + NX)

    def dots(z, acc):
        w = ww[0, z, own, :]
        zz = z0[0, z, own, :]
        q = q0[0, z, own, :]
        r = fin[1, 0, z, own, :]
        p = diag[0, z, own, :] * w - off_diagonal(ww, z, PAD, NX, 1)[0]
        last[0, 0, z, own, :] = zz
        last[1, 0, z, own, :] = w
        terms = (r * zz, zz * q, r * w, q * w, zz * p, w * p)
        return tuple(a + t[0:8] + t[8:16] for a, t in zip(acc, terms))

    zero = jnp.zeros((8, LANES), F32)
    acc = lax.fori_loop(PAD, PAD + NZ, dots, (zero,) * 6)
    which = lax.broadcasted_iota(jnp.int32, (8, LANES), 0)
    part = zero
    for i, a in enumerate(acc):
        part = jnp.where(which == i, jnp.sum(a, axis=0, keepdims=True), part)

    rank1 = gy * (gzs // 2) + gz // 2
    red1[rank1] = part
    cps1 = []
    for i, o in enumerate(group1):
        cp = pltpu.make_async_remote_copy(
            src_ref=red1.at[rank1],
            dst_ref=red1.at[rank1],
            send_sem=rs1.at[i],
            recv_sem=rr1.at[i],
            device_id=peer1(*o),
            device_id_type=MESH,
        )
        cp.start()
        cps1.append(cp)
    ex4 = Exchange(sizes, last, 2, 4, NZ, 16, pks4, pkr4, ssems.at[3], rsems.at[3])
    ex4.pack()
    ex4.start()
    for cp in cps1:
        cp.wait_recv()
    part = red1[0]
    for i in range(1, len(group1) + 1):
        part = part + red1[i]
    rank2 = gx * 2 + lax.rem(gz, 2)
    red2[rank2] = part
    cps2 = []
    for i, o in enumerate(group2):
        cp = pltpu.make_async_remote_copy(
            src_ref=red2.at[rank2],
            dst_ref=red2.at[rank2],
            send_sem=rs2.at[i],
            recv_sem=rr2.at[i],
            device_id=peer2(*o),
            device_id_type=MESH,
        )
        cp.start()
        cps2.append(cp)
    ex4.wait()
    ex4.unpack()
    for cp in cps2:
        cp.wait_recv()
    total = red2[0]
    for i in range(1, len(group2) + 1):
        total = total + red2[i]
    total = jnp.broadcast_to(jnp.sum(total, axis=1, keepdims=True), (8, LANES))
    rz, zq, rw, qw, zp, wp = (total[i : i + 1, :] for i in range(6))
    a0 = rz / zq
    rz1 = a0 * (a0 * qw - rw)
    beta = rz1 / rz
    gamma = 1.0 + beta
    a1 = rz1 / (gamma * gamma * zq - a0 * gamma * (zp + qw) + a0 * a0 * wp)
    c1 = jnp.broadcast_to(a0 + a1 * gamma, (WIN, LANES))
    c2 = jnp.broadcast_to(-a1 * a0, (WIN, LANES))

    def solution_plane(z):
        inside = plane_in(z, NZ)
        for s in range(2):
            x = c1 * last[0, s, z, LO:HI, :] + c2 * last[1, s, z, LO:HI, :]
            vv[s, z, LO:HI, :] = x * (mask[s, LO:HI, :] * inside)

    loop(4, 28, solution_plane)

    def copy_out(z):
        out_t[z] = vv[0, z + PAD, own, :]

    loop(0, NZ, copy_out)

    def sensitivity(z):
        here = [vv[s, z, LO:HI, :] for s in range(2)]
        ahead, behind = lane_neighbours(here[0], here[1], 1)
        inside = plane_in(z, NZ)
        for s in range(2):
            x = here[s]
            g = (x - vv[s, z - 1, LO:HI, :]) ** 2 + (x - vv[s, z + 1, LO:HI, :]) ** 2
            g = g + (x - vv[s, z, LO - 1 : HI - 1, :]) ** 2
            g = g + (x - vv[s, z, LO + 1 : HI + 1, :]) ** 2
            g = g + ((x - ahead[s]) ** 2 + (x - behind[s]) ** 2)
            r = fin[0, s, z, LO:HI, :] * (mask[s, LO:HI, :] * inside)
            v = (-3.0 * (1.0 - KMIN) * 0.5) * (r * r) * g
            z0[s, z, LO:HI, :] = v
            ww[s, z, LO:HI, :] = v * (1.0 / (1.0 + 6.0 * FILTER_WEIGHT))

    loop(5, 27, sensitivity)

    wlane = lane_iota(WIN)
    wrow = lax.broadcasted_iota(jnp.int32, (WIN, LANES), 0) + LO - PAD + gx * NX
    outside_row = jnp.where(wrow == 0, 1.0, 0.0) + jnp.where(wrow == gxs * NX - 1, 1.0, 0.0)
    outside_main = outside_row + jnp.where((wlane == 0) & (gy == 0), 1.0, 0.0)
    outside_main = outside_main + jnp.where((wlane == LANES - 1) & (gy == gys - 1), 1.0, 0.0)
    outside = (outside_main, outside_row)
    weight = FILTER_WEIGHT / (1.0 + 6.0 * FILTER_WEIGHT)

    def blur(f, f_next, first, end):
        def body(z):
            here = [f[s, z, LO:HI, :] for s in range(2)]
            ahead, behind = lane_neighbours(here[0], here[1], 1)
            inside = plane_in(z, NZ)
            g = gz * NZ + z - PAD
            ends = jnp.where((g == 0) | (g == gzs * NZ - 1), 1.0, 0.0).astype(F32)
            for s in range(2):
                t = f[s, z - 1, LO:HI, :] + f[s, z + 1, LO:HI, :]
                t = t + (f[s, z, LO - 1 : HI - 1, :] + f[s, z, LO + 1 : HI + 1, :])
                t = t + (ahead[s] + behind[s])
                t = t + (outside[s] + ends) * here[s]
                f_next[s, z, LO:HI, :] = ww[s, z, LO:HI, :] + t * (
                    mask[s, LO:HI, :] * (inside * weight)
                )

        loop(first, end, body)

    blur(z0, q0, 6, 26)
    blur(q0, z0, 7, 25)

    def blur_out(k):
        z = k + PAD
        f = z0
        here = [f[s, z, own, :] for s in range(2)]
        ahead, behind = lane_neighbours(here[0], here[1], 1)
        g = gz * NZ + k
        ends = jnp.where((g == 0) | (g == gzs * NZ - 1), 1.0, 0.0).astype(F32)
        t = f[0, z - 1, own, :] + f[0, z + 1, own, :]
        t = t + (f[0, z, PAD - 1 : PAD + NX - 1, :] + f[0, z, PAD + 1 : PAD + NX + 1, :])
        t = t + (ahead[0] + behind[0])
        t = t + (outside[0][PAD - LO : PAD - LO + NX] + ends) * here[0]
        out_f[k] = ww[0, z, own, :] + t * weight

    loop(0, NZ, blur_out)

    for ex in (ex1, ex2, ex3, ex4):
        ex.finish()
    for cp in cps1 + cps2:
        cp.wait_send()


def local(sizes, density, volume_power_source):
    shape = jax.ShapeDtypeStruct((NZ, NX, LANES), F32)
    vmem = pl.BlockSpec(memory_space=pltpu.VMEM)

    def fine(*lead, rows=FZ):
        return pltpu.VMEM((*lead, 2, FZ, rows, LANES), F32)

    def coarse(*lead):
        return pltpu.VMEM((*lead, 2, CZP, 32, LANES), F32)

    n = len(NEIGHBOURS)
    g1 = sizes[1] * (sizes[2] // 2)
    g2 = sizes[0] * 2
    scratch = [
        fine(2),
        fine(rows=40),
        *[fine() for _ in range(10)],
        fine(2),
        fine(),
        pltpu.VMEM((2, FZ, LANES), F32),
        coarse(3),
        coarse(1),
        *[coarse() for _ in range(8)],
        pltpu.VMEM((2, 24, LANES), F32),
        pltpu.VMEM((CZP, 2, FZ, LANES), F32),
        pltpu.VMEM((CZ, 1, NX, LANES), F32),
        pltpu.VMEM((2, 2, NX, LANES), F32),
        pltpu.VMEM((2, 2, 4, FZ, LANES), F32),
        pltpu.VMEM((3, 2, CX, LANES), F32),
        pltpu.VMEM((2, 3, 6, 24, LANES), F32),
        pltpu.VMEM((1, 2, CX, LANES), F32),
        pltpu.VMEM((2, 1, 6, 24, LANES), F32),
        pltpu.VMEM((2, 2, NX, LANES), F32),
        pltpu.VMEM((2, 2, 4, FZ, LANES), F32),
        pltpu.VMEM((g1, 8, LANES), F32),
        pltpu.VMEM((g2, 8, LANES), F32),
        pltpu.SemaphoreType.DMA((4, n)),
        pltpu.SemaphoreType.DMA((4, n)),
        pltpu.SemaphoreType.DMA((g1 - 1,)),
        pltpu.SemaphoreType.DMA((g1 - 1,)),
        pltpu.SemaphoreType.DMA((g2 - 1,)),
        pltpu.SemaphoreType.DMA((g2 - 1,)),
    ]
    return pl.pallas_call(
        functools.partial(kernel, sizes),
        out_shape=(shape, shape),
        in_specs=[vmem, vmem],
        out_specs=(vmem, vmem),
        scratch_shapes=scratch,
        compiler_params=pltpu.CompilerParams(
            collective_id=0, has_side_effects=True, vmem_limit_bytes=48 * 1024 * 1024
        ),
        name="heat_sink_step",
    )(density, volume_power_source)


def solution(mesh):
    sizes = tuple(mesh.shape[a] for a in ("gx", "gy", "gz"))
    spec = P("gz", "gx", "gy")
    return jax.shard_map(
        functools.partial(local, sizes),
        mesh=mesh,
        in_specs=(spec, spec),
        out_specs=(spec, spec),
        check_vma=False,
    )
```

```python
import functools
import itertools

import jax
import jax.numpy as jnp
from jax import lax
from jax.experimental import pallas as pl
from jax.experimental.pallas import tpu as pltpu
from jax.sharding import PartitionSpec as P

KMIN = 0.001
OMEGA = 0.8
FILTER_WEIGHT = 4.0
MESH = pl.DeviceIdType.MESH
F32 = jnp.float32

LANES = 128
NZ = NX = 16
CZ = CX = 8
PAD = 8
FZ = NZ + 2 * PAD
CZP = CZ + 2 * PAD
LO, HI = 4, 28
WIN = HI - LO
CLO, CWIN = 4, 16

NEIGHBOURS = sorted(
    (o for o in itertools.product((-1, 0, 1), repeat=3) if o != (0, 0, 0)),
    key=lambda o: (sum(map(abs, o)), o),
)


def place(sizes, offset):
    dz, dx, dy = offset
    gx, gy, gz = sizes
    return (
        lax.rem(lax.axis_index("gx") + dx + gx, gx),
        lax.rem(lax.axis_index("gy") + dy + gy, gy),
        lax.rem(lax.axis_index("gz") + dz + gz, gz),
    )


def other_core():
    gz = lax.axis_index("gz")
    return gz + 1 - 2 * lax.rem(gz, 2)


def lane_iota(rows):
    return lax.broadcasted_iota(jnp.int32, (rows, LANES), 1)


def lane_neighbours(main, side, step):
    lane = lane_iota(main.shape[0])
    up_main, up_side = pltpu.roll(main, LANES - step, 1), pltpu.roll(side, LANES - step, 1)
    dn_main, dn_side = pltpu.roll(main, step, 1), pltpu.roll(side, step, 1)
    last, first = lane >= LANES - step, lane < step
    ahead = (jnp.where(last, up_side, up_main), jnp.where(last, up_main, up_side))
    behind = (jnp.where(first, dn_side, dn_main), jnp.where(first, dn_main, dn_side))
    return ahead, behind


def pair_lanes(v):
    even = lax.rem(lane_iota(v.shape[0]), 2) == 0
    return v + jnp.where(even, pltpu.roll(v, LANES - 1, 1), pltpu.roll(v, 1, 1))


def loop(lower, upper, body):
    for i in range(lower, upper):
        body(i)


class Exchange:
    def __init__(self, sizes, arr, fields, halo, n, group, pks, pkr, ssem, rsem):
        self.sizes, self.arr, self.fields, self.halo, self.n = sizes, arr, fields, halo, n
        self.group = group
        self.per = LANES // group
        self.pks, self.pkr, self.ssem, self.rsem = pks, pkr, ssem, rsem
        self.copies = []

    def pack(self):
        per, group, n = self.per, self.group, self.n
        lane = lane_iota(n)
        for f in range(self.fields):
            for g in range(n // per):
                acc = None
                for k in range(per):
                    v = self.arr[f, 0, PAD + g * per + k, PAD : PAD + n, :]
                    v = pltpu.roll(v, group * k + group // 2, 1)
                    acc = v if acc is None else jnp.where(lane >= group * k, v, acc)
                self.pks[f, g] = acc

    def start(self):
        n, h, per = self.n, self.halo, self.per
        groups = n // per
        side_groups = -(-h // per)
        for i, (dz, dx, dy) in enumerate(NEIGHBOURS):
            rows = {0: (0, n, PAD), 1: (n - PAD, PAD, 0), -1: (0, PAD, PAD + n)}[dx]
            if dy == 0:
                planes = {0: (0, n, PAD), 1: (n - h, h, PAD - h), -1: (0, h, PAD + n)}[dz]
                src = self.arr.at[:, 0, pl.ds(PAD + planes[0], planes[1]), pl.ds(PAD + rows[0], rows[1]), :]
                dst = self.arr.at[:, 0, pl.ds(planes[2], planes[1]), pl.ds(rows[2], rows[1]), :]
            else:
                first = PAD // per
                s = side_groups
                gr = {0: (0, groups, first), 1: (groups - s, s, first - s), -1: (0, s, first + groups)}[dz]
                src = self.pks.at[:, pl.ds(gr[0], gr[1]), pl.ds(rows[0], rows[1]), :]
                dst = self.pkr.at[0 if dy == 1 else 1, :, pl.ds(gr[2], gr[1]), pl.ds(rows[2], rows[1]), :]
            cp = pltpu.make_async_remote_copy(
                src_ref=src,
                dst_ref=dst,
                send_sem=self.ssem.at[i],
                recv_sem=self.rsem.at[i],
                device_id=place(self.sizes, (dz, dx, dy)),
                device_id_type=MESH,
            )
            cp.start()
            self.copies.append(cp)

    def wait(self):
        for cp in self.copies:
            cp.wait_recv()

    def unpack(self):
        per, group, n, h = self.per, self.group, self.n, self.halo
        rows = n + 2 * PAD
        low = lax.rem(lane_iota(rows), group) < group // 2

        def body(g):
            for f in range(self.fields):
                merged = jnp.where(low, self.pkr[0, f, g], self.pkr[1, f, g])
                for k in range(per):
                    self.arr[f, 1, g * per + k, 0:rows, :] = pltpu.roll(
                        merged, LANES - group * k - group // 2, 1
                    )

        first = (PAD - h) // per
        last = -(-(PAD + n + h) // per)
        loop(first, last, body)

    def finish(self):
        for cp in self.copies:
            cp.wait_send()


def kernel(
    sizes,
    rho_ref,
    src_ref,
    out_t,
    out_f,
    fin,
    cond,
    kzm,
    kx,
    kyp,
    kym,
    diag,
    inv,
    zpre,
    vv,
    z0,
    q0,
    last,
    ww,
    mask,
    cin,
    cin2,
    cc,
    kcz,
    kcx,
    kcyp,
    kcym,
    cinv,
    ea,
    eb,
    cmask,
    refined,
    tmp,
    pks1,
    pkr1,
    pks2,
    pkr2,
    pks3,
    pkr3,
    pks4,
    pkr4,
    red1,
    red2,
    ssems,
    rsems,
    rs1,
    rr1,
    rs2,
    rr2,
):
    gxs, gys, gzs = sizes
    gx, gy, gz = lax.axis_index("gx"), lax.axis_index("gy"), lax.axis_index("gz")

    def peer1(dy, dz):
        return (gx, lax.rem(gy + dy, gys), lax.rem(gz + 2 * dz, gzs))

    def peer2(dx, flip):
        return (lax.rem(gx + dx, gxs), gy, other_core() if flip else gz)

    group1 = [(dy, dz) for dy in range(gys) for dz in range(gzs // 2) if (dy, dz) != (0, 0)]
    group2 = [(dx, fl) for dx in range(gxs) for fl in range(2) if (dx, fl) != (0, 0)]

    barrier = pltpu.get_barrier_semaphore()
    partners = [place(sizes, o) for o in NEIGHBOURS]
    partners += [peer1(*o) for o in group1 if o not in ((1, 0), (gys - 1, 0))]
    partners += [peer2(*o) for o in group2 if o[0] not in (0, 1, gxs - 1)]
    for device in partners:
        pl.semaphore_signal(barrier, inc=1, device_id=device, device_id_type=MESH)

    fin[0, 0, PAD : PAD + NZ, PAD : PAD + NX, :] = rho_ref[...]
    fin[1, 0, PAD : PAD + NZ, PAD : PAD + NX, :] = src_ref[...]
    ex1 = Exchange(sizes, fin, 2, 5, NZ, 16, pks1, pkr1, ssems.at[0], rsems.at[0])
    ex1.pack()

    row = lax.broadcasted_iota(jnp.int32, (FZ, LANES), 0) - PAD + gx * NX
    lane = lane_iota(FZ)
    row_in = (row >= 0) & (row < gxs * NX)
    left, right = gy > 0, gy < gys - 1
    right_end = jnp.where(right, 8, 0)
    left_start = jnp.where(left, LANES - 8, LANES)
    side_in = row_in & ((lane < right_end) | (lane >= left_start))
    mask[0] = jnp.where(row_in, 1.0, 0.0)
    mask[1] = jnp.where(side_in, 1.0, 0.0)
    crow = lax.broadcasted_iota(jnp.int32, (24, LANES), 0) - PAD + gx * CX
    clane = lane_iota(24)
    crow_in = (crow >= 0) & (crow < gxs * CX)
    cside_in = crow_in & (
        (clane < jnp.where(right, 16, 0)) | (clane >= jnp.where(left, LANES - 16, LANES))
    )
    cmask[0] = jnp.where(crow_in, 1.0, 0.0)
    cmask[1] = jnp.where(cside_in, 1.0, 0.0)

    def plane_in(z, cells):
        g = gz * cells + z - PAD
        return jnp.where((g >= 0) & (g < gzs * cells), 1.0, 0.0).astype(F32)

    pl.semaphore_wait(barrier, len(partners))
    ex1.start()
    ex1.wait()
    ex1.unpack()

    def conductivity(z):
        inside = plane_in(z, NZ)
        for s in range(2):
            r = fin[0, s, z]
            cond[s, z, 0:FZ, :] = (mask[s] * inside) * (KMIN + (1.0 - KMIN) * (r * r * r))

    loop(3, 29, conductivity)

    def faces(z):
        here = [cond[s, z, LO:HI, :] for s in range(2)]
        ahead, behind = lane_neighbours(here[0], here[1], 1)
        inside = plane_in(z, NZ)
        for s in range(2):
            c = here[s]
            zm = 0.5 * (cond[s, z - 1, LO:HI, :] + c)
            zp = 0.5 * (cond[s, z + 1, LO:HI, :] + c)
            xp = 0.5 * (cond[s, z, LO + 1 : HI + 1, :] + c)
            xm = 0.5 * (cond[s, z, LO - 1 : HI - 1, :] + c)
            yp = 0.5 * (ahead[s] + c)
            ym = 0.5 * (behind[s] + c)
            d = (zm + zp) + (xp + xm) + (yp + ym)
            kzm[s, z, LO:HI, :] = zm
            kx[s, z, LO:HI, :] = xp
            kx[s, z, LO - 1 : LO, :] = xm[0:1, :]
            kyp[s, z, LO:HI, :] = yp
            kym[s, z, LO:HI, :] = ym
            diag[s, z, LO:HI, :] = d
            ok = mask[s, LO:HI, :] * inside > 0.5
            i = jnp.where(ok, OMEGA / d, 0.0)
            inv[s, z, LO:HI, :] = i
            zpre[s, z, LO:HI, :] = i * fin[1, s, z, LO:HI, :]

    loop(4, 28, faces)

    def off_diagonal(field, z, lo, n, sides):
        here = [field[s, z, lo : lo + n, :] for s in range(2)]
        ahead, behind = lane_neighbours(here[0], here[1], 1)
        out = []
        for s in range(sides):
            t = kzm[s, z, lo : lo + n, :] * field[s, z - 1, lo : lo + n, :]
            t = t + kzm[s, z + 1, lo : lo + n, :] * field[s, z + 1, lo : lo + n, :]
            u = kx[s, z, lo : lo + n, :] * field[s, z, lo + 1 : lo + n + 1, :]
            u = u + kx[s, z, lo - 1 : lo + n - 1, :] * field[s, z, lo - 1 : lo + n - 1, :]
            v = kyp[s, z, lo : lo + n, :] * ahead[s] + kym[s, z, lo : lo + n, :] * behind[s]
            out.append((t + u) + v)
        return out

    def coarse_rhs(load, field, dest):
        def body(k):
            total = None
            for j in range(2):
                z = PAD + 2 * k + j
                t = (1.0 - OMEGA) * load(z) + off_diagonal(field, z, PAD, NX, 1)[0]
                total = t if total is None else total + t
            tmp[k, 0, 0:NX, :] = pair_lanes(total)
            dest[0, 0, PAD + k, PAD : PAD + CX, :] = (
                tmp[k, 0, pl.ds(0, CX, 2), :] + tmp[k, 0, pl.ds(1, CX, 2), :]
            )

        loop(0, CZ, body)

    coarse_rhs(lambda z: fin[1, 0, z, PAD : PAD + NX, :], zpre, cin)

    def coarse_cond(vc):
        z = 2 * vc - PAD
        for s in range(2):
            u = cond[s, z, 0:FZ, :] + cond[s, z + 1, 0:FZ, :]
            refined[vc, s] = pair_lanes(u)
            cc[s, vc, 4:20, :] = 0.125 * (
                refined[vc, s, pl.ds(0, 16, 2), :] + refined[vc, s, pl.ds(1, 16, 2), :]
            )

    loop(7, 17, coarse_cond)

    def coarse_diag(vc):
        c = cc[0, vc, 8:16, :]
        ahead, behind = lane_neighbours(c, cc[1, vc, 8:16, :], 2)
        t = cc[0, vc - 1, 8:16, :] + cc[0, vc + 1, 8:16, :]
        t = t + (cc[0, vc, 7:15, :] + cc[0, vc, 9:17, :])
        t = t + (ahead[0] + behind[0])
        cin[1, 0, vc, 8:16, :] = c
        cin[2, 0, vc, 8:16, :] = OMEGA / (2.0 * (6.0 * c + t))

    loop(8, 16, coarse_diag)

    ex2 = Exchange(sizes, cin, 3, 5, CZ, 32, pks2, pkr2, ssems.at[1], rsems.at[1])
    ex2.pack()
    ex2.start()
    ex2.wait()
    ex2.unpack()

    def coarse_masked(vc):
        inside = plane_in(vc, CZ)
        for s in range(2):
            ok = cmask[s] * inside > 0.5
            cc[s, vc, 0:24, :] = jnp.where(ok, cin[1, s, vc, 0:24, :], 0.0)
            i = jnp.where(ok, cin[2, s, vc, 0:24, :], 0.0)
            cinv[s, vc, 0:24, :] = i
            ea[s, vc, 0:24, :] = i * cin[0, s, vc, 0:24, :]

    loop(3, 21, coarse_masked)

    def coarse_faces(vc):
        lo, hi = CLO, CLO + CWIN
        here = [cc[s, vc, lo:hi, :] for s in range(2)]
        ahead, behind = lane_neighbours(here[0], here[1], 2)
        for s in range(2):
            c = here[s]
            kcz[s, vc, lo:hi, :] = 2.0 * (c + cc[s, vc - 1, lo:hi, :])
            kcx[s, vc, lo:hi, :] = 2.0 * (c + cc[s, vc, lo + 1 : hi + 1, :])
            kcx[s, vc, lo - 1 : lo, :] = 2.0 * (c[0:1, :] + cc[s, vc, lo - 1 : lo, :])
            kcyp[s, vc, lo:hi, :] = 2.0 * (c + ahead[s])
            kcym[s, vc, lo:hi, :] = 2.0 * (c + behind[s])

    loop(4, 21, coarse_faces)

    def sweep(e, e_next, rhs, first, end):
        lo, hi = CLO, CLO + CWIN

        def body(vc):
            here = [e[s, vc, lo:hi, :] for s in range(2)]
            ahead, behind = lane_neighbours(here[0], here[1], 2)
            for s in range(2):
                t = kcz[s, vc, lo:hi, :] * e[s, vc - 1, lo:hi, :]
                t = t + kcz[s, vc + 1, lo:hi, :] * e[s, vc + 1, lo:hi, :]
                u = kcx[s, vc, lo:hi, :] * e[s, vc, lo + 1 : hi + 1, :]
                u = u + kcx[s, vc, lo - 1 : hi - 1, :] * e[s, vc, lo - 1 : hi - 1, :]
                v = kcyp[s, vc, lo:hi, :] * ahead[s] + kcym[s, vc, lo:hi, :] * behind[s]
                r = rhs[0, s, vc, lo:hi, :] + ((t + u) + v)
                e_next[s, vc, lo:hi, :] = (1.0 - OMEGA) * here[s] + cinv[s, vc, lo:hi, :] * r

        loop(first, end, body)

    def add_refined(e, base, first, end):
        def body(vc):
            for s in range(2):
                v = e[s, vc, CLO : CLO + CWIN, :]
                refined[vc, s, pl.ds(0, CWIN, 2), :] = v
                refined[vc, s, pl.ds(1, CWIN, 2), :] = v
                fine = refined[vc, s, LO:HI, :]
                for j in range(2):
                    z = 2 * vc - PAD + j
                    vv[s, z, LO:HI, :] = base[s, z, LO:HI, :] + fine

        loop(first, end, body)

    sweep(ea, eb, cin, 4, 20)
    sweep(eb, ea, cin, 5, 19)
    sweep(ea, eb, cin, 6, 18)
    add_refined(eb, zpre, 6, 18)

    def post(z):
        b = off_diagonal(vv, z, LO, WIN, 2)
        for s in range(2):
            z0[s, z, LO:HI, :] = (1.0 - OMEGA) * vv[s, z, LO:HI, :] + inv[s, z, LO:HI, :] * (
                fin[1, s, z, LO:HI, :] + b[s]
            )

    loop(5, 27, post)

    def image(z):
        b = off_diagonal(z0, z, LO, WIN, 2)
        for s in range(2):
            q = diag[s, z, LO:HI, :] * z0[s, z, LO:HI, :] - b[s]
            q0[s, z, LO:HI, :] = q
            zpre[s, z, LO:HI, :] = inv[s, z, LO:HI, :] * q

    loop(6, 26, image)

    coarse_rhs(lambda z: q0[0, z, PAD : PAD + NX, :], zpre, cin2)
    ex3 = Exchange(sizes, cin2, 1, 4, CZ, 32, pks3, pkr3, ssems.at[2], rsems.at[2])
    ex3.pack()
    ex3.start()
    ex3.wait()
    ex3.unpack()

    def first_correction(vc):
        for s in range(2):
            ea[s, vc, 0:24, :] = cinv[s, vc, 0:24, :] * cin2[0, s, vc, 0:24, :]

    loop(4, 20, first_correction)
    sweep(ea, eb, cin2, 5, 19)
    sweep(eb, ea, cin2, 6, 18)
    sweep(ea, eb, cin2, 7, 17)
    add_refined(eb, zpre, 7, 17)

    def post_second(z):
        b = off_diagonal(vv, z, LO, WIN, 2)
        for s in range(2):
            ww[s, z, LO:HI, :] = (1.0 - OMEGA) * vv[s, z, LO:HI, :] + inv[s, z, LO:HI, :] * (
                q0[s, z, LO:HI, :] + b[s]
            )

    loop(7, 25, post_second)

    own = slice(PAD, PAD + NX)

    def dots(z, acc):
        w = ww[0, z, own, :]
        zz = z0[0, z, own, :]
        q = q0[0, z, own, :]
        r = fin[1, 0, z, own, :]
        p = diag[0, z, own, :] * w - off_diagonal(ww, z, PAD, NX, 1)[0]
        last[0, 0, z, own, :] = zz
        last[1, 0, z, own, :] = w
        terms = (r * zz, zz * q, r * w, q * w, zz * p, w * p)
        return tuple(a + t[0:8] + t[8:16] for a, t in zip(acc, terms))

    zero = jnp.zeros((8, LANES), F32)
    acc = (zero,) * 6
    for z in range(PAD, PAD + NZ):
        acc = dots(z, acc)
    which = lax.broadcasted_iota(jnp.int32, (8, LANES), 0)
    part = zero
    for i, a in enumerate(acc):
        part = jnp.where(which == i, jnp.sum(a, axis=0, keepdims=True), part)

    rank1 = gy * (gzs // 2) + gz // 2
    red1[rank1] = part
    cps1 = []
    for i, o in enumerate(group1):
        cp = pltpu.make_async_remote_copy(
            src_ref=red1.at[rank1],
            dst_ref=red1.at[rank1],
            send_sem=rs1.at[i],
            recv_sem=rr1.at[i],
            device_id=peer1(*o),
            device_id_type=MESH,
        )
        cp.start()
        cps1.append(cp)
    ex4 = Exchange(sizes, last, 2, 4, NZ, 16, pks4, pkr4, ssems.at[3], rsems.at[3])
    ex4.pack()
    ex4.start()
    for cp in cps1:
        cp.wait_recv()
    part = red1[0]
    for i in range(1, len(group1) + 1):
        part = part + red1[i]
    rank2 = gx * 2 + lax.rem(gz, 2)
    red2[rank2] = part
    cps2 = []
    for i, o in enumerate(group2):
        cp = pltpu.make_async_remote_copy(
            src_ref=red2.at[rank2],
            dst_ref=red2.at[rank2],
            send_sem=rs2.at[i],
            recv_sem=rr2.at[i],
            device_id=peer2(*o),
            device_id_type=MESH,
        )
        cp.start()
        cps2.append(cp)
    ex4.wait()
    ex4.unpack()
    for cp in cps2:
        cp.wait_recv()
    total = red2[0]
    for i in range(1, len(group2) + 1):
        total = total + red2[i]
    total = jnp.broadcast_to(jnp.sum(total, axis=1, keepdims=True), (8, LANES))
    rz, zq, rw, qw, zp, wp = (total[i : i + 1, :] for i in range(6))
    a0 = rz / zq
    rz1 = a0 * (a0 * qw - rw)
    beta = rz1 / rz
    gamma = 1.0 + beta
    a1 = rz1 / (gamma * gamma * zq - a0 * gamma * (zp + qw) + a0 * a0 * wp)
    c1 = jnp.broadcast_to(a0 + a1 * gamma, (WIN, LANES))
    c2 = jnp.broadcast_to(-a1 * a0, (WIN, LANES))

    def solution_plane(z):
        inside = plane_in(z, NZ)
        for s in range(2):
            x = c1 * last[0, s, z, LO:HI, :] + c2 * last[1, s, z, LO:HI, :]
            vv[s, z, LO:HI, :] = x * (mask[s, LO:HI, :] * inside)

    loop(4, 28, solution_plane)

    def copy_out(z):
        out_t[z] = vv[0, z + PAD, own, :]

    loop(0, NZ, copy_out)

    def sensitivity(z):
        here = [vv[s, z, LO:HI, :] for s in range(2)]
        ahead, behind = lane_neighbours(here[0], here[1], 1)
        inside = plane_in(z, NZ)
        for s in range(2):
            x = here[s]
            g = (x - vv[s, z - 1, LO:HI, :]) ** 2 + (x - vv[s, z + 1, LO:HI, :]) ** 2
            g = g + (x - vv[s, z, LO - 1 : HI - 1, :]) ** 2
            g = g + (x - vv[s, z, LO + 1 : HI + 1, :]) ** 2
            g = g + ((x - ahead[s]) ** 2 + (x - behind[s]) ** 2)
            r = fin[0, s, z, LO:HI, :] * (mask[s, LO:HI, :] * inside)
            v = (-3.0 * (1.0 - KMIN) * 0.5) * (r * r) * g
            z0[s, z, LO:HI, :] = v
            ww[s, z, LO:HI, :] = v * (1.0 / (1.0 + 6.0 * FILTER_WEIGHT))

    loop(5, 27, sensitivity)

    wlane = lane_iota(WIN)
    wrow = lax.broadcasted_iota(jnp.int32, (WIN, LANES), 0) + LO - PAD + gx * NX
    outside_row = jnp.where(wrow == 0, 1.0, 0.0) + jnp.where(wrow == gxs * NX - 1, 1.0, 0.0)
    outside_main = outside_row + jnp.where((wlane == 0) & (gy == 0), 1.0, 0.0)
    outside_main = outside_main + jnp.where((wlane == LANES - 1) & (gy == gys - 1), 1.0, 0.0)
    outside = (outside_main, outside_row)
    weight = FILTER_WEIGHT / (1.0 + 6.0 * FILTER_WEIGHT)

    def blur(f, f_next, first, end):
        def body(z):
            here = [f[s, z, LO:HI, :] for s in range(2)]
            ahead, behind = lane_neighbours(here[0], here[1], 1)
            inside = plane_in(z, NZ)
            g = gz * NZ + z - PAD
            ends = jnp.where((g == 0) | (g == gzs * NZ - 1), 1.0, 0.0).astype(F32)
            for s in range(2):
                t = f[s, z - 1, LO:HI, :] + f[s, z + 1, LO:HI, :]
                t = t + (f[s, z, LO - 1 : HI - 1, :] + f[s, z, LO + 1 : HI + 1, :])
                t = t + (ahead[s] + behind[s])
                t = t + (outside[s] + ends) * here[s]
                f_next[s, z, LO:HI, :] = ww[s, z, LO:HI, :] + t * (
                    mask[s, LO:HI, :] * (inside * weight)
                )

        loop(first, end, body)

    blur(z0, q0, 6, 26)
    blur(q0, z0, 7, 25)

    def blur_out(k):
        z = k + PAD
        f = z0
        here = [f[s, z, own, :] for s in range(2)]
        ahead, behind = lane_neighbours(here[0], here[1], 1)
        g = gz * NZ + k
        ends = jnp.where((g == 0) | (g == gzs * NZ - 1), 1.0, 0.0).astype(F32)
        t = f[0, z - 1, own, :] + f[0, z + 1, own, :]
        t = t + (f[0, z, PAD - 1 : PAD + NX - 1, :] + f[0, z, PAD + 1 : PAD + NX + 1, :])
        t = t + (ahead[0] + behind[0])
        t = t + (outside[0][PAD - LO : PAD - LO + NX] + ends) * here[0]
        out_f[k] = ww[0, z, own, :] + t * weight

    loop(0, NZ, blur_out)

    for ex in (ex1, ex2, ex3, ex4):
        ex.finish()
    for cp in cps1 + cps2:
        cp.wait_send()


def local(sizes, density, volume_power_source):
    shape = jax.ShapeDtypeStruct((NZ, NX, LANES), F32)
    vmem = pl.BlockSpec(memory_space=pltpu.VMEM)

    def fine(*lead, rows=FZ):
        return pltpu.VMEM((*lead, 2, FZ, rows, LANES), F32)

    def coarse(*lead):
        return pltpu.VMEM((*lead, 2, CZP, 32, LANES), F32)

    n = len(NEIGHBOURS)
    g1 = sizes[1] * (sizes[2] // 2)
    g2 = sizes[0] * 2
    scratch = [
        fine(2),
        fine(rows=40),
        *[fine() for _ in range(10)],
        fine(2),
        fine(),
        pltpu.VMEM((2, FZ, LANES), F32),
        coarse(3),
        coarse(1),
        *[coarse() for _ in range(8)],
        pltpu.VMEM((2, 24, LANES), F32),
        pltpu.VMEM((CZP, 2, FZ, LANES), F32),
        pltpu.VMEM((CZ, 1, NX, LANES), F32),
        pltpu.VMEM((2, 2, NX, LANES), F32),
        pltpu.VMEM((2, 2, 4, FZ, LANES), F32),
        pltpu.VMEM((3, 2, CX, LANES), F32),
        pltpu.VMEM((2, 3, 6, 24, LANES), F32),
        pltpu.VMEM((1, 2, CX, LANES), F32),
        pltpu.VMEM((2, 1, 6, 24, LANES), F32),
        pltpu.VMEM((2, 2, NX, LANES), F32),
        pltpu.VMEM((2, 2, 4, FZ, LANES), F32),
        pltpu.VMEM((g1, 8, LANES), F32),
        pltpu.VMEM((g2, 8, LANES), F32),
        pltpu.SemaphoreType.DMA((4, n)),
        pltpu.SemaphoreType.DMA((4, n)),
        pltpu.SemaphoreType.DMA((g1 - 1,)),
        pltpu.SemaphoreType.DMA((g1 - 1,)),
        pltpu.SemaphoreType.DMA((g2 - 1,)),
        pltpu.SemaphoreType.DMA((g2 - 1,)),
    ]
    return pl.pallas_call(
        functools.partial(kernel, sizes),
        out_shape=(shape, shape),
        in_specs=[vmem, vmem],
        out_specs=(vmem, vmem),
        scratch_shapes=scratch,
        compiler_params=pltpu.CompilerParams(
            collective_id=0, has_side_effects=True, vmem_limit_bytes=48 * 1024 * 1024
        ),
        name="heat_sink_step",
    )(density, volume_power_source)


def solution(mesh):
    sizes = tuple(mesh.shape[a] for a in ("gx", "gy", "gz"))
    spec = P("gz", "gx", "gy")
    return jax.shard_map(
        functools.partial(local, sizes),
        mesh=mesh,
        in_specs=(spec, spec),
        out_specs=(spec, spec),
        check_vma=False,
    )
```

```python
import functools
import itertools

import jax
import jax.numpy as jnp
from jax import lax
from jax.experimental import pallas as pl
from jax.experimental.pallas import tpu as pltpu
from jax.sharding import PartitionSpec as P

KMIN = 0.001
OMEGA = 0.8
FILTER_WEIGHT = 4.0
MESH = pl.DeviceIdType.MESH
F32 = jnp.float32

LANES = 128
NZ = NX = 16
CZ = CX = 8
PAD = 8
FZ = NZ + 2 * PAD
CZP = CZ + 2 * PAD
LO, HI = 4, 28
WIN = HI - LO
CLO, CWIN = 4, 16

NEIGHBOURS = sorted(
    (o for o in itertools.product((-1, 0, 1), repeat=3) if o != (0, 0, 0)),
    key=lambda o: (sum(map(abs, o)), o),
)


def place(sizes, offset):
    dz, dx, dy = offset
    gx, gy, gz = sizes
    return (
        lax.rem(lax.axis_index("gx") + dx + gx, gx),
        lax.rem(lax.axis_index("gy") + dy + gy, gy),
        lax.rem(lax.axis_index("gz") + dz + gz, gz),
    )


def other_core():
    gz = lax.axis_index("gz")
    return gz + 1 - 2 * lax.rem(gz, 2)


def lane_iota(rows):
    return lax.broadcasted_iota(jnp.int32, (rows, LANES), 1)


def lane_neighbours(main, side, step):
    lane = lane_iota(main.shape[0])
    up_main, up_side = pltpu.roll(main, LANES - step, 1), pltpu.roll(side, LANES - step, 1)
    dn_main, dn_side = pltpu.roll(main, step, 1), pltpu.roll(side, step, 1)
    last, first = lane >= LANES - step, lane < step
    ahead = (jnp.where(last, up_side, up_main), jnp.where(last, up_main, up_side))
    behind = (jnp.where(first, dn_side, dn_main), jnp.where(first, dn_main, dn_side))
    return ahead, behind


def pair_lanes(v):
    even = (lane_iota(v.shape[0]) & 1) == 0
    return v + jnp.where(even, pltpu.roll(v, LANES - 1, 1), pltpu.roll(v, 1, 1))


def loop(lower, upper, body):
    for i in range(lower, upper):
        body(i)


class Exchange:
    def __init__(self, sizes, arr, depth, rows, group, pks, pkr, ssem, rsem):
        self.sizes, self.arr, self.depth, self.rows, self.group = sizes, arr, depth, rows, group
        self.fields = arr.shape[0]
        self.per = LANES // group
        self.pks, self.pkr, self.ssem, self.rsem = pks, pkr, ssem, rsem
        self.copies = []

    def slot(self, plane, f):
        return divmod(plane * self.fields + f, self.per)

    def pack(self):
        (nz, pz, _), (nr, pr, _) = self.depth, self.rows
        slot_of = lane_iota(nr) >> (self.group.bit_length() - 1)
        packed = {}
        for p in range(nz):
            for f in range(self.fields):
                g, q = self.slot(p, f)
                v = self.arr[f, 0, pz + p, pr : pr + nr, :]
                v = pltpu.roll(v, self.group * q, 1) if q else v
                for side, at in ((0, q), (1, (q + self.per - 1) % self.per)):
                    old = packed.get((side, g))
                    packed[side, g] = v if old is None else jnp.where(slot_of == at, v, old)
        for (side, g), v in packed.items():
            self.pks[side, g] = v

    def start(self):
        (nz, pz, hz), (nr, pr, hr) = self.depth, self.rows
        groups = self.slot(nz - 1, self.fields - 1)[0] + 1
        for i, (dz, dx, dy) in enumerate(NEIGHBOURS):
            r = {0: (0, nr, pr), 1: (nr - hr, hr, pr - hr), -1: (0, hr, pr + nr)}[dx]
            if dy == 0:
                z = {0: (0, nz, pz), 1: (nz - hz, hz, pz - hz), -1: (0, hz, pz + nz)}[dz]
                src = self.arr.at[:, 0, pl.ds(pz + z[0], z[1]), pl.ds(pr + r[0], r[1]), :]
                dst = self.arr.at[:, 0, pl.ds(z[2], z[1]), pl.ds(r[2], r[1]), :]
            else:
                first = self.slot(nz - hz, 0)[0] if dz == 1 else 0
                end = self.slot(hz - 1, self.fields - 1)[0] + 1 if dz == -1 else groups
                g = pl.ds(first, end - first)
                src = self.pks.at[0 if dy == -1 else 1, g, pl.ds(r[0], r[1]), :]
                dst = self.pkr.at[0 if dy == -1 else 1, 1 - dz, g, pl.ds(r[2], r[1]), :]
            cp = pltpu.make_async_remote_copy(
                src_ref=src,
                dst_ref=dst,
                send_sem=self.ssem.at[i],
                recv_sem=self.rsem.at[i],
                device_id=place(self.sizes, (dz, dx, dy)),
                device_id_type=MESH,
            )
            cp.start()
            self.copies.append(cp)

    def wait(self):
        for cp in self.copies:
            cp.wait_recv()

    def unpack(self):
        (nz, pz, hz), (nr, pr, hr) = self.depth, self.rows
        rows = nr + 2 * pr
        slot_of = lane_iota(rows) >> (self.group.bit_length() - 1)
        for region, planes in ((0, range(nz - hz, nz)), (1, range(nz)), (2, range(hz))):
            for p in planes:
                for f in range(self.fields):
                    g, q = self.slot(p, f)
                    v = jnp.where(slot_of == q, self.pkr[0, region, g], self.pkr[1, region, g])
                    v = pltpu.roll(v, LANES - self.group * q, 1) if q else v
                    self.arr[f, 1, pz + (region - 1) * nz + p, 0:rows, :] = v

    def finish(self):
        for cp in self.copies:
            cp.wait_send()


def kernel(
    sizes,
    rho_ref,
    src_ref,
    out_t,
    out_f,
    fin,
    cond,
    kzm,
    kx,
    kyp,
    kym,
    diag,
    inv,
    zpre,
    vv,
    z0,
    q0,
    lz,
    lw,
    ww,
    mask,
    cin,
    cin2,
    rhs,
    cc,
    kcz,
    kcx,
    kcyp,
    kcym,
    cinv,
    ea,
    eb,
    cmask,
    refined,
    tmp,
    pks1,
    pkr1,
    pks2,
    pkr2,
    pks3,
    pkr3,
    pks4,
    pkr4,
    pks5,
    pkr5,
    red0,
    red1,
    red2,
    insem,
    ssems,
    rsems,
    rs0,
    rr0,
    rs1,
    rr1,
    rs2,
    rr2,
):
    gxs, gys, gzs = sizes
    gx, gy, gz = lax.axis_index("gx"), lax.axis_index("gy"), lax.axis_index("gz")

    def peer0(_):
        return (gx, gy, other_core())

    def peer1(o):
        return (gx, lax.rem(gy + o[0], gys), lax.rem(gz + 2 * o[1], gzs))

    def peer2(dx):
        return (lax.rem(gx + dx, gxs), gy, gz)

    group1 = [(dy, dz) for dy in range(gys) for dz in range(gzs // 2) if (dy, dz) != (0, 0)]
    group2 = list(range(1, gxs))

    loads = [
        pltpu.make_async_copy(ref, fin.at[f, 0, pl.ds(PAD, NZ), pl.ds(PAD, NX), :], insem.at[f])
        for f, ref in enumerate((rho_ref, src_ref))
    ]
    for cp in loads:
        cp.start()
    barrier = pltpu.get_barrier_semaphore()
    partners = [place(sizes, o) for o in NEIGHBOURS]
    for device in partners:
        pl.semaphore_signal(barrier, inc=1, device_id=device, device_id_type=MESH)

    row = lax.broadcasted_iota(jnp.int32, (FZ, LANES), 0) - PAD + gx * NX
    lane = lane_iota(FZ)
    row_in = (row >= 0) & (row < gxs * NX)
    left, right = gy > 0, gy < gys - 1
    right_end = jnp.where(right, 8, 0)
    left_start = jnp.where(left, LANES - 8, LANES)
    side_in = row_in & ((lane < right_end) | (lane >= left_start))
    mask[0] = jnp.where(row_in, 1.0, 0.0)
    mask[1] = jnp.where(side_in, 1.0, 0.0)
    crow = lax.broadcasted_iota(jnp.int32, (32, LANES), 0) - PAD + gx * CX
    clane = lane_iota(32)
    crow_in = (crow >= 0) & (crow < gxs * CX)
    cside_in = crow_in & (
        (clane < jnp.where(right, 16, 0)) | (clane >= jnp.where(left, LANES - 16, LANES))
    )
    cmask[0] = jnp.where(crow_in, 1.0, 0.0)
    cmask[1] = jnp.where(cside_in, 1.0, 0.0)

    def plane_in(z, cells):
        g = gz * cells + z - PAD
        return jnp.where((g >= 0) & (g < gzs * cells), 1.0, 0.0).astype(F32)

    ex1 = Exchange(sizes, fin, (NZ, PAD, 5), (NX, PAD, 5), 8, pks1, pkr1, ssems.at[0], rsems.at[0])
    for cp in loads:
        cp.wait()
    ex1.pack()
    pl.semaphore_wait(barrier, len(partners))
    ex1.start()
    ex1.wait()
    ex1.unpack()

    def conductivity(z):
        inside = plane_in(z, NZ)
        for s in range(2):
            r = fin[0, s, z]
            cond[s, z, 0:FZ, :] = (mask[s] * inside) * (KMIN + (1.0 - KMIN) * (r * r * r))

    loop(3, 29, conductivity)

    def faces(z):
        here = [cond[s, z, LO:HI, :] for s in range(2)]
        ahead, behind = lane_neighbours(here[0], here[1], 1)
        inside = plane_in(z, NZ)
        for s in range(2):
            c = here[s]
            zm = 0.5 * (cond[s, z - 1, LO:HI, :] + c)
            zp = 0.5 * (cond[s, z + 1, LO:HI, :] + c)
            xp = 0.5 * (cond[s, z, LO + 1 : HI + 1, :] + c)
            xm = 0.5 * (cond[s, z, LO - 1 : HI - 1, :] + c)
            yp = 0.5 * (ahead[s] + c)
            ym = 0.5 * (behind[s] + c)
            d = (zm + zp) + (xp + xm) + (yp + ym)
            kzm[s, z, LO:HI, :] = zm
            kx[s, z, LO:HI, :] = xp
            kx[s, z, LO - 1 : LO, :] = xm[0:1, :]
            kyp[s, z, LO:HI, :] = yp
            kym[s, z, LO:HI, :] = ym
            diag[s, z, LO:HI, :] = d
            ok = mask[s, LO:HI, :] * inside > 0.5
            i = jnp.where(ok, OMEGA / d, 0.0)
            inv[s, z, LO:HI, :] = i
            zpre[s, z, LO:HI, :] = i * fin[1, s, z, LO:HI, :]

    loop(4, 28, faces)

    def off_diagonal(field, z, lo, n, sides):
        here = [field[s, z, lo : lo + n, :] for s in range(2)]
        ahead, behind = lane_neighbours(here[0], here[1], 1)
        out = []
        for s in range(sides):
            t = kzm[s, z, lo : lo + n, :] * field[s, z - 1, lo : lo + n, :]
            t = t + kzm[s, z + 1, lo : lo + n, :] * field[s, z + 1, lo : lo + n, :]
            u = kx[s, z, lo : lo + n, :] * field[s, z, lo + 1 : lo + n + 1, :]
            u = u + kx[s, z, lo - 1 : lo + n - 1, :] * field[s, z, lo - 1 : lo + n - 1, :]
            v = kyp[s, z, lo : lo + n, :] * ahead[s] + kym[s, z, lo : lo + n, :] * behind[s]
            out.append((t + u) + v)
        return out

    even8 = (lane_iota(CX) & 1) == 0
    even24 = (lane_iota(24) & 1) == 0

    def block_rows(total, k):
        tmp[k] = pair_lanes(total)
        return tmp[k, pl.ds(0, CX, 2), :] + tmp[k, pl.ds(1, CX, 2), :]

    def coarse_rhs(load, field, k):
        total = None
        for j in range(2):
            z = PAD + 2 * k + j
            t = (1.0 - OMEGA) * load(z) + off_diagonal(field, z, PAD, NX, 1)[0]
            total = t if total is None else total + t
        return block_rows(total, k)

    for k in range(CZ):
        z = PAD + 2 * k
        c = cond[0, z, PAD : PAD + NX, :] + cond[0, z + 1, PAD : PAD + NX, :]
        c = 0.125 * block_rows(c, CZ + k)
        r = coarse_rhs(lambda z: fin[1, 0, z, PAD : PAD + NX, :], zpre, k)
        cin[0, 0, PAD + k, PAD : PAD + CX, :] = jnp.where(even8, c, r)

    ex2 = Exchange(sizes, cin, (CZ, PAD, 6), (CX, PAD, 6), 16, pks2, pkr2, ssems.at[1], rsems.at[1])
    ex2.pack()
    ex2.start()
    ex2.wait()
    ex2.unpack()

    def split(v):
        return (
            jnp.where(even24, v, pltpu.roll(v, 1, 1)),
            jnp.where(even24, pltpu.roll(v, LANES - 1, 1), v),
        )

    def coarse_masked(vc):
        inside = plane_in(vc, CZ)
        for s in range(2):
            c, r = split(cin[0, s, vc, 0:24, :])
            cc[s, vc, 0:24, :] = jnp.where(cmask[s, 0:24, :] * inside > 0.5, c, 0.0)
            rhs[s, vc, 0:24, :] = r

    loop(2, 22, coarse_masked)

    def coarse_faces(vc):
        lo, hi = 3, 27
        here = [cc[s, vc, lo:hi, :] for s in range(2)]
        ahead, behind = lane_neighbours(here[0], here[1], 2)
        inside = plane_in(vc, CZ)
        for s in range(2):
            c = here[s]
            zm = 2.0 * (c + cc[s, vc - 1, lo:hi, :])
            zp = 2.0 * (c + cc[s, vc + 1, lo:hi, :])
            xm = 2.0 * (c + cc[s, vc, lo - 1 : hi - 1, :])
            xp = 2.0 * (c + cc[s, vc, lo + 1 : hi + 1, :])
            yp = 2.0 * (c + ahead[s])
            ym = 2.0 * (c + behind[s])
            kcz[s, vc, lo:hi, :] = zm
            kcx[s, vc, lo:hi, :] = xp
            kcyp[s, vc, lo:hi, :] = yp
            kcym[s, vc, lo:hi, :] = ym
            d = (zm + zp) + (xm + xp) + (yp + ym)
            i = jnp.where(cmask[s, lo:hi, :] * inside > 0.5, OMEGA / d, 0.0)
            cinv[s, vc, lo:hi, :] = i
            ea[s, vc, lo:hi, :] = i * rhs[s, vc, lo:hi, :]

    loop(3, 21, coarse_faces)

    def sweep(e, e_next, first, end):
        lo, hi = CLO, CLO + CWIN

        def body(vc):
            here = [e[s, vc, lo:hi, :] for s in range(2)]
            ahead, behind = lane_neighbours(here[0], here[1], 2)
            for s in range(2):
                t = kcz[s, vc, lo:hi, :] * e[s, vc - 1, lo:hi, :]
                t = t + kcz[s, vc + 1, lo:hi, :] * e[s, vc + 1, lo:hi, :]
                u = kcx[s, vc, lo:hi, :] * e[s, vc, lo + 1 : hi + 1, :]
                u = u + kcx[s, vc, lo - 1 : hi - 1, :] * e[s, vc, lo - 1 : hi - 1, :]
                v = kcyp[s, vc, lo:hi, :] * ahead[s] + kcym[s, vc, lo:hi, :] * behind[s]
                r = rhs[s, vc, lo:hi, :] + ((t + u) + v)
                e_next[s, vc, lo:hi, :] = (1.0 - OMEGA) * here[s] + cinv[s, vc, lo:hi, :] * r

        loop(first, end, body)

    def add_refined(e, base, first, end):
        def body(vc):
            for s in range(2):
                v = e[s, vc, CLO : CLO + CWIN, :]
                refined[vc, s, pl.ds(0, CWIN, 2), :] = v
                refined[vc, s, pl.ds(1, CWIN, 2), :] = v
                fine = refined[vc, s, LO:HI, :]
                for j in range(2):
                    z = 2 * vc - PAD + j
                    vv[s, z, LO:HI, :] = base[s, z, LO:HI, :] + fine

        loop(first, end, body)

    sweep(ea, eb, 4, 20)
    sweep(eb, ea, 5, 19)
    sweep(ea, eb, 6, 18)
    add_refined(eb, zpre, 6, 18)

    def post(z):
        b = off_diagonal(vv, z, LO, WIN, 2)
        for s in range(2):
            z0[s, z, LO:HI, :] = (1.0 - OMEGA) * vv[s, z, LO:HI, :] + inv[s, z, LO:HI, :] * (
                fin[1, s, z, LO:HI, :] + b[s]
            )

    loop(5, 27, post)

    def image(z):
        b = off_diagonal(z0, z, LO, WIN, 2)
        for s in range(2):
            q = diag[s, z, LO:HI, :] * z0[s, z, LO:HI, :] - b[s]
            q0[s, z, LO:HI, :] = q
            zpre[s, z, LO:HI, :] = inv[s, z, LO:HI, :] * q

    loop(6, 26, image)

    for k in range(CZ // 2):
        r = [
            coarse_rhs(lambda z: q0[0, z, PAD : PAD + NX, :], zpre, 2 * k + j) for j in range(2)
        ]
        cin2[0, 0, PAD // 2 + k, PAD : PAD + CX, :] = jnp.where(even8, r[0], r[1])
    ex3 = Exchange(
        sizes, cin2, (CZ // 2, PAD // 2, 2), (CX, PAD, 4), 8, pks3, pkr3, ssems.at[2], rsems.at[2]
    )
    ex3.pack()
    ex3.start()

    own = slice(PAD, PAD + NX)
    for z in range(PAD, PAD + NZ):
        lz[0, 0, z, own, :] = z0[0, z, own, :]
    ex4 = Exchange(sizes, lz, (NZ, PAD, 4), (NX, PAD, 4), 8, pks4, pkr4, ssems.at[3], rsems.at[3])
    ex4.pack()
    ex3.wait()
    ex4.start()
    ex3.unpack()

    def first_correction(v2):
        for s in range(2):
            for j, r in enumerate(split(cin2[0, s, v2, 0:24, :])):
                vc = 2 * v2 + j
                rhs[s, vc, 0:24, :] = r
                ea[s, vc, 3:27, :] = cinv[s, vc, 3:27, :] * rhs[s, vc, 3:27, :]

    loop(2, 10, first_correction)
    sweep(ea, eb, 5, 19)
    sweep(eb, ea, 6, 18)
    sweep(ea, eb, 7, 17)
    add_refined(eb, zpre, 7, 17)

    def post_second(z):
        b = off_diagonal(vv, z, LO, WIN, 2)
        for s in range(2):
            ww[s, z, LO:HI, :] = (1.0 - OMEGA) * vv[s, z, LO:HI, :] + inv[s, z, LO:HI, :] * (
                q0[s, z, LO:HI, :] + b[s]
            )

    loop(7, 25, post_second)

    def dots(z, acc):
        w = ww[0, z, own, :]
        zz = z0[0, z, own, :]
        q = q0[0, z, own, :]
        r = fin[1, 0, z, own, :]
        p = diag[0, z, own, :] * w - off_diagonal(ww, z, PAD, NX, 1)[0]
        lw[0, 0, z, own, :] = w
        terms = (r * zz, zz * q, r * w, q * w, zz * p, w * p)
        return tuple(a + t[0:8] + t[8:16] for a, t in zip(acc, terms))

    zero = jnp.zeros((8, LANES), F32)
    acc = (zero,) * 6
    for z in range(PAD, PAD + NZ):
        acc = dots(z, acc)
    which = lax.broadcasted_iota(jnp.int32, (8, LANES), 0)
    part = zero
    for i, a in enumerate(acc):
        part = jnp.where(which == i, jnp.sum(a, axis=0, keepdims=True), part)

    reduce_copies = []

    def share(part, slots, rank, offsets, peer, ssem, rsem):
        slots[rank] = part
        copies = []
        for i, o in enumerate(offsets):
            cp = pltpu.make_async_remote_copy(
                src_ref=slots.at[rank],
                dst_ref=slots.at[rank],
                send_sem=ssem.at[i],
                recv_sem=rsem.at[i],
                device_id=peer(o),
                device_id_type=MESH,
            )
            cp.start()
            copies.append(cp)
        reduce_copies.extend(copies)
        return copies

    def total_of(slots, copies):
        for cp in copies:
            cp.wait_recv()
        values = [slots[i] for i in range(slots.shape[0])]
        while len(values) > 1:
            values = [a + b for a, b in zip(values[0::2], values[1::2])]
        return values[0]

    copies = share(part, red0, lax.rem(gz, 2), [0], peer0, rs0, rr0)
    ex5 = Exchange(sizes, lw, (NZ, PAD, 4), (NX, PAD, 4), 8, pks5, pkr5, ssems.at[4], rsems.at[4])
    ex5.pack()
    part = total_of(red0, copies)
    copies = share(part, red1, gy * (gzs // 2) + gz // 2, group1, peer1, rs1, rr1)
    ex5.start()
    ex4.wait()
    ex4.unpack()
    part = total_of(red1, copies)
    copies = share(part, red2, gx, group2, peer2, rs2, rr2)
    ex5.wait()
    ex5.unpack()
    total = total_of(red2, copies)
    total = jnp.broadcast_to(jnp.sum(total, axis=1, keepdims=True), (8, LANES))
    rz, zq, rw, qw, zp, wp = (total[i : i + 1, :] for i in range(6))
    a0 = rz / zq
    rz1 = a0 * (a0 * qw - rw)
    beta = rz1 / rz
    gamma = 1.0 + beta
    a1 = rz1 / (gamma * gamma * zq - a0 * gamma * (zp + qw) + a0 * a0 * wp)
    c1 = jnp.broadcast_to(a0 + a1 * gamma, (WIN, LANES))
    c2 = jnp.broadcast_to(-a1 * a0, (WIN, LANES))

    def solution_plane(z):
        inside = plane_in(z, NZ)
        for s in range(2):
            x = c1 * lz[0, s, z, LO:HI, :] + c2 * lw[0, s, z, LO:HI, :]
            vv[s, z, LO:HI, :] = x * (mask[s, LO:HI, :] * inside)

    loop(4, 28, solution_plane)

    def copy_out(z):
        out_t[z] = vv[0, z + PAD, own, :]

    loop(0, NZ, copy_out)

    def sensitivity(z):
        here = [vv[s, z, LO:HI, :] for s in range(2)]
        ahead, behind = lane_neighbours(here[0], here[1], 1)
        inside = plane_in(z, NZ)
        for s in range(2):
            x = here[s]
            g = (x - vv[s, z - 1, LO:HI, :]) ** 2 + (x - vv[s, z + 1, LO:HI, :]) ** 2
            g = g + (x - vv[s, z, LO - 1 : HI - 1, :]) ** 2
            g = g + (x - vv[s, z, LO + 1 : HI + 1, :]) ** 2
            g = g + ((x - ahead[s]) ** 2 + (x - behind[s]) ** 2)
            r = fin[0, s, z, LO:HI, :] * (mask[s, LO:HI, :] * inside)
            v = (-3.0 * (1.0 - KMIN) * 0.5) * (r * r) * g
            z0[s, z, LO:HI, :] = v
            ww[s, z, LO:HI, :] = v * (1.0 / (1.0 + 6.0 * FILTER_WEIGHT))

    loop(5, 27, sensitivity)

    wlane = lane_iota(WIN)
    wrow = lax.broadcasted_iota(jnp.int32, (WIN, LANES), 0) + LO - PAD + gx * NX
    outside_row = jnp.where(wrow == 0, 1.0, 0.0) + jnp.where(wrow == gxs * NX - 1, 1.0, 0.0)
    outside_main = outside_row + jnp.where((wlane == 0) & (gy == 0), 1.0, 0.0)
    outside_main = outside_main + jnp.where((wlane == LANES - 1) & (gy == gys - 1), 1.0, 0.0)
    outside = (outside_main, outside_row)
    weight = FILTER_WEIGHT / (1.0 + 6.0 * FILTER_WEIGHT)

    def blur(f, f_next, first, end):
        def body(z):
            here = [f[s, z, LO:HI, :] for s in range(2)]
            ahead, behind = lane_neighbours(here[0], here[1], 1)
            inside = plane_in(z, NZ)
            g = gz * NZ + z - PAD
            ends = jnp.where((g == 0) | (g == gzs * NZ - 1), 1.0, 0.0).astype(F32)
            for s in range(2):
                t = f[s, z - 1, LO:HI, :] + f[s, z + 1, LO:HI, :]
                t = t + (f[s, z, LO - 1 : HI - 1, :] + f[s, z, LO + 1 : HI + 1, :])
                t = t + (ahead[s] + behind[s])
                t = t + (outside[s] + ends) * here[s]
                f_next[s, z, LO:HI, :] = ww[s, z, LO:HI, :] + t * (
                    mask[s, LO:HI, :] * (inside * weight)
                )

        loop(first, end, body)

    blur(z0, q0, 6, 26)
    blur(q0, z0, 7, 25)

    def blur_out(k):
        z = k + PAD
        f = z0
        here = [f[s, z, own, :] for s in range(2)]
        ahead, behind = lane_neighbours(here[0], here[1], 1)
        g = gz * NZ + k
        ends = jnp.where((g == 0) | (g == gzs * NZ - 1), 1.0, 0.0).astype(F32)
        t = f[0, z - 1, own, :] + f[0, z + 1, own, :]
        t = t + (f[0, z, PAD - 1 : PAD + NX - 1, :] + f[0, z, PAD + 1 : PAD + NX + 1, :])
        t = t + (ahead[0] + behind[0])
        t = t + (outside[0][PAD - LO : PAD - LO + NX] + ends) * here[0]
        out_f[k] = ww[0, z, own, :] + t * weight

    loop(0, NZ, blur_out)

    for ex in (ex1, ex2, ex3, ex4, ex5):
        ex.finish()
    for cp in reduce_copies:
        cp.wait_send()


def local(sizes, density, volume_power_source):
    shape = pltpu.VMEM((NZ, NX, LANES), F32)
    vmem = pl.BlockSpec(memory_space=pltpu.VMEM)

    def fine(*lead, rows=FZ):
        return pltpu.VMEM((*lead, 2, FZ, rows, LANES), F32)

    def coarse(*lead):
        return pltpu.VMEM((*lead, 2, CZP, 32, LANES), F32)

    def packs(groups, rows):
        own = pltpu.VMEM((2, groups, rows, LANES), F32)
        return own, pltpu.VMEM((2, 3, groups, rows + 2 * PAD, LANES), F32)

    n = len(NEIGHBOURS)
    counts = (2, sizes[1] * (sizes[2] // 2), sizes[0])
    scratch = [
        fine(2),
        fine(rows=40),
        *[fine() for _ in range(10)],
        fine(1),
        fine(1),
        fine(),
        pltpu.VMEM((2, FZ, LANES), F32),
        coarse(1),
        pltpu.VMEM((1, 2, CZP // 2, 32, LANES), F32),
        *[coarse() for _ in range(9)],
        pltpu.VMEM((2, 32, LANES), F32),
        pltpu.VMEM((CZP, 2, FZ, LANES), F32),
        pltpu.VMEM((2 * CZ, NX, LANES), F32),
        *packs(2, NX),
        *packs(1, CX),
        *packs(1, CX),
        *packs(1, NX),
        *packs(1, NX),
        *[pltpu.VMEM((c, 8, LANES), F32) for c in counts],
        pltpu.SemaphoreType.DMA((2,)),
        pltpu.SemaphoreType.DMA((5, n)),
        pltpu.SemaphoreType.DMA((5, n)),
        *[pltpu.SemaphoreType.DMA((c - 1,)) for c in counts for _ in range(2)],
    ]
    return pl.pallas_call(
        functools.partial(kernel, sizes),
        out_shape=(shape, shape),
        in_specs=[pl.BlockSpec(memory_space=pltpu.HBM)] * 2,
        out_specs=(vmem, vmem),
        scratch_shapes=scratch,
        compiler_params=pltpu.CompilerParams(
            collective_id=0, has_side_effects=True, vmem_limit_bytes=48 * 1024 * 1024
        ),
        name="heat_sink_step",
    )(*(pltpu.with_memory_space_constraint(x, pltpu.HBM) for x in (density, volume_power_source)))


def solution(mesh):
    sizes = tuple(mesh.shape[a] for a in ("gx", "gy", "gz"))
    spec = P("gz", "gx", "gy")
    return jax.shard_map(
        functools.partial(local, sizes),
        mesh=mesh,
        in_specs=(spec, spec),
        out_specs=(spec, spec),
        check_vma=False,
    )
```

```python
import functools
import itertools

import jax
import jax.numpy as jnp
from jax import lax
from jax.experimental import pallas as pl
from jax.experimental.pallas import tpu as pltpu
from jax.sharding import PartitionSpec as P

KMIN = 0.001
OMEGA = 0.8
FILTER_WEIGHT = 4.0
MESH = pl.DeviceIdType.MESH
F32 = jnp.float32

LANES = 128
NZ = NX = 16
CZ = CX = 8
PAD = 8
FZ = NZ + 2 * PAD
CZP = CZ + 2 * PAD
LO, HI = 4, 28
WIN = HI - LO
CLO, CWIN = 4, 16

NEIGHBOURS = sorted(
    (o for o in itertools.product((-1, 0, 1), repeat=3) if o != (0, 0, 0)),
    key=lambda o: (sum(map(abs, o)), o),
)


def place(sizes, offset):
    dz, dx, dy = offset
    gx, gy, gz = sizes
    return (
        lax.rem(lax.axis_index("gx") + dx + gx, gx),
        lax.rem(lax.axis_index("gy") + dy + gy, gy),
        lax.rem(lax.axis_index("gz") + dz + gz, gz),
    )


def other_core():
    gz = lax.axis_index("gz")
    return gz + 1 - 2 * lax.rem(gz, 2)


def lane_iota(rows):
    return lax.broadcasted_iota(jnp.int32, (rows, LANES), 1)


def lane_neighbours(main, side, step):
    lane = lane_iota(main.shape[0])
    up_main, up_side = pltpu.roll(main, LANES - step, 1), pltpu.roll(side, LANES - step, 1)
    dn_main, dn_side = pltpu.roll(main, step, 1), pltpu.roll(side, step, 1)
    last, first = lane >= LANES - step, lane < step
    ahead = (jnp.where(last, up_side, up_main), jnp.where(last, up_main, up_side))
    behind = (jnp.where(first, dn_side, dn_main), jnp.where(first, dn_main, dn_side))
    return ahead, behind


def pair_lanes(v):
    even = (lane_iota(v.shape[0]) & 1) == 0
    return v + jnp.where(even, pltpu.roll(v, LANES - 1, 1), pltpu.roll(v, 1, 1))


def loop(lower, upper, body):
    for i in range(lower, upper):
        body(i)


def wait_rows(span, rows, sem):
    view = span.at[pl.ds(0, rows)]
    pltpu.make_async_copy(view, view, sem).wait()


class Exchange:
    def __init__(self, sizes, arr, depth, rows, group, pks, pkr, ssem, rsem, span):
        self.sizes, self.arr, self.depth, self.rows, self.group = sizes, arr, depth, rows, group
        self.fields = arr.shape[0]
        self.per = LANES // group
        self.pks, self.pkr, self.ssem, self.rsem, self.span = pks, pkr, ssem, rsem, span
        self.sent = 0

    def slot(self, plane, f):
        return divmod(plane * self.fields + f, self.per)

    def pack(self):
        (nz, pz, _), (nr, pr, _) = self.depth, self.rows
        slot_of = lane_iota(nr) >> (self.group.bit_length() - 1)
        packed = {}
        for p in range(nz):
            for f in range(self.fields):
                g, q = self.slot(p, f)
                v = self.arr[f, 0, pz + p, pr : pr + nr, :]
                v = pltpu.roll(v, self.group * q, 1) if q else v
                for side, at in ((0, q), (1, (q + self.per - 1) % self.per)):
                    old = packed.get((side, g))
                    packed[side, g] = v if old is None else jnp.where(slot_of == at, v, old)
        for (side, g), v in packed.items():
            self.pks[side, g] = v

    def start(self):
        (nz, pz, hz), (nr, pr, hr) = self.depth, self.rows
        groups = self.slot(nz - 1, self.fields - 1)[0] + 1
        for dz, dx, dy in NEIGHBOURS:
            r = {0: (0, nr, pr), 1: (nr - hr, hr, pr - hr), -1: (0, hr, pr + nr)}[dx]
            if dy == 0:
                z = {0: (0, nz, pz), 1: (nz - hz, hz, pz - hz), -1: (0, hz, pz + nz)}[dz]
                src = self.arr.at[:, 0, pl.ds(pz + z[0], z[1]), pl.ds(pr + r[0], r[1]), :]
                dst = self.arr.at[:, 0, pl.ds(z[2], z[1]), pl.ds(r[2], r[1]), :]
            else:
                first = self.slot(nz - hz, 0)[0] if dz == 1 else 0
                end = self.slot(hz - 1, self.fields - 1)[0] + 1 if dz == -1 else groups
                g = pl.ds(first, end - first)
                src = self.pks.at[0 if dy == -1 else 1, g, pl.ds(r[0], r[1]), :]
                dst = self.pkr.at[0 if dy == -1 else 1, 1 - dz, g, pl.ds(r[2], r[1]), :]
            cp = pltpu.make_async_remote_copy(
                src_ref=src,
                dst_ref=dst,
                send_sem=self.ssem,
                recv_sem=self.rsem,
                device_id=place(self.sizes, (dz, dx, dy)),
                device_id_type=MESH,
            )
            cp.start()
            count = 1
            for d in src.shape:
                count *= d
            self.sent += count // LANES

    def wait(self):
        wait_rows(self.span, self.sent, self.rsem)

    def unpack(self):
        (nz, pz, hz), (nr, pr, hr) = self.depth, self.rows
        rows = nr + 2 * pr
        slot_of = lane_iota(rows) >> (self.group.bit_length() - 1)
        for region, planes in ((0, range(nz - hz, nz)), (1, range(nz)), (2, range(hz))):
            for p in planes:
                for f in range(self.fields):
                    g, q = self.slot(p, f)
                    v = jnp.where(slot_of == q, self.pkr[0, region, g], self.pkr[1, region, g])
                    v = pltpu.roll(v, LANES - self.group * q, 1) if q else v
                    self.arr[f, 1, pz + (region - 1) * nz + p, 0:rows, :] = v

    def finish(self):
        wait_rows(self.span, self.sent, self.ssem)


def kernel(
    sizes,
    rho_ref,
    src_ref,
    out_t,
    out_f,
    fin,
    cond,
    kzm,
    kx,
    kyp,
    kym,
    diag,
    inv,
    zpre,
    vv,
    z0,
    q0,
    lz,
    lw,
    ww,
    mask,
    cin,
    cin2,
    rhs,
    cc,
    kcz,
    kcx,
    kcyp,
    kcym,
    cinv,
    ea,
    eb,
    cmask,
    refined,
    tmp,
    pks1,
    pkr1,
    pks2,
    pkr2,
    pks3,
    pkr3,
    pks4,
    pkr4,
    pks5,
    pkr5,
    red0,
    red1,
    red2,
    span,
    insem,
    ssems,
    rsems,
):
    gxs, gys, gzs = sizes
    gx, gy, gz = lax.axis_index("gx"), lax.axis_index("gy"), lax.axis_index("gz")

    def peer0(_):
        return (gx, gy, other_core())

    def peer1(o):
        return (gx, lax.rem(gy + o[0], gys), lax.rem(gz + 2 * o[1], gzs))

    def peer2(dx):
        return (lax.rem(gx + dx, gxs), gy, gz)

    group1 = [(dy, dz) for dy in range(gys) for dz in range(gzs // 2) if (dy, dz) != (0, 0)]
    group2 = list(range(1, gxs))

    loads = [
        pltpu.make_async_copy(ref, fin.at[f, 0, pl.ds(PAD, NZ), pl.ds(PAD, NX), :], insem.at[f])
        for f, ref in enumerate((rho_ref, src_ref))
    ]
    for cp in loads:
        cp.start()
    barrier = pltpu.get_barrier_semaphore()
    partners = [place(sizes, o) for o in NEIGHBOURS]
    for device in partners:
        pl.semaphore_signal(barrier, inc=1, device_id=device, device_id_type=MESH)

    row = lax.broadcasted_iota(jnp.int32, (FZ, LANES), 0) - PAD + gx * NX
    lane = lane_iota(FZ)
    row_in = (row >= 0) & (row < gxs * NX)
    left, right = gy > 0, gy < gys - 1
    right_end = jnp.where(right, 8, 0)
    left_start = jnp.where(left, LANES - 8, LANES)
    side_in = row_in & ((lane < right_end) | (lane >= left_start))
    mask[0] = jnp.where(row_in, 1.0, 0.0)
    mask[1] = jnp.where(side_in, 1.0, 0.0)
    crow = lax.broadcasted_iota(jnp.int32, (32, LANES), 0) - PAD + gx * CX
    clane = lane_iota(32)
    crow_in = (crow >= 0) & (crow < gxs * CX)
    cside_in = crow_in & (
        (clane < jnp.where(right, 16, 0)) | (clane >= jnp.where(left, LANES - 16, LANES))
    )
    cmask[0] = jnp.where(crow_in, 1.0, 0.0)
    cmask[1] = jnp.where(cside_in, 1.0, 0.0)

    def plane_in(z, cells):
        g = gz * cells + z - PAD
        return jnp.where((g >= 0) & (g < gzs * cells), 1.0, 0.0).astype(F32)

    ex1 = Exchange(sizes, fin, (NZ, PAD, 5), (NX, PAD, 5), 8, pks1, pkr1, ssems.at[0], rsems.at[0], span)
    for cp in loads:
        cp.wait()
    ex1.pack()
    pl.semaphore_wait(barrier, len(partners))
    ex1.start()
    ex1.wait()
    ex1.unpack()

    def conductivity(z):
        inside = plane_in(z, NZ)
        for s in range(2):
            r = fin[0, s, z]
            cond[s, z, 0:FZ, :] = (mask[s] * inside) * (KMIN + (1.0 - KMIN) * (r * r * r))

    loop(3, 29, conductivity)

    def faces(z):
        here = [cond[s, z, LO:HI, :] for s in range(2)]
        ahead, behind = lane_neighbours(here[0], here[1], 1)
        inside = plane_in(z, NZ)
        for s in range(2):
            c = here[s]
            zm = 0.5 * (cond[s, z - 1, LO:HI, :] + c)
            zp = 0.5 * (cond[s, z + 1, LO:HI, :] + c)
            xp = 0.5 * (cond[s, z, LO + 1 : HI + 1, :] + c)
            xm = 0.5 * (cond[s, z, LO - 1 : HI - 1, :] + c)
            yp = 0.5 * (ahead[s] + c)
            ym = 0.5 * (behind[s] + c)
            d = (zm + zp) + (xp + xm) + (yp + ym)
            kzm[s, z, LO:HI, :] = zm
            kx[s, z, LO:HI, :] = xp
            kx[s, z, LO - 1 : LO, :] = xm[0:1, :]
            kyp[s, z, LO:HI, :] = yp
            kym[s, z, LO:HI, :] = ym
            diag[s, z, LO:HI, :] = d
            ok = mask[s, LO:HI, :] * inside > 0.5
            i = jnp.where(ok, OMEGA / d, 0.0)
            inv[s, z, LO:HI, :] = i
            zpre[s, z, LO:HI, :] = i * fin[1, s, z, LO:HI, :]

    loop(4, 28, faces)

    def off_diagonal(field, z, lo, n, sides):
        here = [field[s, z, lo : lo + n, :] for s in range(2)]
        ahead, behind = lane_neighbours(here[0], here[1], 1)
        out = []
        for s in range(sides):
            t = kzm[s, z, lo : lo + n, :] * field[s, z - 1, lo : lo + n, :]
            t = t + kzm[s, z + 1, lo : lo + n, :] * field[s, z + 1, lo : lo + n, :]
            u = kx[s, z, lo : lo + n, :] * field[s, z, lo + 1 : lo + n + 1, :]
            u = u + kx[s, z, lo - 1 : lo + n - 1, :] * field[s, z, lo - 1 : lo + n - 1, :]
            v = kyp[s, z, lo : lo + n, :] * ahead[s] + kym[s, z, lo : lo + n, :] * behind[s]
            out.append((t + u) + v)
        return out

    even8 = (lane_iota(CX) & 1) == 0
    even24 = (lane_iota(24) & 1) == 0

    def block_rows(total, k):
        tmp[k] = pair_lanes(total)
        return tmp[k, pl.ds(0, CX, 2), :] + tmp[k, pl.ds(1, CX, 2), :]

    def coarse_rhs(load, field, k):
        total = None
        for j in range(2):
            z = PAD + 2 * k + j
            t = (1.0 - OMEGA) * load(z) + off_diagonal(field, z, PAD, NX, 1)[0]
            total = t if total is None else total + t
        return block_rows(total, k)

    for k in range(CZ):
        z = PAD + 2 * k
        c = cond[0, z, PAD : PAD + NX, :] + cond[0, z + 1, PAD : PAD + NX, :]
        c = 0.125 * block_rows(c, CZ + k)
        r = coarse_rhs(lambda z: fin[1, 0, z, PAD : PAD + NX, :], zpre, k)
        cin[0, 0, PAD + k, PAD : PAD + CX, :] = jnp.where(even8, c, r)

    ex2 = Exchange(sizes, cin, (CZ, PAD, 6), (CX, PAD, 6), 16, pks2, pkr2, ssems.at[1], rsems.at[1], span)
    ex2.pack()
    ex2.start()
    ex2.wait()
    ex2.unpack()

    def split(v):
        return (
            jnp.where(even24, v, pltpu.roll(v, 1, 1)),
            jnp.where(even24, pltpu.roll(v, LANES - 1, 1), v),
        )

    def coarse_masked(vc):
        inside = plane_in(vc, CZ)
        for s in range(2):
            c, r = split(cin[0, s, vc, 0:24, :])
            cc[s, vc, 0:24, :] = jnp.where(cmask[s, 0:24, :] * inside > 0.5, c, 0.0)
            rhs[s, vc, 0:24, :] = r

    loop(2, 22, coarse_masked)

    def coarse_faces(vc):
        lo, hi = 3, 27
        here = [cc[s, vc, lo:hi, :] for s in range(2)]
        ahead, behind = lane_neighbours(here[0], here[1], 2)
        inside = plane_in(vc, CZ)
        for s in range(2):
            c = here[s]
            zm = 2.0 * (c + cc[s, vc - 1, lo:hi, :])
            zp = 2.0 * (c + cc[s, vc + 1, lo:hi, :])
            xm = 2.0 * (c + cc[s, vc, lo - 1 : hi - 1, :])
            xp = 2.0 * (c + cc[s, vc, lo + 1 : hi + 1, :])
            yp = 2.0 * (c + ahead[s])
            ym = 2.0 * (c + behind[s])
            kcz[s, vc, lo:hi, :] = zm
            kcx[s, vc, lo:hi, :] = xp
            kcyp[s, vc, lo:hi, :] = yp
            kcym[s, vc, lo:hi, :] = ym
            d = (zm + zp) + (xm + xp) + (yp + ym)
            i = jnp.where(cmask[s, lo:hi, :] * inside > 0.5, OMEGA / d, 0.0)
            cinv[s, vc, lo:hi, :] = i
            ea[s, vc, lo:hi, :] = i * rhs[s, vc, lo:hi, :]

    loop(3, 21, coarse_faces)

    def sweep(e, e_next, first, end):
        lo, hi = CLO, CLO + CWIN

        def body(vc):
            here = [e[s, vc, lo:hi, :] for s in range(2)]
            ahead, behind = lane_neighbours(here[0], here[1], 2)
            for s in range(2):
                t = kcz[s, vc, lo:hi, :] * e[s, vc - 1, lo:hi, :]
                t = t + kcz[s, vc + 1, lo:hi, :] * e[s, vc + 1, lo:hi, :]
                u = kcx[s, vc, lo:hi, :] * e[s, vc, lo + 1 : hi + 1, :]
                u = u + kcx[s, vc, lo - 1 : hi - 1, :] * e[s, vc, lo - 1 : hi - 1, :]
                v = kcyp[s, vc, lo:hi, :] * ahead[s] + kcym[s, vc, lo:hi, :] * behind[s]
                r = rhs[s, vc, lo:hi, :] + ((t + u) + v)
                e_next[s, vc, lo:hi, :] = (1.0 - OMEGA) * here[s] + cinv[s, vc, lo:hi, :] * r

        loop(first, end, body)

    def add_refined(e, base, first, end):
        def body(vc):
            for s in range(2):
                v = e[s, vc, CLO : CLO + CWIN, :]
                refined[vc, s, pl.ds(0, CWIN, 2), :] = v
                refined[vc, s, pl.ds(1, CWIN, 2), :] = v
                fine = refined[vc, s, LO:HI, :]
                for j in range(2):
                    z = 2 * vc - PAD + j
                    vv[s, z, LO:HI, :] = base[s, z, LO:HI, :] + fine

        loop(first, end, body)

    sweep(ea, eb, 4, 20)
    sweep(eb, ea, 5, 19)
    sweep(ea, eb, 6, 18)
    add_refined(eb, zpre, 6, 18)

    def post(z):
        b = off_diagonal(vv, z, LO, WIN, 2)
        for s in range(2):
            z0[s, z, LO:HI, :] = (1.0 - OMEGA) * vv[s, z, LO:HI, :] + inv[s, z, LO:HI, :] * (
                fin[1, s, z, LO:HI, :] + b[s]
            )

    loop(5, 27, post)

    def image(z):
        b = off_diagonal(z0, z, LO, WIN, 2)
        for s in range(2):
            q = diag[s, z, LO:HI, :] * z0[s, z, LO:HI, :] - b[s]
            q0[s, z, LO:HI, :] = q
            zpre[s, z, LO:HI, :] = inv[s, z, LO:HI, :] * q

    loop(6, 26, image)

    for k in range(CZ // 2):
        r = [
            coarse_rhs(lambda z: q0[0, z, PAD : PAD + NX, :], zpre, 2 * k + j) for j in range(2)
        ]
        cin2[0, 0, PAD // 2 + k, PAD : PAD + CX, :] = jnp.where(even8, r[0], r[1])
    ex3 = Exchange(
        sizes, cin2, (CZ // 2, PAD // 2, 2), (CX, PAD, 4), 8, pks3, pkr3, ssems.at[2], rsems.at[2], span
    )
    ex3.pack()
    ex3.start()

    own = slice(PAD, PAD + NX)
    for z in range(PAD, PAD + NZ):
        lz[0, 0, z, own, :] = z0[0, z, own, :]
    ex4 = Exchange(sizes, lz, (NZ, PAD, 4), (NX, PAD, 4), 8, pks4, pkr4, ssems.at[3], rsems.at[3], span)
    ex4.pack()
    ex3.wait()
    ex4.start()
    ex3.unpack()

    def first_correction(v2):
        for s in range(2):
            for j, r in enumerate(split(cin2[0, s, v2, 0:24, :])):
                vc = 2 * v2 + j
                rhs[s, vc, 0:24, :] = r
                ea[s, vc, 3:27, :] = cinv[s, vc, 3:27, :] * rhs[s, vc, 3:27, :]

    loop(2, 10, first_correction)
    sweep(ea, eb, 5, 19)
    sweep(eb, ea, 6, 18)
    sweep(ea, eb, 7, 17)
    add_refined(eb, zpre, 7, 17)

    def post_second(z):
        b = off_diagonal(vv, z, LO, WIN, 2)
        for s in range(2):
            ww[s, z, LO:HI, :] = (1.0 - OMEGA) * vv[s, z, LO:HI, :] + inv[s, z, LO:HI, :] * (
                q0[s, z, LO:HI, :] + b[s]
            )

    loop(7, 25, post_second)

    def dots(z, acc):
        w = ww[0, z, own, :]
        zz = z0[0, z, own, :]
        q = q0[0, z, own, :]
        r = fin[1, 0, z, own, :]
        p = diag[0, z, own, :] * w - off_diagonal(ww, z, PAD, NX, 1)[0]
        lw[0, 0, z, own, :] = w
        terms = (r * zz, zz * q, r * w, q * w, zz * p, w * p)
        return tuple(a + t[0:8] + t[8:16] for a, t in zip(acc, terms))

    zero = jnp.zeros((8, LANES), F32)
    acc = (zero,) * 6
    for z in range(PAD, PAD + NZ):
        acc = dots(z, acc)
    which = lax.broadcasted_iota(jnp.int32, (8, LANES), 0)
    part = zero
    for i, a in enumerate(acc):
        part = jnp.where(which == i, jnp.sum(a, axis=0, keepdims=True), part)

    shared = []

    def share(part, slots, rank, offsets, peer, sem):
        slots[rank] = part
        for o in offsets:
            pltpu.make_async_remote_copy(
                src_ref=slots.at[rank],
                dst_ref=slots.at[rank],
                send_sem=ssems.at[sem],
                recv_sem=rsems.at[sem],
                device_id=peer(o),
                device_id_type=MESH,
            ).start()
        shared.append((8 * len(offsets), sem))

    def total_of(slots):
        rows, sem = shared[-1]
        wait_rows(span, rows, rsems.at[sem])
        values = [slots[i] for i in range(slots.shape[0])]
        while len(values) > 1:
            values = [a + b for a, b in zip(values[0::2], values[1::2])]
        return values[0]

    share(part, red0, lax.rem(gz, 2), [0], peer0, 5)
    ex5 = Exchange(sizes, lw, (NZ, PAD, 4), (NX, PAD, 4), 8, pks5, pkr5, ssems.at[4], rsems.at[4], span)
    ex5.pack()
    part = total_of(red0)
    share(part, red1, gy * (gzs // 2) + gz // 2, group1, peer1, 6)
    ex5.start()
    ex4.wait()
    ex4.unpack()
    part = total_of(red1)
    share(part, red2, gx, group2, peer2, 7)
    ex5.wait()
    ex5.unpack()
    total = total_of(red2)
    total = jnp.broadcast_to(jnp.sum(total, axis=1, keepdims=True), (8, LANES))
    rz, zq, rw, qw, zp, wp = (total[i : i + 1, :] for i in range(6))
    a0 = rz / zq
    rz1 = a0 * (a0 * qw - rw)
    beta = rz1 / rz
    gamma = 1.0 + beta
    a1 = rz1 / (gamma * gamma * zq - a0 * gamma * (zp + qw) + a0 * a0 * wp)
    c1 = jnp.broadcast_to(a0 + a1 * gamma, (WIN, LANES))
    c2 = jnp.broadcast_to(-a1 * a0, (WIN, LANES))

    def solution_plane(z):
        inside = plane_in(z, NZ)
        for s in range(2):
            x = c1 * lz[0, s, z, LO:HI, :] + c2 * lw[0, s, z, LO:HI, :]
            vv[s, z, LO:HI, :] = x * (mask[s, LO:HI, :] * inside)

    loop(4, 28, solution_plane)

    def copy_out(z):
        out_t[z] = vv[0, z + PAD, own, :]

    loop(0, NZ, copy_out)

    def sensitivity(z):
        here = [vv[s, z, LO:HI, :] for s in range(2)]
        ahead, behind = lane_neighbours(here[0], here[1], 1)
        inside = plane_in(z, NZ)
        for s in range(2):
            x = here[s]
            g = (x - vv[s, z - 1, LO:HI, :]) ** 2 + (x - vv[s, z + 1, LO:HI, :]) ** 2
            g = g + (x - vv[s, z, LO - 1 : HI - 1, :]) ** 2
            g = g + (x - vv[s, z, LO + 1 : HI + 1, :]) ** 2
            g = g + ((x - ahead[s]) ** 2 + (x - behind[s]) ** 2)
            r = fin[0, s, z, LO:HI, :] * (mask[s, LO:HI, :] * inside)
            v = (-3.0 * (1.0 - KMIN) * 0.5) * (r * r) * g
            z0[s, z, LO:HI, :] = v
            ww[s, z, LO:HI, :] = v * (1.0 / (1.0 + 6.0 * FILTER_WEIGHT))

    loop(5, 27, sensitivity)

    wlane = lane_iota(WIN)
    wrow = lax.broadcasted_iota(jnp.int32, (WIN, LANES), 0) + LO - PAD + gx * NX
    outside_row = jnp.where(wrow == 0, 1.0, 0.0) + jnp.where(wrow == gxs * NX - 1, 1.0, 0.0)
    outside_main = outside_row + jnp.where((wlane == 0) & (gy == 0), 1.0, 0.0)
    outside_main = outside_main + jnp.where((wlane == LANES - 1) & (gy == gys - 1), 1.0, 0.0)
    outside = (outside_main, outside_row)
    weight = FILTER_WEIGHT / (1.0 + 6.0 * FILTER_WEIGHT)

    def blur(f, f_next, first, end):
        def body(z):
            here = [f[s, z, LO:HI, :] for s in range(2)]
            ahead, behind = lane_neighbours(here[0], here[1], 1)
            inside = plane_in(z, NZ)
            g = gz * NZ + z - PAD
            ends = jnp.where((g == 0) | (g == gzs * NZ - 1), 1.0, 0.0).astype(F32)
            for s in range(2):
                t = f[s, z - 1, LO:HI, :] + f[s, z + 1, LO:HI, :]
                t = t + (f[s, z, LO - 1 : HI - 1, :] + f[s, z, LO + 1 : HI + 1, :])
                t = t + (ahead[s] + behind[s])
                t = t + (outside[s] + ends) * here[s]
                f_next[s, z, LO:HI, :] = ww[s, z, LO:HI, :] + t * (
                    mask[s, LO:HI, :] * (inside * weight)
                )

        loop(first, end, body)

    blur(z0, q0, 6, 26)
    blur(q0, z0, 7, 25)

    def blur_out(k):
        z = k + PAD
        f = z0
        here = [f[s, z, own, :] for s in range(2)]
        ahead, behind = lane_neighbours(here[0], here[1], 1)
        g = gz * NZ + k
        ends = jnp.where((g == 0) | (g == gzs * NZ - 1), 1.0, 0.0).astype(F32)
        t = f[0, z - 1, own, :] + f[0, z + 1, own, :]
        t = t + (f[0, z, PAD - 1 : PAD + NX - 1, :] + f[0, z, PAD + 1 : PAD + NX + 1, :])
        t = t + (ahead[0] + behind[0])
        t = t + (outside[0][PAD - LO : PAD - LO + NX] + ends) * here[0]
        out_f[k] = ww[0, z, own, :] + t * weight

    loop(0, NZ, blur_out)

    for ex in (ex1, ex2, ex3, ex4, ex5):
        ex.finish()
    for rows, sem in shared:
        wait_rows(span, rows, ssems.at[sem])


def store(t_ref, f_ref, out_t, out_f, sem):
    copies = [
        pltpu.make_async_copy(src, dst, sem.at[i])
        for i, (src, dst) in enumerate(((t_ref, out_t), (f_ref, out_f)))
    ]
    for cp in copies:
        cp.start()
    for cp in copies:
        cp.wait()


def local(sizes, density, volume_power_source):
    shape = pltpu.VMEM((NZ, NX, LANES), F32)
    vmem = pl.BlockSpec(memory_space=pltpu.VMEM)

    def fine(*lead, rows=FZ):
        return pltpu.VMEM((*lead, 2, FZ, rows, LANES), F32)

    def coarse(*lead):
        return pltpu.VMEM((*lead, 2, CZP, 32, LANES), F32)

    def packs(groups, rows):
        own = pltpu.VMEM((2, groups, rows, LANES), F32)
        return own, pltpu.VMEM((2, 3, groups, rows + 2 * PAD, LANES), F32)

    counts = (2, sizes[1] * (sizes[2] // 2), sizes[0])
    scratch = [
        fine(2),
        fine(rows=40),
        *[fine() for _ in range(10)],
        fine(1),
        fine(1),
        fine(),
        pltpu.VMEM((2, FZ, LANES), F32),
        coarse(1),
        pltpu.VMEM((1, 2, CZP // 2, 32, LANES), F32),
        *[coarse() for _ in range(9)],
        pltpu.VMEM((2, 32, LANES), F32),
        pltpu.VMEM((CZP, 2, FZ, LANES), F32),
        pltpu.VMEM((2 * CZ, NX, LANES), F32),
        *packs(2, NX),
        *packs(1, CX),
        *packs(1, CX),
        *packs(1, NX),
        *packs(1, NX),
        *[pltpu.VMEM((c, 8, LANES), F32) for c in counts],
        pltpu.VMEM((2048, LANES), F32),
        pltpu.SemaphoreType.DMA((2,)),
        pltpu.SemaphoreType.DMA((8,)),
        pltpu.SemaphoreType.DMA((8,)),
    ]
    outs = pl.pallas_call(
        functools.partial(kernel, sizes),
        out_shape=(shape, shape),
        in_specs=[pl.BlockSpec(memory_space=pltpu.HBM)] * 2,
        out_specs=(vmem, vmem),
        scratch_shapes=scratch,
        compiler_params=pltpu.CompilerParams(
            collective_id=0, has_side_effects=True, vmem_limit_bytes=48 * 1024 * 1024
        ),
        name="heat_sink_step",
    )(*(pltpu.with_memory_space_constraint(x, pltpu.HBM) for x in (density, volume_power_source)))
    hbm = pl.BlockSpec(memory_space=pltpu.HBM)
    return pl.pallas_call(
        store,
        out_shape=(jax.ShapeDtypeStruct((NZ, NX, LANES), F32),) * 2,
        in_specs=[vmem, vmem],
        out_specs=(hbm, hbm),
        scratch_shapes=[pltpu.SemaphoreType.DMA((2,))],
        name="store_outputs",
    )(*(pltpu.with_memory_space_constraint(x, pltpu.VMEM) for x in outs))


def solution(mesh):
    sizes = tuple(mesh.shape[a] for a in ("gx", "gy", "gz"))
    spec = P("gz", "gx", "gy")
    return jax.shard_map(
        functools.partial(local, sizes),
        mesh=mesh,
        in_specs=(spec, spec),
        out_specs=(spec, spec),
        check_vma=False,
    )
```

```python
import functools
import itertools

import jax
import jax.numpy as jnp
from jax import lax
from jax.experimental import pallas as pl
from jax.experimental.pallas import tpu as pltpu
from jax.sharding import PartitionSpec as P

KMIN = 0.001
OMEGA = 0.8
FILTER_WEIGHT = 4.0
MESH = pl.DeviceIdType.MESH
F32 = jnp.float32

LANES = 128
NZ = NX = 16
CZ = CX = 8
PAD = 8
FZ = NZ + 2 * PAD
CZP = CZ + 2 * PAD
LO, HI = 4, 28
WIN = HI - LO
CLO, CWIN = 4, 16

NEIGHBOURS = sorted(
    (o for o in itertools.product((-1, 0, 1), repeat=3) if o != (0, 0, 0)),
    key=lambda o: (-sum(map(abs, o)), o[2] == 0, o),
)


def place(sizes, offset):
    dz, dx, dy = offset
    gx, gy, gz = sizes
    return (
        lax.rem(lax.axis_index("gx") + dx + gx, gx),
        lax.rem(lax.axis_index("gy") + dy + gy, gy),
        lax.rem(lax.axis_index("gz") + dz + gz, gz),
    )


def other_core():
    gz = lax.axis_index("gz")
    return gz + 1 - 2 * lax.rem(gz, 2)


def lane_iota(rows):
    return lax.broadcasted_iota(jnp.int32, (rows, LANES), 1)


def lane_neighbours(main, side, step):
    lane = lane_iota(main.shape[0])
    up_main, up_side = pltpu.roll(main, LANES - step, 1), pltpu.roll(side, LANES - step, 1)
    dn_main, dn_side = pltpu.roll(main, step, 1), pltpu.roll(side, step, 1)
    last, first = lane >= LANES - step, lane < step
    ahead = (jnp.where(last, up_side, up_main), jnp.where(last, up_main, up_side))
    behind = (jnp.where(first, dn_side, dn_main), jnp.where(first, dn_main, dn_side))
    return ahead, behind


def pair_lanes(v):
    even = (lane_iota(v.shape[0]) & 1) == 0
    return v + jnp.where(even, pltpu.roll(v, LANES - 1, 1), pltpu.roll(v, 1, 1))


def loop(lower, upper, body):
    for i in range(lower, upper):
        body(i)


def wait_rows(span, rows, sem):
    view = span.at[pl.ds(0, rows)]
    pltpu.make_async_copy(view, view, sem).wait()


class Exchange:
    def __init__(self, sizes, arr, depth, rows, group, pks, pkr, ssem, rsem, span):
        self.sizes, self.arr, self.depth, self.rows, self.group = sizes, arr, depth, rows, group
        self.fields = arr.shape[0]
        self.per = LANES // group
        self.pks, self.pkr, self.ssem, self.rsem, self.span = pks, pkr, ssem, rsem, span
        self.sent = 0

    def slot(self, plane, f):
        return divmod(plane * self.fields + f, self.per)

    def pack(self):
        (nz, pz, _), (nr, pr, _) = self.depth, self.rows
        slot_of = lane_iota(nr) >> (self.group.bit_length() - 1)
        packed = {}
        for p in range(nz):
            for f in range(self.fields):
                g, q = self.slot(p, f)
                v = self.arr[f, 0, pz + p, pr : pr + nr, :]
                v = pltpu.roll(v, self.group * q, 1) if q else v
                for side, at in ((0, q), (1, (q + self.per - 1) % self.per)):
                    old = packed.get((side, g))
                    packed[side, g] = v if old is None else jnp.where(slot_of == at, v, old)
        for (side, g), v in packed.items():
            self.pks[side, g] = v

    def start(self):
        (nz, pz, hz), (nr, pr, hr) = self.depth, self.rows
        groups = self.slot(nz - 1, self.fields - 1)[0] + 1
        for dz, dx, dy in NEIGHBOURS:
            r = {0: (0, nr, pr), 1: (nr - hr, hr, pr - hr), -1: (0, hr, pr + nr)}[dx]
            if dy == 0:
                z = {0: (0, nz, pz), 1: (nz - hz, hz, pz - hz), -1: (0, hz, pz + nz)}[dz]
                src = self.arr.at[:, 0, pl.ds(pz + z[0], z[1]), pl.ds(pr + r[0], r[1]), :]
                dst = self.arr.at[:, 0, pl.ds(z[2], z[1]), pl.ds(r[2], r[1]), :]
            else:
                first = self.slot(nz - hz, 0)[0] if dz == 1 else 0
                end = self.slot(hz - 1, self.fields - 1)[0] + 1 if dz == -1 else groups
                g = pl.ds(first, end - first)
                src = self.pks.at[0 if dy == -1 else 1, g, pl.ds(r[0], r[1]), :]
                dst = self.pkr.at[0 if dy == -1 else 1, 1 - dz, g, pl.ds(r[2], r[1]), :]
            cp = pltpu.make_async_remote_copy(
                src_ref=src,
                dst_ref=dst,
                send_sem=self.ssem,
                recv_sem=self.rsem,
                device_id=place(self.sizes, (dz, dx, dy)),
                device_id_type=MESH,
            )
            cp.start()
            count = 1
            for d in src.shape:
                count *= d
            self.sent += count // LANES

    def wait(self):
        wait_rows(self.span, self.sent, self.rsem)

    def unpack(self, near=0, far=PAD):
        (nz, pz, hz), (nr, pr, hr) = self.depth, self.rows
        rows = nr + 2 * pr
        slot_of = lane_iota(rows) >> (self.group.bit_length() - 1)
        for region, planes in ((0, range(nz - hz, nz)), (1, range(nz)), (2, range(hz))):
            for p in planes:
                outside = {0: nz - p, 1: 0, 2: p + 1}[region]
                if not near <= outside <= far:
                    continue
                for f in range(self.fields):
                    g, q = self.slot(p, f)
                    v = jnp.where(slot_of == q, self.pkr[0, region, g], self.pkr[1, region, g])
                    v = pltpu.roll(v, LANES - self.group * q, 1) if q else v
                    self.arr[f, 1, pz + (region - 1) * nz + p, 0:rows, :] = v

    def finish(self):
        wait_rows(self.span, self.sent, self.ssem)


def kernel(
    sizes,
    rho_ref,
    src_ref,
    out_t,
    out_f,
    fin,
    cond,
    kzm,
    kx,
    kyp,
    kym,
    diag,
    inv,
    zpre,
    vv,
    z0,
    q0,
    lz,
    lw,
    ww,
    mask,
    cin,
    cin2,
    rhs,
    cc,
    kcz,
    kcx,
    kcyp,
    kcym,
    cinv,
    ea,
    eb,
    cmask,
    refined,
    tmp,
    pks1,
    pkr1,
    pks2,
    pkr2,
    pks3,
    pkr3,
    pks4,
    pkr4,
    pks5,
    pkr5,
    red0,
    red1,
    red2,
    parts,
    span,
    insem,
    ssems,
    rsems,
):
    gxs, gys, gzs = sizes
    gx, gy, gz = lax.axis_index("gx"), lax.axis_index("gy"), lax.axis_index("gz")

    def peer0(_):
        return (gx, gy, other_core())

    def peer1(o):
        return (gx, lax.rem(gy + o[0], gys), lax.rem(gz + 2 * o[1], gzs))

    def peer2(dx):
        return (lax.rem(gx + dx, gxs), gy, gz)

    def hops(d, n):
        return min(d, n - d)

    group1 = [(dy, dz) for dy in range(gys) for dz in range(gzs // 2) if (dy, dz) != (0, 0)]
    group1.sort(key=lambda o: -hops(o[0], gys) - hops(o[1], gzs // 2))
    group2 = sorted(range(1, gxs), key=lambda o: -hops(o, gxs))

    loads = [
        pltpu.make_async_copy(ref, fin.at[f, 0, pl.ds(PAD, NZ), pl.ds(PAD, NX), :], insem.at[f])
        for f, ref in enumerate((rho_ref, src_ref))
    ]
    for cp in loads:
        cp.start()
    barrier = pltpu.get_barrier_semaphore()
    partners = [place(sizes, o) for o in NEIGHBOURS]
    for device in partners:
        pl.semaphore_signal(barrier, inc=1, device_id=device, device_id_type=MESH)

    def plane_in(z, cells):
        g = gz * cells + z - PAD
        return jnp.where((g >= 0) & (g < gzs * cells), 1.0, 0.0).astype(F32)

    ex1 = Exchange(sizes, fin, (NZ, PAD, 5), (NX, PAD, 5), 8, pks1, pkr1, ssems.at[0], rsems.at[0], span)
    for cp in loads:
        cp.wait()
    ex1.pack()
    pl.semaphore_wait(barrier, len(partners))
    ex1.start()

    row = lax.broadcasted_iota(jnp.int32, (FZ, LANES), 0) - PAD + gx * NX
    lane = lane_iota(FZ)
    row_in = (row >= 0) & (row < gxs * NX)
    left, right = gy > 0, gy < gys - 1
    right_end = jnp.where(right, 8, 0)
    left_start = jnp.where(left, LANES - 8, LANES)
    side_in = row_in & ((lane < right_end) | (lane >= left_start))
    mask[0] = jnp.where(row_in, 1.0, 0.0)
    mask[1] = jnp.where(side_in, 1.0, 0.0)
    crow = lax.broadcasted_iota(jnp.int32, (32, LANES), 0) - PAD + gx * CX
    clane = lane_iota(32)
    crow_in = (crow >= 0) & (crow < gxs * CX)
    cside_in = crow_in & (
        (clane < jnp.where(right, 16, 0)) | (clane >= jnp.where(left, LANES - 16, LANES))
    )
    cmask[0] = jnp.where(crow_in, 1.0, 0.0)
    cmask[1] = jnp.where(cside_in, 1.0, 0.0)

    ex1.wait()
    ex1.unpack(0, 2)

    def conductivity(z):
        inside = plane_in(z, NZ)
        for s in range(2):
            r = fin[0, s, z]
            cond[s, z, 0:FZ, :] = (mask[s] * inside) * (KMIN + (1.0 - KMIN) * (r * r * r))

    loop(6, 26, conductivity)

    def faces(z):
        here = [cond[s, z, LO:HI, :] for s in range(2)]
        ahead, behind = lane_neighbours(here[0], here[1], 1)
        inside = plane_in(z, NZ)
        for s in range(2):
            c = here[s]
            zm = 0.5 * (cond[s, z - 1, LO:HI, :] + c)
            zp = 0.5 * (cond[s, z + 1, LO:HI, :] + c)
            xp = 0.5 * (cond[s, z, LO + 1 : HI + 1, :] + c)
            xm = 0.5 * (cond[s, z, LO - 1 : HI - 1, :] + c)
            yp = 0.5 * (ahead[s] + c)
            ym = 0.5 * (behind[s] + c)
            d = (zm + zp) + (xp + xm) + (yp + ym)
            kzm[s, z, LO:HI, :] = zm
            kx[s, z, LO:HI, :] = xp
            kx[s, z, LO - 1 : LO, :] = xm[0:1, :]
            kyp[s, z, LO:HI, :] = yp
            kym[s, z, LO:HI, :] = ym
            diag[s, z, LO:HI, :] = d
            ok = mask[s, LO:HI, :] * inside > 0.5
            i = jnp.where(ok, OMEGA / d, 0.0)
            inv[s, z, LO:HI, :] = i
            zpre[s, z, LO:HI, :] = i * fin[1, s, z, LO:HI, :]

    loop(7, 25, faces)

    def off_diagonal(field, z, lo, n, sides):
        here = [field[s, z, lo : lo + n, :] for s in range(2)]
        ahead, behind = lane_neighbours(here[0], here[1], 1)
        out = []
        for s in range(sides):
            t = kzm[s, z, lo : lo + n, :] * field[s, z - 1, lo : lo + n, :]
            t = t + kzm[s, z + 1, lo : lo + n, :] * field[s, z + 1, lo : lo + n, :]
            u = kx[s, z, lo : lo + n, :] * field[s, z, lo + 1 : lo + n + 1, :]
            u = u + kx[s, z, lo - 1 : lo + n - 1, :] * field[s, z, lo - 1 : lo + n - 1, :]
            v = kyp[s, z, lo : lo + n, :] * ahead[s] + kym[s, z, lo : lo + n, :] * behind[s]
            out.append((t + u) + v)
        return out

    even8 = (lane_iota(CX) & 1) == 0
    even24 = (lane_iota(24) & 1) == 0

    def block_rows(total, k):
        tmp[k] = pair_lanes(total)
        return tmp[k, pl.ds(0, CX, 2), :] + tmp[k, pl.ds(1, CX, 2), :]

    def coarse_rhs(load, field, k):
        total = None
        for j in range(2):
            z = PAD + 2 * k + j
            t = (1.0 - OMEGA) * load(z) + off_diagonal(field, z, PAD, NX, 1)[0]
            total = t if total is None else total + t
        return block_rows(total, k)

    for k in range(CZ):
        z = PAD + 2 * k
        c = cond[0, z, PAD : PAD + NX, :] + cond[0, z + 1, PAD : PAD + NX, :]
        c = 0.125 * block_rows(c, CZ + k)
        r = coarse_rhs(lambda z: fin[1, 0, z, PAD : PAD + NX, :], zpre, k)
        cin[0, 0, PAD + k, PAD : PAD + CX, :] = jnp.where(even8, c, r)

    ex2 = Exchange(sizes, cin, (CZ, PAD, 6), (CX, PAD, 6), 16, pks2, pkr2, ssems.at[1], rsems.at[1], span)
    ex2.pack()
    ex2.start()
    ex1.unpack(3, 5)
    loop(3, 6, conductivity)
    loop(26, 29, conductivity)
    loop(4, 7, faces)
    loop(25, 28, faces)
    ex2.wait()
    ex2.unpack()

    def split(v):
        return (
            jnp.where(even24, v, pltpu.roll(v, 1, 1)),
            jnp.where(even24, pltpu.roll(v, LANES - 1, 1), v),
        )

    def coarse_masked(vc):
        inside = plane_in(vc, CZ)
        for s in range(2):
            c, r = split(cin[0, s, vc, 0:24, :])
            cc[s, vc, 0:24, :] = jnp.where(cmask[s, 0:24, :] * inside > 0.5, c, 0.0)
            rhs[s, vc, 0:24, :] = r

    loop(2, 22, coarse_masked)

    def coarse_faces(vc):
        lo, hi = 3, 27
        here = [cc[s, vc, lo:hi, :] for s in range(2)]
        ahead, behind = lane_neighbours(here[0], here[1], 2)
        inside = plane_in(vc, CZ)
        for s in range(2):
            c = here[s]
            zm = 2.0 * (c + cc[s, vc - 1, lo:hi, :])
            zp = 2.0 * (c + cc[s, vc + 1, lo:hi, :])
            xm = 2.0 * (c + cc[s, vc, lo - 1 : hi - 1, :])
            xp = 2.0 * (c + cc[s, vc, lo + 1 : hi + 1, :])
            yp = 2.0 * (c + ahead[s])
            ym = 2.0 * (c + behind[s])
            kcz[s, vc, lo:hi, :] = zm
            kcx[s, vc, lo:hi, :] = xp
            kcyp[s, vc, lo:hi, :] = yp
            kcym[s, vc, lo:hi, :] = ym
            d = (zm + zp) + (xm + xp) + (yp + ym)
            i = jnp.where(cmask[s, lo:hi, :] * inside > 0.5, OMEGA / d, 0.0)
            cinv[s, vc, lo:hi, :] = i
            ea[s, vc, lo:hi, :] = i * rhs[s, vc, lo:hi, :]

    loop(3, 21, coarse_faces)

    def sweep(e, e_next, first, end):
        lo, hi = CLO, CLO + CWIN

        def body(vc):
            here = [e[s, vc, lo:hi, :] for s in range(2)]
            ahead, behind = lane_neighbours(here[0], here[1], 2)
            for s in range(2):
                t = kcz[s, vc, lo:hi, :] * e[s, vc - 1, lo:hi, :]
                t = t + kcz[s, vc + 1, lo:hi, :] * e[s, vc + 1, lo:hi, :]
                u = kcx[s, vc, lo:hi, :] * e[s, vc, lo + 1 : hi + 1, :]
                u = u + kcx[s, vc, lo - 1 : hi - 1, :] * e[s, vc, lo - 1 : hi - 1, :]
                v = kcyp[s, vc, lo:hi, :] * ahead[s] + kcym[s, vc, lo:hi, :] * behind[s]
                r = rhs[s, vc, lo:hi, :] + ((t + u) + v)
                e_next[s, vc, lo:hi, :] = (1.0 - OMEGA) * here[s] + cinv[s, vc, lo:hi, :] * r

        loop(first, end, body)

    def add_refined(e, base, first, end):
        def body(vc):
            for s in range(2):
                v = e[s, vc, CLO : CLO + CWIN, :]
                refined[vc, s, pl.ds(0, CWIN, 2), :] = v
                refined[vc, s, pl.ds(1, CWIN, 2), :] = v
                fine = refined[vc, s, LO:HI, :]
                for j in range(2):
                    z = 2 * vc - PAD + j
                    vv[s, z, LO:HI, :] = base[s, z, LO:HI, :] + fine

        loop(first, end, body)

    sweep(ea, eb, 4, 20)
    sweep(eb, ea, 5, 19)
    sweep(ea, eb, 6, 18)
    add_refined(eb, zpre, 6, 18)

    def post(z):
        b = off_diagonal(vv, z, LO, WIN, 2)
        for s in range(2):
            z0[s, z, LO:HI, :] = (1.0 - OMEGA) * vv[s, z, LO:HI, :] + inv[s, z, LO:HI, :] * (
                fin[1, s, z, LO:HI, :] + b[s]
            )

    loop(6, 26, post)

    def image(z):
        b = off_diagonal(z0, z, LO, WIN, 2)
        for s in range(2):
            q = diag[s, z, LO:HI, :] * z0[s, z, LO:HI, :] - b[s]
            q0[s, z, LO:HI, :] = q
            zpre[s, z, LO:HI, :] = inv[s, z, LO:HI, :] * q

    loop(7, 25, image)

    for k in range(CZ // 2):
        r = [
            coarse_rhs(lambda z: q0[0, z, PAD : PAD + NX, :], zpre, 2 * k + j) for j in range(2)
        ]
        cin2[0, 0, PAD // 2 + k, PAD : PAD + CX, :] = jnp.where(even8, r[0], r[1])
    ex3 = Exchange(
        sizes, cin2, (CZ // 2, PAD // 2, 2), (CX, PAD, 4), 8, pks3, pkr3, ssems.at[2], rsems.at[2], span
    )
    ex3.pack()
    ex3.start()

    own = slice(PAD, PAD + NX)
    for z in range(PAD, PAD + NZ):
        lz[0, 0, z, own, :] = z0[0, z, own, :]
    ex4 = Exchange(sizes, lz, (NZ, PAD, 4), (NX, PAD, 4), 8, pks4, pkr4, ssems.at[3], rsems.at[3], span)
    ex4.pack()
    ex4.start()
    for z in (5, 26):
        post(z)
    for z in (6, 25):
        image(z)
    ex3.wait()
    ex3.unpack()

    def first_correction(v2):
        for s in range(2):
            for j, r in enumerate(split(cin2[0, s, v2, 0:24, :])):
                vc = 2 * v2 + j
                rhs[s, vc, 0:24, :] = r
                ea[s, vc, 3:27, :] = cinv[s, vc, 3:27, :] * rhs[s, vc, 3:27, :]

    loop(2, 10, first_correction)
    sweep(ea, eb, 5, 19)
    sweep(eb, ea, 6, 18)
    sweep(ea, eb, 7, 17)
    add_refined(eb, zpre, 7, 17)

    def post_second(z):
        b = off_diagonal(vv, z, LO, WIN, 2)
        for s in range(2):
            ww[s, z, LO:HI, :] = (1.0 - OMEGA) * vv[s, z, LO:HI, :] + inv[s, z, LO:HI, :] * (
                q0[s, z, LO:HI, :] + b[s]
            )

    loop(8, 24, post_second)

    for z in range(PAD, PAD + NZ):
        lw[0, 0, z, own, :] = ww[0, z, own, :] - z0[0, z, own, :]
    ex5 = Exchange(sizes, lw, (NZ, PAD, 4), (NX, PAD, 4), 8, pks5, pkr5, ssems.at[4], rsems.at[4], span)
    ex5.pack()
    ex5.start()
    for z in (7, 24):
        post_second(z)

    def dots(z, acc):
        w = ww[0, z, own, :]
        zz = z0[0, z, own, :]
        q = q0[0, z, own, :]
        r = fin[1, 0, z, own, :]
        p = diag[0, z, own, :] * w - off_diagonal(ww, z, PAD, NX, 1)[0]
        terms = (r * zz, zz * q, r * w, q * w, zz * p, w * p)
        return tuple(a + t[0:8] + t[8:16] for a, t in zip(acc, terms))

    zero = jnp.zeros((8, LANES), F32)
    acc = (zero,) * 6
    for z in range(PAD, PAD + NZ):
        acc = dots(z, acc)
    which = lax.broadcasted_iota(jnp.int32, (8, LANES), 0)
    part = zero
    for i, a in enumerate(acc):
        part = jnp.where(which == i, jnp.sum(a, axis=0, keepdims=True), part)

    shared = []

    def share(part, slots, rank, offsets, peer, sem):
        slots[rank] = part
        for o in offsets:
            pltpu.make_async_remote_copy(
                src_ref=slots.at[rank],
                dst_ref=slots.at[rank],
                send_sem=ssems.at[sem],
                recv_sem=rsems.at[sem],
                device_id=peer(o),
                device_id_type=MESH,
            ).start()
        shared.append((8 * len(offsets), sem))

    def total_of(slots):
        rows, sem = shared[-1]
        wait_rows(span, rows, rsems.at[sem])
        values = [slots[i] for i in range(slots.shape[0])]
        while len(values) > 1:
            values = [a + b for a, b in zip(values[0::2], values[1::2])]
        return values[0]

    wlane = lane_iota(WIN)
    wrow = lax.broadcasted_iota(jnp.int32, (WIN, LANES), 0) + LO - PAD + gx * NX
    outside_row = jnp.where(wrow == 0, 1.0, 0.0) + jnp.where(wrow == gxs * NX - 1, 1.0, 0.0)
    outside_main = outside_row + jnp.where((wlane == 0) & (gy == 0), 1.0, 0.0)
    outside_main = outside_main + jnp.where((wlane == LANES - 1) & (gy == gys - 1), 1.0, 0.0)
    outside = (outside_main, outside_row)
    weight = FILTER_WEIGHT / (1.0 + 6.0 * FILTER_WEIGHT)
    rest = 1.0 / (1.0 + 6.0 * FILTER_WEIGHT)

    def masked(src, dst):
        def body(z):
            inside = plane_in(z, NZ)
            for s in range(2):
                dst[s, z, LO:HI, :] = src[0, s, z, LO:HI, :] * (mask[s, LO:HI, :] * inside)

        loop(4, 28, body)

    def gaps(field, z):
        here = [field[s, z, LO:HI, :] for s in range(2)]
        ahead, behind = lane_neighbours(here[0], here[1], 1)
        return [
            (
                here[s] - field[s, z - 1, LO:HI, :],
                here[s] - field[s, z + 1, LO:HI, :],
                here[s] - field[s, z, LO - 1 : HI - 1, :],
                here[s] - field[s, z, LO + 1 : HI + 1, :],
                here[s] - ahead[s],
                here[s] - behind[s],
            )
            for s in range(2)
        ]

    def product(p, q):
        t = [a * b for a, b in zip(p, q)]
        return ((t[0] + t[1]) + (t[2] + t[3])) + (t[4] + t[5])

    def blurred(f, z, lo, n, sides, first):
        here = [f[s, z, lo : lo + n, :] for s in range(2)]
        ahead, behind = lane_neighbours(here[0], here[1], 1)
        g = gz * NZ + z - PAD
        ends = jnp.where((g == 0) | (g == gzs * NZ - 1), 1.0, 0.0).astype(F32)
        out = []
        for s in range(sides):
            t = f[s, z - 1, lo : lo + n, :] + f[s, z + 1, lo : lo + n, :]
            t = t + (f[s, z, lo - 1 : lo + n - 1, :] + f[s, z, lo + 1 : lo + n + 1, :])
            t = t + (ahead[s] + behind[s])
            t = t + (outside[s][lo - LO : lo - LO + n] + ends) * here[s]
            out.append(rest * first[s, z, lo : lo + n, :] + weight * t)
        return out

    def filtered(f, one, two, out):
        def sweep_to(src, dst):
            def body(z):
                inside = plane_in(z, NZ)
                for s, v in enumerate(blurred(src, z, LO, WIN, 2, f)):
                    dst[s, z, LO:HI, :] = v * (mask[s, LO:HI, :] * inside)

            return body

        loop(6, 26, sweep_to(f, one))
        loop(7, 25, sweep_to(one, two))
        for z in range(PAD, PAD + NZ):
            parts[out, z - PAD] = blurred(two, z, PAD, NX, 1, f)[0]

    share(part, red0, lax.rem(gz, 2), [0], peer0, 5)
    part = total_of(red0)
    share(part, red1, gy * (gzs // 2) + gz // 2, group1, peer1, 6)
    ex4.wait()
    ex4.unpack()
    masked(lz, vv)

    def sensitivity(z):
        d = gaps(vv, z)
        inside = plane_in(z, NZ)
        for s in range(2):
            r = fin[0, s, z, LO:HI, :]
            k = (r * r) * (mask[s, LO:HI, :] * (inside * (-3.0 * (1.0 - KMIN) * 0.5)))
            diag[s, z, LO:HI, :] = k
            z0[s, z, LO:HI, :] = k * product(d[s], d[s])

    loop(5, 27, sensitivity)
    filtered(z0, q0, ww, 0)
    part = total_of(red1)
    share(part, red2, gx, group2, peer2, 7)
    ex5.wait()
    ex5.unpack()
    masked(lw, zpre)

    def sensitivity_rest(z):
        d, e = gaps(vv, z), gaps(zpre, z)
        for s in range(2):
            k = diag[s, z, LO:HI, :]
            kzm[s, z, LO:HI, :] = k * product(d[s], e[s])
            kym[s, z, LO:HI, :] = k * product(e[s], e[s])

    loop(5, 27, sensitivity_rest)
    filtered(kzm, kx, kyp, 1)
    filtered(kym, cond, inv, 2)

    total = total_of(red2)
    total = jnp.broadcast_to(jnp.sum(total, axis=1, keepdims=True), (8, LANES))
    rz, zq, rw, qw, zp, wp = (total[i : i + 1, :] for i in range(6))
    a0 = rz / zq
    rz1 = a0 * (a0 * qw - rw)
    beta = rz1 / rz
    gamma = 1.0 + beta
    a1 = rz1 / (gamma * gamma * zq - a0 * gamma * (zp + qw) + a0 * a0 * wp)
    c1 = jnp.broadcast_to(a0 + a1 * gamma - a1 * a0, (NX, LANES))
    c2 = jnp.broadcast_to(-a1 * a0, (NX, LANES))
    f0, f1, f2 = c1 * c1, 2.0 * c1 * c2, c2 * c2
    for k in range(NZ):
        out_t[k] = c1 * vv[0, k + PAD, own, :] + c2 * zpre[0, k + PAD, own, :]
        out_f[k] = (f0 * parts[0, k] + f1 * parts[1, k]) + f2 * parts[2, k]

    for ex in (ex1, ex2, ex3, ex4, ex5):
        ex.finish()
    for rows, sem in shared:
        wait_rows(span, rows, ssems.at[sem])


def store(t_ref, f_ref, out_t, out_f, sem):
    copies = [
        pltpu.make_async_copy(src, dst, sem.at[i])
        for i, (src, dst) in enumerate(((t_ref, out_t), (f_ref, out_f)))
    ]
    for cp in copies:
        cp.start()
    for cp in copies:
        cp.wait()


def local(sizes, density, volume_power_source):
    shape = pltpu.VMEM((NZ, NX, LANES), F32)
    vmem = pl.BlockSpec(memory_space=pltpu.VMEM)

    def fine(*lead, rows=FZ):
        return pltpu.VMEM((*lead, 2, FZ, rows, LANES), F32)

    def coarse(*lead):
        return pltpu.VMEM((*lead, 2, CZP, 32, LANES), F32)

    def packs(groups, rows):
        own = pltpu.VMEM((2, groups, rows, LANES), F32)
        return own, pltpu.VMEM((2, 3, groups, rows + 2 * PAD, LANES), F32)

    counts = (2, sizes[1] * (sizes[2] // 2), sizes[0])
    scratch = [
        fine(2),
        fine(rows=40),
        *[fine() for _ in range(10)],
        fine(1),
        fine(1),
        fine(),
        pltpu.VMEM((2, FZ, LANES), F32),
        coarse(1),
        pltpu.VMEM((1, 2, CZP // 2, 32, LANES), F32),
        *[coarse() for _ in range(9)],
        pltpu.VMEM((2, 32, LANES), F32),
        pltpu.VMEM((CZP, 2, FZ, LANES), F32),
        pltpu.VMEM((2 * CZ, NX, LANES), F32),
        *packs(2, NX),
        *packs(1, CX),
        *packs(1, CX),
        *packs(1, NX),
        *packs(1, NX),
        *[pltpu.VMEM((c, 8, LANES), F32) for c in counts],
        pltpu.VMEM((3, NZ, NX, LANES), F32),
        pltpu.VMEM((2048, LANES), F32),
        pltpu.SemaphoreType.DMA((2,)),
        pltpu.SemaphoreType.DMA((8,)),
        pltpu.SemaphoreType.DMA((8,)),
    ]
    outs = pl.pallas_call(
        functools.partial(kernel, sizes),
        out_shape=(shape, shape),
        in_specs=[pl.BlockSpec(memory_space=pltpu.HBM)] * 2,
        out_specs=(vmem, vmem),
        scratch_shapes=scratch,
        compiler_params=pltpu.CompilerParams(
            collective_id=0, has_side_effects=True, vmem_limit_bytes=48 * 1024 * 1024
        ),
        name="heat_sink_step",
    )(*(pltpu.with_memory_space_constraint(x, pltpu.HBM) for x in (density, volume_power_source)))
    hbm = pl.BlockSpec(memory_space=pltpu.HBM)
    return pl.pallas_call(
        store,
        out_shape=(jax.ShapeDtypeStruct((NZ, NX, LANES), F32),) * 2,
        in_specs=[vmem, vmem],
        out_specs=(hbm, hbm),
        scratch_shapes=[pltpu.SemaphoreType.DMA((2,))],
        name="store_outputs",
    )(*(pltpu.with_memory_space_constraint(x, pltpu.VMEM) for x in outs))


def solution(mesh):
    sizes = tuple(mesh.shape[a] for a in ("gx", "gy", "gz"))
    spec = P("gz", "gx", "gy")
    return jax.shard_map(
        functools.partial(local, sizes),
        mesh=mesh,
        in_specs=(spec, spec),
        out_specs=(spec, spec),
        check_vma=False,
    )
```

```python
import functools
import itertools

import jax
import jax.numpy as jnp
from jax import lax
from jax.experimental import pallas as pl
from jax.experimental.pallas import tpu as pltpu
from jax.sharding import PartitionSpec as P

KMIN = 0.001
OMEGA = 0.8
FILTER_WEIGHT = 4.0
MESH = pl.DeviceIdType.MESH
F32 = jnp.float32

LANES = 128
NZ = NX = 16
CZ = CX = 8
PAD = 8
FZ = NZ + 2 * PAD
CZP = CZ + 2 * PAD
LO, HI = 4, 28
WIN = HI - LO
CLO, CWIN = 4, 16

NEIGHBOURS = sorted(
    (o for o in itertools.product((-1, 0, 1), repeat=3) if o != (0, 0, 0)),
    key=lambda o: (-sum(map(abs, o)), o[2] == 0, o),
)


def place(sizes, offset):
    dz, dx, dy = offset
    gx, gy, gz = sizes
    return (
        lax.rem(lax.axis_index("gx") + dx + gx, gx),
        lax.rem(lax.axis_index("gy") + dy + gy, gy),
        lax.rem(lax.axis_index("gz") + dz + gz, gz),
    )


def other_core():
    gz = lax.axis_index("gz")
    return gz + 1 - 2 * lax.rem(gz, 2)


def lane_iota(rows):
    return lax.broadcasted_iota(jnp.int32, (rows, LANES), 1)


def lane_neighbours(main, side, step):
    lane = lane_iota(main.shape[0])
    up_main, up_side = pltpu.roll(main, LANES - step, 1), pltpu.roll(side, LANES - step, 1)
    dn_main, dn_side = pltpu.roll(main, step, 1), pltpu.roll(side, step, 1)
    last, first = lane >= LANES - step, lane < step
    ahead = (jnp.where(last, up_side, up_main), jnp.where(last, up_main, up_side))
    behind = (jnp.where(first, dn_side, dn_main), jnp.where(first, dn_main, dn_side))
    return ahead, behind


def pair_lanes(v):
    even = (lane_iota(v.shape[0]) & 1) == 0
    return v + jnp.where(even, pltpu.roll(v, LANES - 1, 1), pltpu.roll(v, 1, 1))


def loop(lower, upper, body):
    for i in range(lower, upper):
        body(i)


def wait_rows(span, rows, sem):
    view = span.at[pl.ds(0, rows)]
    pltpu.make_async_copy(view, view, sem).wait()


class Exchange:
    def __init__(self, sizes, arr, depth, rows, group, pks, pkr, ssem, rsem, span):
        self.sizes, self.arr, self.depth, self.rows, self.group = sizes, arr, depth, rows, group
        self.fields = arr.shape[0]
        self.per = LANES // group
        self.pks, self.pkr, self.ssem, self.rsem, self.span = pks, pkr, ssem, rsem, span
        self.sent = 0

    def slot(self, plane, f):
        return divmod(plane * self.fields + f, self.per)

    def pack(self):
        (nz, pz, _), (nr, pr, _) = self.depth, self.rows
        slot_of = lane_iota(nr) >> (self.group.bit_length() - 1)
        packed = {}
        for p in range(nz):
            for f in range(self.fields):
                g, q = self.slot(p, f)
                v = self.arr[f, 0, pz + p, pr : pr + nr, :]
                v = pltpu.roll(v, self.group * q, 1) if q else v
                for side, at in ((0, q), (1, (q + self.per - 1) % self.per)):
                    old = packed.get((side, g))
                    packed[side, g] = v if old is None else jnp.where(slot_of == at, v, old)
        for (side, g), v in packed.items():
            self.pks[side, g] = v

    def start(self):
        (nz, pz, hz), (nr, pr, hr) = self.depth, self.rows
        groups = self.slot(nz - 1, self.fields - 1)[0] + 1
        for dz, dx, dy in NEIGHBOURS:
            r = {0: (0, nr, pr), 1: (nr - hr, hr, pr - hr), -1: (0, hr, pr + nr)}[dx]
            if dy == 0:
                z = {0: (0, nz, pz), 1: (nz - hz, hz, pz - hz), -1: (0, hz, pz + nz)}[dz]
                src = self.arr.at[:, 0, pl.ds(pz + z[0], z[1]), pl.ds(pr + r[0], r[1]), :]
                dst = self.arr.at[:, 0, pl.ds(z[2], z[1]), pl.ds(r[2], r[1]), :]
            else:
                first = self.slot(nz - hz, 0)[0] if dz == 1 else 0
                end = self.slot(hz - 1, self.fields - 1)[0] + 1 if dz == -1 else groups
                g = pl.ds(first, end - first)
                src = self.pks.at[0 if dy == -1 else 1, g, pl.ds(r[0], r[1]), :]
                dst = self.pkr.at[0 if dy == -1 else 1, 1 - dz, g, pl.ds(r[2], r[1]), :]
            cp = pltpu.make_async_remote_copy(
                src_ref=src,
                dst_ref=dst,
                send_sem=self.ssem,
                recv_sem=self.rsem,
                device_id=place(self.sizes, (dz, dx, dy)),
                device_id_type=MESH,
            )
            cp.start()
            count = 1
            for d in src.shape:
                count *= d
            self.sent += count // LANES

    def wait(self):
        wait_rows(self.span, self.sent, self.rsem)

    def unpack(self, near=0, far=PAD):
        (nz, pz, hz), (nr, pr, hr) = self.depth, self.rows
        rows = nr + 2 * pr
        slot_of = lane_iota(rows) >> (self.group.bit_length() - 1)
        for region, planes in ((0, range(nz - hz, nz)), (1, range(nz)), (2, range(hz))):
            for p in planes:
                outside = {0: nz - p, 1: 0, 2: p + 1}[region]
                if not near <= outside <= far:
                    continue
                for f in range(self.fields):
                    g, q = self.slot(p, f)
                    v = jnp.where(slot_of == q, self.pkr[0, region, g], self.pkr[1, region, g])
                    v = pltpu.roll(v, LANES - self.group * q, 1) if q else v
                    self.arr[f, 1, pz + (region - 1) * nz + p, 0:rows, :] = v

    def finish(self):
        wait_rows(self.span, self.sent, self.ssem)


def kernel(
    sizes,
    rho_ref,
    src_ref,
    out_t,
    out_f,
    fin,
    cond,
    kzm,
    kx,
    kyp,
    kym,
    diag,
    inv,
    zpre,
    vv,
    z0,
    q0,
    lz,
    lw,
    ww,
    mask,
    cinc,
    cin,
    cin2,
    rhs,
    cc,
    kcz,
    kcx,
    kcyp,
    kcym,
    cinv,
    ea,
    eb,
    cmask,
    refined,
    tmp,
    pks0,
    pkr0,
    pks1,
    pkr1,
    pks2,
    pkr2,
    pks3,
    pkr3,
    pks4,
    pkr4,
    pks5,
    pkr5,
    red0,
    red1,
    red2,
    parts,
    span,
    insem,
    ssems,
    rsems,
):
    gxs, gys, gzs = sizes
    gx, gy, gz = lax.axis_index("gx"), lax.axis_index("gy"), lax.axis_index("gz")

    def peer0(_):
        return (gx, gy, other_core())

    def peer1(o):
        return (gx, lax.rem(gy + o[0], gys), lax.rem(gz + 2 * o[1], gzs))

    def peer2(dx):
        return (lax.rem(gx + dx, gxs), gy, gz)

    def hops(d, n):
        return min(d, n - d)

    group1 = [(dy, dz) for dy in range(gys) for dz in range(gzs // 2) if (dy, dz) != (0, 0)]
    group1.sort(key=lambda o: -hops(o[0], gys) - hops(o[1], gzs // 2))
    group2 = sorted(range(1, gxs), key=lambda o: -hops(o, gxs))

    loads = [
        pltpu.make_async_copy(ref, fin.at[f, 0, pl.ds(PAD, NZ), pl.ds(PAD, NX), :], insem.at[f])
        for f, ref in enumerate((rho_ref, src_ref))
    ]
    for cp in loads:
        cp.start()
    barrier = pltpu.get_barrier_semaphore()
    partners = [place(sizes, o) for o in NEIGHBOURS]
    for device in partners:
        pl.semaphore_signal(barrier, inc=1, device_id=device, device_id_type=MESH)

    def plane_in(z, cells):
        g = gz * cells + z - PAD
        return jnp.where((g >= 0) & (g < gzs * cells), 1.0, 0.0).astype(F32)

    ex1 = Exchange(sizes, fin, (NZ, PAD, 5), (NX, PAD, 5), 8, pks1, pkr1, ssems.at[0], rsems.at[0], span)
    for cp in loads:
        cp.wait()
    ex1.pack()
    pl.semaphore_wait(barrier, len(partners))
    ex1.start()

    row = lax.broadcasted_iota(jnp.int32, (FZ, LANES), 0) - PAD + gx * NX
    lane = lane_iota(FZ)
    row_in = (row >= 0) & (row < gxs * NX)
    left, right = gy > 0, gy < gys - 1
    right_end = jnp.where(right, 8, 0)
    left_start = jnp.where(left, LANES - 8, LANES)
    side_in = row_in & ((lane < right_end) | (lane >= left_start))
    mask[0] = jnp.where(row_in, 1.0, 0.0)
    mask[1] = jnp.where(side_in, 1.0, 0.0)
    crow = lax.broadcasted_iota(jnp.int32, (32, LANES), 0) - PAD + gx * CX
    clane = lane_iota(32)
    crow_in = (crow >= 0) & (crow < gxs * CX)
    cside_in = crow_in & (
        (clane < jnp.where(right, 16, 0)) | (clane >= jnp.where(left, LANES - 16, LANES))
    )
    cmask[0] = jnp.where(crow_in, 1.0, 0.0)
    cmask[1] = jnp.where(cside_in, 1.0, 0.0)

    even8 = (lane_iota(CX) & 1) == 0
    even24 = (lane_iota(24) & 1) == 0

    def block_rows(total, k):
        tmp[k] = pair_lanes(total)
        return tmp[k, pl.ds(0, CX, 2), :] + tmp[k, pl.ds(1, CX, 2), :]

    def pairs_exchange(arr, halo, rows, group, pks, pkr, sem):
        return Exchange(
            sizes,
            arr,
            (CZ // 2, PAD // 2, halo),
            (CX, PAD, rows),
            group,
            pks,
            pkr,
            ssems.at[sem],
            rsems.at[sem],
            span,
        )

    for k in range(CZ // 2):
        both = []
        for j in range(2):
            total = None
            for z in (PAD + 4 * k + 2 * j, PAD + 4 * k + 2 * j + 1):
                r = fin[0, 0, z, PAD : PAD + NX, :]
                c = KMIN + (1.0 - KMIN) * (r * r * r)
                total = c if total is None else total + c
            both.append(0.125 * block_rows(total, CZ + 2 * k + j))
        cinc[0, 0, PAD // 2 + k, PAD : PAD + CX, :] = jnp.where(even8, both[0], both[1])
    ex0 = pairs_exchange(cinc, 3, 6, 16, pks0, pkr0, 8)
    ex0.pack()
    ex0.start()

    ex1.wait()
    ex1.unpack(0, 2)

    def conductivity(z):
        inside = plane_in(z, NZ)
        for s in range(2):
            r = fin[0, s, z]
            cond[s, z, 0:FZ, :] = (mask[s] * inside) * (KMIN + (1.0 - KMIN) * (r * r * r))

    loop(6, 26, conductivity)

    def faces(z):
        here = [cond[s, z, LO:HI, :] for s in range(2)]
        ahead, behind = lane_neighbours(here[0], here[1], 1)
        inside = plane_in(z, NZ)
        for s in range(2):
            c = here[s]
            zm = 0.5 * (cond[s, z - 1, LO:HI, :] + c)
            zp = 0.5 * (cond[s, z + 1, LO:HI, :] + c)
            xp = 0.5 * (cond[s, z, LO + 1 : HI + 1, :] + c)
            xm = 0.5 * (cond[s, z, LO - 1 : HI - 1, :] + c)
            yp = 0.5 * (ahead[s] + c)
            ym = 0.5 * (behind[s] + c)
            d = (zm + zp) + (xp + xm) + (yp + ym)
            kzm[s, z, LO:HI, :] = zm
            kx[s, z, LO:HI, :] = xp
            kx[s, z, LO - 1 : LO, :] = xm[0:1, :]
            kyp[s, z, LO:HI, :] = yp
            kym[s, z, LO:HI, :] = ym
            diag[s, z, LO:HI, :] = d
            ok = mask[s, LO:HI, :] * inside > 0.5
            i = jnp.where(ok, OMEGA / d, 0.0)
            inv[s, z, LO:HI, :] = i
            zpre[s, z, LO:HI, :] = i * fin[1, s, z, LO:HI, :]

    loop(7, 25, faces)

    def off_diagonal(field, z, lo, n, sides):
        here = [field[s, z, lo : lo + n, :] for s in range(2)]
        ahead, behind = lane_neighbours(here[0], here[1], 1)
        out = []
        for s in range(sides):
            t = kzm[s, z, lo : lo + n, :] * field[s, z - 1, lo : lo + n, :]
            t = t + kzm[s, z + 1, lo : lo + n, :] * field[s, z + 1, lo : lo + n, :]
            u = kx[s, z, lo : lo + n, :] * field[s, z, lo + 1 : lo + n + 1, :]
            u = u + kx[s, z, lo - 1 : lo + n - 1, :] * field[s, z, lo - 1 : lo + n - 1, :]
            v = kyp[s, z, lo : lo + n, :] * ahead[s] + kym[s, z, lo : lo + n, :] * behind[s]
            out.append((t + u) + v)
        return out

    def coarse_rhs(load, field, k):
        total = None
        for j in range(2):
            z = PAD + 2 * k + j
            t = (1.0 - OMEGA) * load(z) + off_diagonal(field, z, PAD, NX, 1)[0]
            total = t if total is None else total + t
        return block_rows(total, k)

    def coarse_rhs_pairs(load, field, dest):
        for k in range(CZ // 2):
            r = [coarse_rhs(load, field, 2 * k + j) for j in range(2)]
            dest[0, 0, PAD // 2 + k, PAD : PAD + CX, :] = jnp.where(even8, r[0], r[1])

    coarse_rhs_pairs(lambda z: fin[1, 0, z, PAD : PAD + NX, :], zpre, cin)
    ex2 = pairs_exchange(cin, 3, 5, 16, pks2, pkr2, 1)
    ex2.pack()
    ex2.start()
    ex1.unpack(3, 5)
    loop(3, 6, conductivity)
    loop(26, 29, conductivity)
    loop(4, 7, faces)
    loop(25, 28, faces)
    ex0.wait()
    ex0.unpack()

    def split(v):
        return (
            jnp.where(even24, v, pltpu.roll(v, 1, 1)),
            jnp.where(even24, pltpu.roll(v, LANES - 1, 1), v),
        )

    def coarse_masked(v2):
        for s in range(2):
            for j, c in enumerate(split(cinc[0, s, v2, 0:24, :])):
                vc = 2 * v2 + j
                ok = cmask[s, 0:24, :] * plane_in(vc, CZ) > 0.5
                cc[s, vc, 0:24, :] = jnp.where(ok, c, 0.0)

    loop(1, 11, coarse_masked)

    def coarse_faces(vc):
        lo, hi = 3, 27
        here = [cc[s, vc, lo:hi, :] for s in range(2)]
        ahead, behind = lane_neighbours(here[0], here[1], 2)
        inside = plane_in(vc, CZ)
        for s in range(2):
            c = here[s]
            zm = 2.0 * (c + cc[s, vc - 1, lo:hi, :])
            zp = 2.0 * (c + cc[s, vc + 1, lo:hi, :])
            xm = 2.0 * (c + cc[s, vc, lo - 1 : hi - 1, :])
            xp = 2.0 * (c + cc[s, vc, lo + 1 : hi + 1, :])
            yp = 2.0 * (c + ahead[s])
            ym = 2.0 * (c + behind[s])
            kcz[s, vc, lo:hi, :] = zm
            kcx[s, vc, lo:hi, :] = xp
            kcyp[s, vc, lo:hi, :] = yp
            kcym[s, vc, lo:hi, :] = ym
            d = (zm + zp) + (xm + xp) + (yp + ym)
            i = jnp.where(cmask[s, lo:hi, :] * inside > 0.5, OMEGA / d, 0.0)
            cinv[s, vc, lo:hi, :] = i

    loop(3, 21, coarse_faces)

    def first_correction(arr, vc):
        v2, j = divmod(vc, 2)
        for s in range(2):
            rhs[s, vc, 0:24, :] = split(arr[0, s, v2, 0:24, :])[j]
            ea[s, vc, 3:27, :] = cinv[s, vc, 3:27, :] * rhs[s, vc, 3:27, :]

    ex2.wait()
    ex2.unpack()
    loop(3, 21, lambda vc: first_correction(cin, vc))

    def sweep(e, e_next, first, end):
        lo, hi = CLO, CLO + CWIN

        def body(vc):
            here = [e[s, vc, lo:hi, :] for s in range(2)]
            ahead, behind = lane_neighbours(here[0], here[1], 2)
            for s in range(2):
                t = kcz[s, vc, lo:hi, :] * e[s, vc - 1, lo:hi, :]
                t = t + kcz[s, vc + 1, lo:hi, :] * e[s, vc + 1, lo:hi, :]
                u = kcx[s, vc, lo:hi, :] * e[s, vc, lo + 1 : hi + 1, :]
                u = u + kcx[s, vc, lo - 1 : hi - 1, :] * e[s, vc, lo - 1 : hi - 1, :]
                v = kcyp[s, vc, lo:hi, :] * ahead[s] + kcym[s, vc, lo:hi, :] * behind[s]
                r = rhs[s, vc, lo:hi, :] + ((t + u) + v)
                e_next[s, vc, lo:hi, :] = (1.0 - OMEGA) * here[s] + cinv[s, vc, lo:hi, :] * r

        loop(first, end, body)

    def add_refined(e, base, first, end):
        def body(vc):
            for s in range(2):
                v = e[s, vc, CLO : CLO + CWIN, :]
                refined[vc, s, pl.ds(0, CWIN, 2), :] = v
                refined[vc, s, pl.ds(1, CWIN, 2), :] = v
                fine = refined[vc, s, LO:HI, :]
                for j in range(2):
                    z = 2 * vc - PAD + j
                    vv[s, z, LO:HI, :] = base[s, z, LO:HI, :] + fine

        loop(first, end, body)

    sweep(ea, eb, 4, 20)
    sweep(eb, ea, 5, 19)
    sweep(ea, eb, 6, 18)
    add_refined(eb, zpre, 6, 18)

    def post(z):
        b = off_diagonal(vv, z, LO, WIN, 2)
        for s in range(2):
            z0[s, z, LO:HI, :] = (1.0 - OMEGA) * vv[s, z, LO:HI, :] + inv[s, z, LO:HI, :] * (
                fin[1, s, z, LO:HI, :] + b[s]
            )

    loop(6, 26, post)

    def image(z):
        b = off_diagonal(z0, z, LO, WIN, 2)
        for s in range(2):
            q = diag[s, z, LO:HI, :] * z0[s, z, LO:HI, :] - b[s]
            q0[s, z, LO:HI, :] = q
            zpre[s, z, LO:HI, :] = inv[s, z, LO:HI, :] * q

    loop(7, 25, image)

    coarse_rhs_pairs(lambda z: q0[0, z, PAD : PAD + NX, :], zpre, cin2)
    ex3 = pairs_exchange(cin2, 2, 4, 8, pks3, pkr3, 2)
    ex3.pack()
    ex3.start()

    own = slice(PAD, PAD + NX)
    for z in range(PAD, PAD + NZ):
        lz[0, 0, z, own, :] = z0[0, z, own, :]
    ex4 = Exchange(sizes, lz, (NZ, PAD, 4), (NX, PAD, 4), 8, pks4, pkr4, ssems.at[3], rsems.at[3], span)
    ex4.pack()
    ex4.start()
    for z in (5, 26):
        post(z)
    for z in (6, 25):
        image(z)
    ex3.wait()
    ex3.unpack()

    loop(4, 20, lambda vc: first_correction(cin2, vc))
    sweep(ea, eb, 5, 19)
    sweep(eb, ea, 6, 18)
    sweep(ea, eb, 7, 17)
    add_refined(eb, zpre, 7, 17)

    def post_second(z):
        b = off_diagonal(vv, z, LO, WIN, 2)
        for s in range(2):
            ww[s, z, LO:HI, :] = (1.0 - OMEGA) * vv[s, z, LO:HI, :] + inv[s, z, LO:HI, :] * (
                q0[s, z, LO:HI, :] + b[s]
            )

    loop(8, 24, post_second)

    for z in (7, 24):
        post_second(z)

    def dots(z, acc):
        w = ww[0, z, own, :]
        zz = z0[0, z, own, :]
        q = q0[0, z, own, :]
        r = fin[1, 0, z, own, :]
        p = diag[0, z, own, :] * w - off_diagonal(ww, z, PAD, NX, 1)[0]
        terms = (r * zz, zz * q, r * w, q * w, zz * p, w * p)
        return tuple(a + t[0:8] + t[8:16] for a, t in zip(acc, terms))

    zero = jnp.zeros((8, LANES), F32)
    acc = (zero,) * 6
    for z in range(PAD, PAD + NZ):
        acc = dots(z, acc)
    which = lax.broadcasted_iota(jnp.int32, (8, LANES), 0)
    part = zero
    for i, a in enumerate(acc):
        part = jnp.where(which == i, jnp.sum(a, axis=0, keepdims=True), part)

    shared = []

    def share(part, slots, rank, offsets, peer, sem):
        slots[rank] = part
        for o in offsets:
            pltpu.make_async_remote_copy(
                src_ref=slots.at[rank],
                dst_ref=slots.at[rank],
                send_sem=ssems.at[sem],
                recv_sem=rsems.at[sem],
                device_id=peer(o),
                device_id_type=MESH,
            ).start()
        shared.append((8 * len(offsets), sem))

    def total_of(slots):
        rows, sem = shared[-1]
        wait_rows(span, rows, rsems.at[sem])
        values = [slots[i] for i in range(slots.shape[0])]
        while len(values) > 1:
            values = [a + b for a, b in zip(values[0::2], values[1::2])]
        return values[0]

    wlane = lane_iota(WIN)
    wrow = lax.broadcasted_iota(jnp.int32, (WIN, LANES), 0) + LO - PAD + gx * NX
    outside_row = jnp.where(wrow == 0, 1.0, 0.0) + jnp.where(wrow == gxs * NX - 1, 1.0, 0.0)
    outside_main = outside_row + jnp.where((wlane == 0) & (gy == 0), 1.0, 0.0)
    outside_main = outside_main + jnp.where((wlane == LANES - 1) & (gy == gys - 1), 1.0, 0.0)
    outside = (outside_main, outside_row)
    weight = FILTER_WEIGHT / (1.0 + 6.0 * FILTER_WEIGHT)
    rest = 1.0 / (1.0 + 6.0 * FILTER_WEIGHT)

    def masked(src, dst):
        def body(z):
            inside = plane_in(z, NZ)
            for s in range(2):
                dst[s, z, LO:HI, :] = src[0, s, z, LO:HI, :] * (mask[s, LO:HI, :] * inside)

        loop(4, 28, body)

    def gaps(field, z):
        here = [field[s, z, LO:HI, :] for s in range(2)]
        ahead, behind = lane_neighbours(here[0], here[1], 1)
        return [
            (
                here[s] - field[s, z - 1, LO:HI, :],
                here[s] - field[s, z + 1, LO:HI, :],
                here[s] - field[s, z, LO - 1 : HI - 1, :],
                here[s] - field[s, z, LO + 1 : HI + 1, :],
                here[s] - ahead[s],
                here[s] - behind[s],
            )
            for s in range(2)
        ]

    def product(p, q):
        t = [a * b for a, b in zip(p, q)]
        return ((t[0] + t[1]) + (t[2] + t[3])) + (t[4] + t[5])

    def blurred(f, z, lo, n, sides, first):
        here = [f[s, z, lo : lo + n, :] for s in range(2)]
        ahead, behind = lane_neighbours(here[0], here[1], 1)
        g = gz * NZ + z - PAD
        ends = jnp.where((g == 0) | (g == gzs * NZ - 1), 1.0, 0.0).astype(F32)
        out = []
        for s in range(sides):
            t = f[s, z - 1, lo : lo + n, :] + f[s, z + 1, lo : lo + n, :]
            t = t + (f[s, z, lo - 1 : lo + n - 1, :] + f[s, z, lo + 1 : lo + n + 1, :])
            t = t + (ahead[s] + behind[s])
            t = t + (outside[s][lo - LO : lo - LO + n] + ends) * here[s]
            out.append(rest * first[s, z, lo : lo + n, :] + weight * t)
        return out

    def filtered(f, one, two, out):
        def sweep_to(src, dst):
            def body(z):
                inside = plane_in(z, NZ)
                for s, v in enumerate(blurred(src, z, LO, WIN, 2, f)):
                    dst[s, z, LO:HI, :] = v * (mask[s, LO:HI, :] * inside)

            return body

        loop(6, 26, sweep_to(f, one))
        loop(7, 25, sweep_to(one, two))
        for z in range(PAD, PAD + NZ):
            parts[out, z - PAD] = blurred(two, z, PAD, NX, 1, f)[0]

    share(part, red0, lax.rem(gz, 2), [0], peer0, 5)
    for z in range(PAD, PAD + NZ):
        lw[0, 0, z, own, :] = ww[0, z, own, :] - z0[0, z, own, :]
    ex5 = Exchange(sizes, lw, (NZ, PAD, 4), (NX, PAD, 4), 8, pks5, pkr5, ssems.at[4], rsems.at[4], span)
    ex5.pack()
    ex5.start()
    part = total_of(red0)
    share(part, red1, gy * (gzs // 2) + gz // 2, group1, peer1, 6)
    ex4.wait()
    ex4.unpack()
    masked(lz, vv)

    def sensitivity(z):
        d = gaps(vv, z)
        inside = plane_in(z, NZ)
        for s in range(2):
            r = fin[0, s, z, LO:HI, :]
            k = (r * r) * (mask[s, LO:HI, :] * (inside * (-3.0 * (1.0 - KMIN) * 0.5)))
            diag[s, z, LO:HI, :] = k
            z0[s, z, LO:HI, :] = k * product(d[s], d[s])

    loop(5, 27, sensitivity)
    filtered(z0, q0, ww, 0)
    part = total_of(red1)
    share(part, red2, gx, group2, peer2, 7)
    ex5.wait()
    ex5.unpack()
    masked(lw, zpre)

    def sensitivity_rest(z):
        d, e = gaps(vv, z), gaps(zpre, z)
        for s in range(2):
            k = diag[s, z, LO:HI, :]
            kzm[s, z, LO:HI, :] = k * product(d[s], e[s])
            kym[s, z, LO:HI, :] = k * product(e[s], e[s])

    loop(5, 27, sensitivity_rest)
    filtered(kzm, kx, kyp, 1)
    filtered(kym, cond, inv, 2)

    total = total_of(red2)
    total = jnp.broadcast_to(jnp.sum(total, axis=1, keepdims=True), (8, LANES))
    rz, zq, rw, qw, zp, wp = (total[i : i + 1, :] for i in range(6))
    a0 = rz / zq
    rz1 = a0 * (a0 * qw - rw)
    beta = rz1 / rz
    gamma = 1.0 + beta
    a1 = rz1 / (gamma * gamma * zq - a0 * gamma * (zp + qw) + a0 * a0 * wp)
    c1 = jnp.broadcast_to(a0 + a1 * gamma - a1 * a0, (NX, LANES))
    c2 = jnp.broadcast_to(-a1 * a0, (NX, LANES))
    f0, f1, f2 = c1 * c1, 2.0 * c1 * c2, c2 * c2
    for k in range(NZ):
        out_t[k] = c1 * vv[0, k + PAD, own, :] + c2 * zpre[0, k + PAD, own, :]
        out_f[k] = (f0 * parts[0, k] + f1 * parts[1, k]) + f2 * parts[2, k]

    for ex in (ex0, ex1, ex2, ex3, ex4, ex5):
        ex.finish()
    for rows, sem in shared:
        wait_rows(span, rows, ssems.at[sem])


def store(t_ref, f_ref, out_t, out_f, sem):
    copies = [
        pltpu.make_async_copy(src, dst, sem.at[i])
        for i, (src, dst) in enumerate(((t_ref, out_t), (f_ref, out_f)))
    ]
    for cp in copies:
        cp.start()
    for cp in copies:
        cp.wait()


def local(sizes, density, volume_power_source):
    shape = pltpu.VMEM((NZ, NX, LANES), F32)
    vmem = pl.BlockSpec(memory_space=pltpu.VMEM)

    def fine(*lead, rows=FZ):
        return pltpu.VMEM((*lead, 2, FZ, rows, LANES), F32)

    def coarse(*lead):
        return pltpu.VMEM((*lead, 2, CZP, 32, LANES), F32)

    def packs(groups, rows):
        own = pltpu.VMEM((2, groups, rows, LANES), F32)
        return own, pltpu.VMEM((2, 3, groups, rows + 2 * PAD, LANES), F32)

    counts = (2, sizes[1] * (sizes[2] // 2), sizes[0])
    scratch = [
        fine(2),
        fine(rows=40),
        *[fine() for _ in range(10)],
        fine(1),
        fine(1),
        fine(),
        pltpu.VMEM((2, FZ, LANES), F32),
        *[pltpu.VMEM((1, 2, CZP // 2, 32, LANES), F32) for _ in range(3)],
        *[coarse() for _ in range(9)],
        pltpu.VMEM((2, 32, LANES), F32),
        pltpu.VMEM((CZP, 2, FZ, LANES), F32),
        pltpu.VMEM((2 * CZ, NX, LANES), F32),
        *packs(1, CX),
        *packs(2, NX),
        *packs(1, CX),
        *packs(1, CX),
        *packs(1, NX),
        *packs(1, NX),
        *[pltpu.VMEM((c, 8, LANES), F32) for c in counts],
        pltpu.VMEM((3, NZ, NX, LANES), F32),
        pltpu.VMEM((2048, LANES), F32),
        pltpu.SemaphoreType.DMA((2,)),
        pltpu.SemaphoreType.DMA((9,)),
        pltpu.SemaphoreType.DMA((9,)),
    ]
    outs = pl.pallas_call(
        functools.partial(kernel, sizes),
        out_shape=(shape, shape),
        in_specs=[pl.BlockSpec(memory_space=pltpu.HBM)] * 2,
        out_specs=(vmem, vmem),
        scratch_shapes=scratch,
        compiler_params=pltpu.CompilerParams(
            collective_id=0, has_side_effects=True, vmem_limit_bytes=48 * 1024 * 1024
        ),
        name="heat_sink_step",
    )(*(pltpu.with_memory_space_constraint(x, pltpu.HBM) for x in (density, volume_power_source)))
    hbm = pl.BlockSpec(memory_space=pltpu.HBM)
    return pl.pallas_call(
        store,
        out_shape=(jax.ShapeDtypeStruct((NZ, NX, LANES), F32),) * 2,
        in_specs=[vmem, vmem],
        out_specs=(hbm, hbm),
        scratch_shapes=[pltpu.SemaphoreType.DMA((2,))],
        name="store_outputs",
    )(*(pltpu.with_memory_space_constraint(x, pltpu.VMEM) for x in outs))


def solution(mesh):
    sizes = tuple(mesh.shape[a] for a in ("gx", "gy", "gz"))
    spec = P("gz", "gx", "gy")
    return jax.shard_map(
        functools.partial(local, sizes),
        mesh=mesh,
        in_specs=(spec, spec),
        out_specs=(spec, spec),
        check_vma=False,
    )
```

```python
import functools
import itertools

import jax
import jax.numpy as jnp
from jax import lax
from jax.experimental import pallas as pl
from jax.experimental.pallas import tpu as pltpu
from jax.sharding import PartitionSpec as P

KMIN = 0.001
OMEGA = 0.8
FILTER_WEIGHT = 4.0
MESH = pl.DeviceIdType.MESH
F32 = jnp.float32

LANES = 128
NZ = NX = 16
CZ = CX = 8
PAD = 8
FZ = NZ + 2 * PAD
CZP = CZ + 2 * PAD
LO, HI = 4, 28
WIN = HI - LO
CLO, CWIN = 4, 16

NEIGHBOURS = sorted(
    (o for o in itertools.product((-1, 0, 1), repeat=3) if o != (0, 0, 0)),
    key=lambda o: (-sum(map(abs, o)), o[2] == 0, o),
)


def place(sizes, offset):
    dz, dx, dy = offset
    gx, gy, gz = sizes
    return (
        lax.rem(lax.axis_index("gx") + dx + gx, gx),
        lax.rem(lax.axis_index("gy") + dy + gy, gy),
        lax.rem(lax.axis_index("gz") + dz + gz, gz),
    )


def other_core():
    gz = lax.axis_index("gz")
    return gz + 1 - 2 * lax.rem(gz, 2)


def lane_iota(rows):
    return lax.broadcasted_iota(jnp.int32, (rows, LANES), 1)


def lane_neighbours(main, side, step):
    lane = lane_iota(main.shape[0])
    up_main, up_side = pltpu.roll(main, LANES - step, 1), pltpu.roll(side, LANES - step, 1)
    dn_main, dn_side = pltpu.roll(main, step, 1), pltpu.roll(side, step, 1)
    last, first = lane >= LANES - step, lane < step
    ahead = (jnp.where(last, up_side, up_main), jnp.where(last, up_main, up_side))
    behind = (jnp.where(first, dn_side, dn_main), jnp.where(first, dn_main, dn_side))
    return ahead, behind


def pair_lanes(v):
    even = (lane_iota(v.shape[0]) & 1) == 0
    return v + jnp.where(even, pltpu.roll(v, LANES - 1, 1), pltpu.roll(v, 1, 1))


def loop(lower, upper, body):
    for i in range(lower, upper):
        body(i)


def wait_rows(span, rows, sem):
    view = span.at[pl.ds(0, rows)]
    pltpu.make_async_copy(view, view, sem).wait()


class Exchange:
    def __init__(self, sizes, arr, depth, rows, group, pks, pkr, ssem, rsem, span):
        self.sizes, self.arr, self.depth, self.rows, self.group = sizes, arr, depth, rows, group
        self.fields = arr.shape[0]
        self.per = LANES // group
        self.pks, self.pkr, self.ssem, self.rsem, self.span = pks, pkr, ssem, rsem, span
        self.sent = 0

    def slot(self, plane, f):
        return divmod(plane * self.fields + f, self.per)

    def pack(self):
        (nz, pz, _), (nr, pr, _) = self.depth, self.rows
        slot_of = lane_iota(nr) >> (self.group.bit_length() - 1)
        packed = {}
        for p in range(nz):
            for f in range(self.fields):
                g, q = self.slot(p, f)
                v = self.arr[f, 0, pz + p, pr : pr + nr, :]
                v = pltpu.roll(v, self.group * q, 1) if q else v
                for side, at in ((0, q), (1, (q + self.per - 1) % self.per)):
                    old = packed.get((side, g))
                    packed[side, g] = v if old is None else jnp.where(slot_of == at, v, old)
        for (side, g), v in packed.items():
            self.pks[side, g] = v

    def start(self):
        (nz, pz, hz), (nr, pr, hr) = self.depth, self.rows
        groups = self.slot(nz - 1, self.fields - 1)[0] + 1
        for dz, dx, dy in NEIGHBOURS:
            r = {0: (0, nr, pr), 1: (nr - hr, hr, pr - hr), -1: (0, hr, pr + nr)}[dx]
            if dy == 0:
                z = {0: (0, nz, pz), 1: (nz - hz, hz, pz - hz), -1: (0, hz, pz + nz)}[dz]
                src = self.arr.at[:, 0, pl.ds(pz + z[0], z[1]), pl.ds(pr + r[0], r[1]), :]
                dst = self.arr.at[:, 0, pl.ds(z[2], z[1]), pl.ds(r[2], r[1]), :]
            else:
                first = self.slot(nz - hz, 0)[0] if dz == 1 else 0
                end = self.slot(hz - 1, self.fields - 1)[0] + 1 if dz == -1 else groups
                g = pl.ds(first, end - first)
                src = self.pks.at[0 if dy == -1 else 1, g, pl.ds(r[0], r[1]), :]
                dst = self.pkr.at[0 if dy == -1 else 1, 1 - dz, g, pl.ds(r[2], r[1]), :]
            cp = pltpu.make_async_remote_copy(
                src_ref=src,
                dst_ref=dst,
                send_sem=self.ssem,
                recv_sem=self.rsem,
                device_id=place(self.sizes, (dz, dx, dy)),
                device_id_type=MESH,
            )
            cp.start()
            count = 1
            for d in src.shape:
                count *= d
            self.sent += count // LANES

    def wait(self):
        wait_rows(self.span, self.sent, self.rsem)

    def unpack(self, near=0, far=PAD):
        (nz, pz, hz), (nr, pr, hr) = self.depth, self.rows
        rows = nr + 2 * pr
        slot_of = lane_iota(rows) >> (self.group.bit_length() - 1)
        for region, planes in ((0, range(nz - hz, nz)), (1, range(nz)), (2, range(hz))):
            for p in planes:
                outside = {0: nz - p, 1: 0, 2: p + 1}[region]
                if not near <= outside <= far:
                    continue
                for f in range(self.fields):
                    g, q = self.slot(p, f)
                    v = jnp.where(slot_of == q, self.pkr[0, region, g], self.pkr[1, region, g])
                    v = pltpu.roll(v, LANES - self.group * q, 1) if q else v
                    self.arr[f, 1, pz + (region - 1) * nz + p, 0:rows, :] = v

    def finish(self):
        wait_rows(self.span, self.sent, self.ssem)


def kernel(
    sizes,
    rho_ref,
    src_ref,
    out_t,
    out_f,
    fin,
    cond,
    kzm,
    kx,
    kyp,
    kym,
    diag,
    inv,
    zpre,
    vv,
    z0,
    q0,
    lz,
    lw,
    ww,
    mask,
    cinc,
    cin,
    cin2,
    rhs,
    cc,
    kcz,
    kcx,
    kcyp,
    kcym,
    cinv,
    ea,
    eb,
    cmask,
    refined,
    tmp,
    pks0,
    pkr0,
    pks1,
    pkr1,
    pks2,
    pkr2,
    pks3,
    pkr3,
    pks4,
    pkr4,
    pks5,
    pkr5,
    red0,
    red1,
    red2,
    parts,
    span,
    insem,
    ssems,
    rsems,
):
    gxs, gys, gzs = sizes
    gx, gy, gz = lax.axis_index("gx"), lax.axis_index("gy"), lax.axis_index("gz")

    def peer0(_):
        return (gx, gy, other_core())

    def peer1(o):
        return (gx, lax.rem(gy + o[0], gys), lax.rem(gz + 2 * o[1], gzs))

    def peer2(dx):
        return (lax.rem(gx + dx, gxs), gy, gz)

    def hops(d, n):
        return min(d, n - d)

    group1 = [(dy, dz) for dy in range(gys) for dz in range(gzs // 2) if (dy, dz) != (0, 0)]
    group1.sort(key=lambda o: -hops(o[0], gys) - hops(o[1], gzs // 2))
    group2 = sorted(range(1, gxs), key=lambda o: -hops(o, gxs))

    loads = [
        pltpu.make_async_copy(ref, fin.at[f, 0, pl.ds(PAD, NZ), pl.ds(PAD, NX), :], insem.at[f])
        for f, ref in enumerate((rho_ref, src_ref))
    ]
    for cp in loads:
        cp.start()
    barrier = pltpu.get_barrier_semaphore()
    partners = [place(sizes, o) for o in NEIGHBOURS]
    for device in partners:
        pl.semaphore_signal(barrier, inc=1, device_id=device, device_id_type=MESH)

    def plane_in(z, cells):
        g = gz * cells + z - PAD
        return jnp.where((g >= 0) & (g < gzs * cells), 1.0, 0.0).astype(F32)

    ex1 = Exchange(sizes, fin, (NZ, PAD, 5), (NX, PAD, 5), 8, pks1, pkr1, ssems.at[0], rsems.at[0], span)
    for cp in loads:
        cp.wait()
    ex1.pack()
    pl.semaphore_wait(barrier, len(partners))
    ex1.start()

    row = lax.broadcasted_iota(jnp.int32, (FZ, LANES), 0) - PAD + gx * NX
    lane = lane_iota(FZ)
    row_in = (row >= 0) & (row < gxs * NX)
    left, right = gy > 0, gy < gys - 1
    right_end = jnp.where(right, 8, 0)
    left_start = jnp.where(left, LANES - 8, LANES)
    side_in = row_in & ((lane < right_end) | (lane >= left_start))
    mask[0] = jnp.where(row_in, 1.0, 0.0)
    mask[1] = jnp.where(side_in, 1.0, 0.0)
    crow = lax.broadcasted_iota(jnp.int32, (32, LANES), 0) - PAD + gx * CX
    clane = lane_iota(32)
    crow_in = (crow >= 0) & (crow < gxs * CX)
    cside_in = crow_in & (
        (clane < jnp.where(right, 16, 0)) | (clane >= jnp.where(left, LANES - 16, LANES))
    )
    cmask[0] = jnp.where(crow_in, 1.0, 0.0)
    cmask[1] = jnp.where(cside_in, 1.0, 0.0)

    even8 = (lane_iota(CX) & 1) == 0
    even24 = (lane_iota(24) & 1) == 0

    def block_rows(total, k):
        tmp[k] = pair_lanes(total)
        return tmp[k, pl.ds(0, CX, 2), :] + tmp[k, pl.ds(1, CX, 2), :]

    def pairs_exchange(arr, halo, rows, group, pks, pkr, sem):
        return Exchange(
            sizes,
            arr,
            (CZ // 2, PAD // 2, halo),
            (CX, PAD, rows),
            group,
            pks,
            pkr,
            ssems.at[sem],
            rsems.at[sem],
            span,
        )

    for k in range(CZ // 2):
        both = []
        for j in range(2):
            total = None
            for z in (PAD + 4 * k + 2 * j, PAD + 4 * k + 2 * j + 1):
                r = fin[0, 0, z, PAD : PAD + NX, :]
                c = KMIN + (1.0 - KMIN) * (r * r * r)
                total = c if total is None else total + c
            both.append(0.125 * block_rows(total, CZ + 2 * k + j))
        cinc[0, 0, PAD // 2 + k, PAD : PAD + CX, :] = jnp.where(even8, both[0], both[1])
    ex0 = pairs_exchange(cinc, 3, 6, 16, pks0, pkr0, 8)
    ex0.pack()
    ex0.start()

    ex1.wait()
    ex1.unpack(0, 2)

    def conductivity(z):
        inside = plane_in(z, NZ)
        for s in range(2):
            r = fin[0, s, z]
            cond[s, z, 0:FZ, :] = (mask[s] * inside) * (KMIN + (1.0 - KMIN) * (r * r * r))

    loop(6, 26, conductivity)

    def faces(z):
        here = [cond[s, z, LO:HI, :] for s in range(2)]
        ahead, behind = lane_neighbours(here[0], here[1], 1)
        inside = plane_in(z, NZ)
        for s in range(2):
            c = here[s]
            zm = 0.5 * (cond[s, z - 1, LO:HI, :] + c)
            zp = 0.5 * (cond[s, z + 1, LO:HI, :] + c)
            xp = 0.5 * (cond[s, z, LO + 1 : HI + 1, :] + c)
            xm = 0.5 * (cond[s, z, LO - 1 : HI - 1, :] + c)
            yp = 0.5 * (ahead[s] + c)
            ym = 0.5 * (behind[s] + c)
            d = (zm + zp) + (xp + xm) + (yp + ym)
            kzm[s, z, LO:HI, :] = zm
            kx[s, z, LO:HI, :] = xp
            kx[s, z, LO - 1 : LO, :] = xm[0:1, :]
            kyp[s, z, LO:HI, :] = yp
            kym[s, z, LO:HI, :] = ym
            diag[s, z, LO:HI, :] = d
            ok = mask[s, LO:HI, :] * inside > 0.5
            i = jnp.where(ok, OMEGA / d, 0.0)
            inv[s, z, LO:HI, :] = i
            zpre[s, z, LO:HI, :] = i * fin[1, s, z, LO:HI, :]

    loop(7, 25, faces)

    def off_diagonal(field, z, lo, n, sides):
        here = [field[s, z, lo : lo + n, :] for s in range(2)]
        ahead, behind = lane_neighbours(here[0], here[1], 1)
        out = []
        for s in range(sides):
            t = kzm[s, z, lo : lo + n, :] * field[s, z - 1, lo : lo + n, :]
            t = t + kzm[s, z + 1, lo : lo + n, :] * field[s, z + 1, lo : lo + n, :]
            u = kx[s, z, lo : lo + n, :] * field[s, z, lo + 1 : lo + n + 1, :]
            u = u + kx[s, z, lo - 1 : lo + n - 1, :] * field[s, z, lo - 1 : lo + n - 1, :]
            v = kyp[s, z, lo : lo + n, :] * ahead[s] + kym[s, z, lo : lo + n, :] * behind[s]
            out.append((t + u) + v)
        return out

    def coarse_rhs(load, field, k):
        total = None
        for j in range(2):
            z = PAD + 2 * k + j
            t = (1.0 - OMEGA) * load(z) + off_diagonal(field, z, PAD, NX, 1)[0]
            total = t if total is None else total + t
        return block_rows(total, k)

    def coarse_rhs_pairs(load, field, dest):
        for k in range(CZ // 2):
            r = [coarse_rhs(load, field, 2 * k + j) for j in range(2)]
            dest[0, 0, PAD // 2 + k, PAD : PAD + CX, :] = jnp.where(even8, r[0], r[1])

    coarse_rhs_pairs(lambda z: fin[1, 0, z, PAD : PAD + NX, :], zpre, cin)
    ex2 = pairs_exchange(cin, 3, 5, 16, pks2, pkr2, 1)
    ex2.pack()
    ex2.start()
    ex1.unpack(3, 5)
    loop(3, 6, conductivity)
    loop(26, 29, conductivity)
    loop(4, 7, faces)
    loop(25, 28, faces)
    ex0.wait()
    ex0.unpack()

    def split(v):
        return (
            jnp.where(even24, v, pltpu.roll(v, 1, 1)),
            jnp.where(even24, pltpu.roll(v, LANES - 1, 1), v),
        )

    def coarse_masked(v2):
        for s in range(2):
            for j, c in enumerate(split(cinc[0, s, v2, 0:24, :])):
                vc = 2 * v2 + j
                ok = cmask[s, 0:24, :] * plane_in(vc, CZ) > 0.5
                cc[s, vc, 0:24, :] = jnp.where(ok, c, 0.0)

    loop(1, 11, coarse_masked)

    def coarse_faces(vc):
        lo, hi = 3, 27
        here = [cc[s, vc, lo:hi, :] for s in range(2)]
        ahead, behind = lane_neighbours(here[0], here[1], 2)
        inside = plane_in(vc, CZ)
        for s in range(2):
            c = here[s]
            zm = 2.0 * (c + cc[s, vc - 1, lo:hi, :])
            zp = 2.0 * (c + cc[s, vc + 1, lo:hi, :])
            xm = 2.0 * (c + cc[s, vc, lo - 1 : hi - 1, :])
            xp = 2.0 * (c + cc[s, vc, lo + 1 : hi + 1, :])
            yp = 2.0 * (c + ahead[s])
            ym = 2.0 * (c + behind[s])
            kcz[s, vc, lo:hi, :] = zm
            kcx[s, vc, lo:hi, :] = xp
            kcyp[s, vc, lo:hi, :] = yp
            kcym[s, vc, lo:hi, :] = ym
            d = (zm + zp) + (xm + xp) + (yp + ym)
            i = jnp.where(cmask[s, lo:hi, :] * inside > 0.5, OMEGA / d, 0.0)
            cinv[s, vc, lo:hi, :] = i

    loop(3, 21, coarse_faces)

    def first_correction(arr, vc):
        v2, j = divmod(vc, 2)
        for s in range(2):
            rhs[s, vc, 0:24, :] = split(arr[0, s, v2, 0:24, :])[j]
            ea[s, vc, 3:27, :] = cinv[s, vc, 3:27, :] * rhs[s, vc, 3:27, :]

    ex2.wait()
    ex2.unpack()
    loop(3, 21, lambda vc: first_correction(cin, vc))

    def sweep(e, e_next, first, end):
        lo, hi = CLO, CLO + CWIN

        def body(vc):
            here = [e[s, vc, lo:hi, :] for s in range(2)]
            ahead, behind = lane_neighbours(here[0], here[1], 2)
            for s in range(2):
                t = kcz[s, vc, lo:hi, :] * e[s, vc - 1, lo:hi, :]
                t = t + kcz[s, vc + 1, lo:hi, :] * e[s, vc + 1, lo:hi, :]
                u = kcx[s, vc, lo:hi, :] * e[s, vc, lo + 1 : hi + 1, :]
                u = u + kcx[s, vc, lo - 1 : hi - 1, :] * e[s, vc, lo - 1 : hi - 1, :]
                v = kcyp[s, vc, lo:hi, :] * ahead[s] + kcym[s, vc, lo:hi, :] * behind[s]
                r = rhs[s, vc, lo:hi, :] + ((t + u) + v)
                e_next[s, vc, lo:hi, :] = (1.0 - OMEGA) * here[s] + cinv[s, vc, lo:hi, :] * r

        loop(first, end, body)

    def add_refined(e, base, first, end):
        def body(vc):
            for s in range(2):
                v = e[s, vc, CLO : CLO + CWIN, :]
                refined[vc, s, pl.ds(0, CWIN, 2), :] = v
                refined[vc, s, pl.ds(1, CWIN, 2), :] = v
                fine = refined[vc, s, LO:HI, :]
                for j in range(2):
                    z = 2 * vc - PAD + j
                    vv[s, z, LO:HI, :] = base[s, z, LO:HI, :] + fine

        loop(first, end, body)

    sweep(ea, eb, 4, 20)
    sweep(eb, ea, 5, 19)
    sweep(ea, eb, 6, 18)
    add_refined(eb, zpre, 6, 18)

    def post(z):
        b = off_diagonal(vv, z, LO, WIN, 2)
        for s in range(2):
            z0[s, z, LO:HI, :] = (1.0 - OMEGA) * vv[s, z, LO:HI, :] + inv[s, z, LO:HI, :] * (
                fin[1, s, z, LO:HI, :] + b[s]
            )

    loop(6, 26, post)

    def image(z):
        b = off_diagonal(z0, z, LO, WIN, 2)
        for s in range(2):
            q = diag[s, z, LO:HI, :] * z0[s, z, LO:HI, :] - b[s]
            q0[s, z, LO:HI, :] = q
            zpre[s, z, LO:HI, :] = inv[s, z, LO:HI, :] * q

    loop(7, 25, image)

    coarse_rhs_pairs(lambda z: q0[0, z, PAD : PAD + NX, :], zpre, cin2)
    ex3 = pairs_exchange(cin2, 2, 4, 8, pks3, pkr3, 2)
    ex3.pack()
    ex3.start()

    own = slice(PAD, PAD + NX)
    for z in range(PAD, PAD + NZ):
        lz[0, 0, z, own, :] = z0[0, z, own, :]
    ex4 = Exchange(sizes, lz, (NZ, PAD, 4), (NX, PAD, 4), 8, pks4, pkr4, ssems.at[3], rsems.at[3], span)
    ex4.pack()
    ex4.start()
    for z in (5, 26):
        post(z)
    for z in (6, 25):
        image(z)
    zero = jnp.zeros((8, LANES), F32)
    early = [zero, zero]
    for z in range(PAD, PAD + NZ):
        zz = z0[0, z, own, :]
        for i, t in enumerate((fin[1, 0, z, own, :] * zz, zz * q0[0, z, own, :])):
            early[i] = early[i] + t[0:8] + t[8:16]
    which = lax.broadcasted_iota(jnp.int32, (8, LANES), 0)
    early_part = zero
    for i, a in enumerate(early):
        early_part = jnp.where(which == i, jnp.sum(a, axis=0, keepdims=True), early_part)
    ex3.wait()
    ex3.unpack()

    loop(4, 20, lambda vc: first_correction(cin2, vc))
    sweep(ea, eb, 5, 19)
    sweep(eb, ea, 6, 18)
    sweep(ea, eb, 7, 17)
    add_refined(eb, zpre, 7, 17)

    def post_second(z):
        b = off_diagonal(vv, z, LO, WIN, 2)
        for s in range(2):
            ww[s, z, LO:HI, :] = (1.0 - OMEGA) * vv[s, z, LO:HI, :] + inv[s, z, LO:HI, :] * (
                q0[s, z, LO:HI, :] + b[s]
            )

    loop(8, 24, post_second)

    for z in (7, 24):
        post_second(z)

    def dots(z, acc):
        w = ww[0, z, own, :]
        zz = z0[0, z, own, :]
        q = q0[0, z, own, :]
        r = fin[1, 0, z, own, :]
        p = diag[0, z, own, :] * w - off_diagonal(ww, z, PAD, NX, 1)[0]
        terms = (r * w, q * w, zz * p, w * p)
        return tuple(a + t[0:8] + t[8:16] for a, t in zip(acc, terms))

    acc = (zero,) * 4
    for z in range(PAD, PAD + NZ):
        acc = dots(z, acc)
    part = early_part
    for i, a in enumerate(acc, 2):
        part = jnp.where(which == i, jnp.sum(a, axis=0, keepdims=True), part)

    shared = []

    def share(part, slots, rank, offsets, peer, sem):
        slots[rank] = part
        for o in offsets:
            pltpu.make_async_remote_copy(
                src_ref=slots.at[rank],
                dst_ref=slots.at[rank],
                send_sem=ssems.at[sem],
                recv_sem=rsems.at[sem],
                device_id=peer(o),
                device_id_type=MESH,
            ).start()
        shared.append((8 * len(offsets), sem))

    def total_of(slots):
        rows, sem = shared[-1]
        wait_rows(span, rows, rsems.at[sem])
        values = [slots[i] for i in range(slots.shape[0])]
        while len(values) > 1:
            values = [a + b for a, b in zip(values[0::2], values[1::2])]
        return values[0]

    wlane = lane_iota(WIN)
    wrow = lax.broadcasted_iota(jnp.int32, (WIN, LANES), 0) + LO - PAD + gx * NX
    outside_row = jnp.where(wrow == 0, 1.0, 0.0) + jnp.where(wrow == gxs * NX - 1, 1.0, 0.0)
    outside_main = outside_row + jnp.where((wlane == 0) & (gy == 0), 1.0, 0.0)
    outside_main = outside_main + jnp.where((wlane == LANES - 1) & (gy == gys - 1), 1.0, 0.0)
    outside = (outside_main, outside_row)
    weight = FILTER_WEIGHT / (1.0 + 6.0 * FILTER_WEIGHT)
    rest = 1.0 / (1.0 + 6.0 * FILTER_WEIGHT)

    def masked(src, dst):
        def body(z):
            inside = plane_in(z, NZ)
            for s in range(2):
                dst[s, z, LO:HI, :] = src[0, s, z, LO:HI, :] * (mask[s, LO:HI, :] * inside)

        loop(4, 28, body)

    def gaps(field, z):
        here = [field[s, z, LO:HI, :] for s in range(2)]
        ahead, behind = lane_neighbours(here[0], here[1], 1)
        return [
            (
                here[s] - field[s, z - 1, LO:HI, :],
                here[s] - field[s, z + 1, LO:HI, :],
                here[s] - field[s, z, LO - 1 : HI - 1, :],
                here[s] - field[s, z, LO + 1 : HI + 1, :],
                here[s] - ahead[s],
                here[s] - behind[s],
            )
            for s in range(2)
        ]

    def product(p, q):
        t = [a * b for a, b in zip(p, q)]
        return ((t[0] + t[1]) + (t[2] + t[3])) + (t[4] + t[5])

    def blurred(f, z, lo, n, sides, first):
        here = [f[s, z, lo : lo + n, :] for s in range(2)]
        ahead, behind = lane_neighbours(here[0], here[1], 1)
        g = gz * NZ + z - PAD
        ends = jnp.where((g == 0) | (g == gzs * NZ - 1), 1.0, 0.0).astype(F32)
        out = []
        for s in range(sides):
            t = f[s, z - 1, lo : lo + n, :] + f[s, z + 1, lo : lo + n, :]
            t = t + (f[s, z, lo - 1 : lo + n - 1, :] + f[s, z, lo + 1 : lo + n + 1, :])
            t = t + (ahead[s] + behind[s])
            t = t + (outside[s][lo - LO : lo - LO + n] + ends) * here[s]
            out.append(rest * first[s, z, lo : lo + n, :] + weight * t)
        return out

    def filtered(f, one, two, out):
        def sweep_to(src, dst):
            def body(z):
                inside = plane_in(z, NZ)
                for s, v in enumerate(blurred(src, z, LO, WIN, 2, f)):
                    dst[s, z, LO:HI, :] = v * (mask[s, LO:HI, :] * inside)

            return body

        loop(6, 26, sweep_to(f, one))
        loop(7, 25, sweep_to(one, two))
        for z in range(PAD, PAD + NZ):
            parts[out, z - PAD] = blurred(two, z, PAD, NX, 1, f)[0]

    share(part, red0, lax.rem(gz, 2), [0], peer0, 5)
    for z in range(PAD, PAD + NZ):
        lw[0, 0, z, own, :] = ww[0, z, own, :] - z0[0, z, own, :]
    ex5 = Exchange(sizes, lw, (NZ, PAD, 4), (NX, PAD, 4), 8, pks5, pkr5, ssems.at[4], rsems.at[4], span)
    ex5.pack()
    ex5.start()
    part = total_of(red0)
    share(part, red1, gy * (gzs // 2) + gz // 2, group1, peer1, 6)
    ex4.wait()
    ex4.unpack()
    masked(lz, vv)

    def sensitivity(z):
        d = gaps(vv, z)
        inside = plane_in(z, NZ)
        for s in range(2):
            r = fin[0, s, z, LO:HI, :]
            k = (r * r) * (mask[s, LO:HI, :] * (inside * (-3.0 * (1.0 - KMIN) * 0.5)))
            diag[s, z, LO:HI, :] = k
            z0[s, z, LO:HI, :] = k * product(d[s], d[s])

    loop(5, 27, sensitivity)
    filtered(z0, q0, ww, 0)
    part = total_of(red1)
    share(part, red2, gx, group2, peer2, 7)
    ex5.wait()
    ex5.unpack()
    masked(lw, zpre)

    def sensitivity_rest(z):
        d, e = gaps(vv, z), gaps(zpre, z)
        for s in range(2):
            k = diag[s, z, LO:HI, :]
            kzm[s, z, LO:HI, :] = k * product(d[s], e[s])
            kym[s, z, LO:HI, :] = k * product(e[s], e[s])

    loop(5, 27, sensitivity_rest)
    filtered(kzm, kx, kyp, 1)
    filtered(kym, cond, inv, 2)

    total = total_of(red2)
    total = jnp.broadcast_to(jnp.sum(total, axis=1, keepdims=True), (8, LANES))
    rz, zq, rw, qw, zp, wp = (total[i : i + 1, :] for i in range(6))
    a0 = rz / zq
    rz1 = a0 * (a0 * qw - rw)
    beta = rz1 / rz
    gamma = 1.0 + beta
    a1 = rz1 / (gamma * gamma * zq - a0 * gamma * (zp + qw) + a0 * a0 * wp)
    c1 = jnp.broadcast_to(a0 + a1 * gamma - a1 * a0, (NX, LANES))
    c2 = jnp.broadcast_to(-a1 * a0, (NX, LANES))
    f0, f1, f2 = c1 * c1, 2.0 * c1 * c2, c2 * c2
    for k in range(NZ):
        out_t[k] = c1 * vv[0, k + PAD, own, :] + c2 * zpre[0, k + PAD, own, :]
        out_f[k] = (f0 * parts[0, k] + f1 * parts[1, k]) + f2 * parts[2, k]

    for ex in (ex0, ex1, ex2, ex3, ex4, ex5):
        ex.finish()
    for rows, sem in shared:
        wait_rows(span, rows, ssems.at[sem])


def store(t_ref, f_ref, out_t, out_f, sem):
    copies = [
        pltpu.make_async_copy(src, dst, sem.at[i])
        for i, (src, dst) in enumerate(((t_ref, out_t), (f_ref, out_f)))
    ]
    for cp in copies:
        cp.start()
    for cp in copies:
        cp.wait()


def local(sizes, density, volume_power_source):
    shape = pltpu.VMEM((NZ, NX, LANES), F32)
    vmem = pl.BlockSpec(memory_space=pltpu.VMEM)

    def fine(*lead, rows=FZ):
        return pltpu.VMEM((*lead, 2, FZ, rows, LANES), F32)

    def coarse(*lead):
        return pltpu.VMEM((*lead, 2, CZP, 32, LANES), F32)

    def packs(groups, rows):
        own = pltpu.VMEM((2, groups, rows, LANES), F32)
        return own, pltpu.VMEM((2, 3, groups, rows + 2 * PAD, LANES), F32)

    counts = (2, sizes[1] * (sizes[2] // 2), sizes[0])
    scratch = [
        fine(2),
        fine(rows=40),
        *[fine() for _ in range(10)],
        fine(1),
        fine(1),
        fine(),
        pltpu.VMEM((2, FZ, LANES), F32),
        *[pltpu.VMEM((1, 2, CZP // 2, 32, LANES), F32) for _ in range(3)],
        *[coarse() for _ in range(9)],
        pltpu.VMEM((2, 32, LANES), F32),
        pltpu.VMEM((CZP, 2, FZ, LANES), F32),
        pltpu.VMEM((2 * CZ, NX, LANES), F32),
        *packs(1, CX),
        *packs(2, NX),
        *packs(1, CX),
        *packs(1, CX),
        *packs(1, NX),
        *packs(1, NX),
        *[pltpu.VMEM((c, 8, LANES), F32) for c in counts],
        pltpu.VMEM((3, NZ, NX, LANES), F32),
        pltpu.VMEM((2048, LANES), F32),
        pltpu.SemaphoreType.DMA((2,)),
        pltpu.SemaphoreType.DMA((9,)),
        pltpu.SemaphoreType.DMA((9,)),
    ]
    outs = pl.pallas_call(
        functools.partial(kernel, sizes),
        out_shape=(shape, shape),
        in_specs=[pl.BlockSpec(memory_space=pltpu.HBM)] * 2,
        out_specs=(vmem, vmem),
        scratch_shapes=scratch,
        compiler_params=pltpu.CompilerParams(
            collective_id=0, has_side_effects=True, vmem_limit_bytes=48 * 1024 * 1024
        ),
        name="heat_sink_step",
    )(*(pltpu.with_memory_space_constraint(x, pltpu.HBM) for x in (density, volume_power_source)))
    hbm = pl.BlockSpec(memory_space=pltpu.HBM)
    return pl.pallas_call(
        store,
        out_shape=(jax.ShapeDtypeStruct((NZ, NX, LANES), F32),) * 2,
        in_specs=[vmem, vmem],
        out_specs=(hbm, hbm),
        scratch_shapes=[pltpu.SemaphoreType.DMA((2,))],
        name="store_outputs",
    )(*(pltpu.with_memory_space_constraint(x, pltpu.VMEM) for x in outs))


def solution(mesh):
    sizes = tuple(mesh.shape[a] for a in ("gx", "gy", "gz"))
    spec = P("gz", "gx", "gy")
    return jax.shard_map(
        functools.partial(local, sizes),
        mesh=mesh,
        in_specs=(spec, spec),
        out_specs=(spec, spec),
        check_vma=False,
    )
```
